32 devices in a mesh: tile: 16 (over z, y, x), own: 2 (over core).
Axes of the slice: x: 2, y: 2, z: 4, core: 2. Of those that a mesh axis runs over, the one named last changes fastest.
Arguments:
- features: bfloat16 [512, 8, 768], P('tile'), may hold values from -6 to 6
- cotangent: bfloat16 [512, 8, 768], P('tile'), may hold values from -6 to 6
- depth_kernel: float32 [7, 7, 768], replicated, may hold values from -0.875 to 0.875
- ln_gain: float32 [768], replicated, may hold values from 0.1 to 1.9
- weight_up: bfloat16 [768, 3072], P('tile', 'own'), may hold values from -0.21875 to 0.21875
- bias_up: float32 [3072], P('own'), may hold values from -3 to 3
- weight_down: bfloat16 [3072, 768], P('own', 'tile'), may hold values from -0.109375 to 0.109375
- layer_scale: float32 [768], replicated, may hold values from 0.3 to 3
- tissue: int32 [64, 1], P('tile'), may hold values 0 or 1
- lengths: int32 [16], replicated, may hold values from 1 to 4, 32 in all
Outputs:
- block_out: bfloat16 [512, 8, 768], P(('tile', 'own'))
- grad_features: bfloat16 [512, 8, 768], P(('tile', 'own'))
- muon_up: float32 [768, 3072], P('tile', 'own')
- muon_down: float32 [3072, 768], P('own', 'tile')
The draws below stay inside these ranges and needn't reach their ends.
Inputs may be any that keep to these rules, and one draw needn't show every extreme that they name: `lengths`: patch rows of slide in each strip; they sum to 32, and some strip has exactly 4.
All inputs are finite; a program needn't handle non-finite values. No bound on the sum of `tissue` on one device may be relied on, other than what follows from the above.
Results may differ from the reference program's by a relative error of at most 0.015.
Values may be sent and summed in bfloat16 or wider, within the bound.
No kernel may reach another device: no remote copies, remote signals or barrier semaphores. Data moves between devices by JAX's collectives and lax.ppermute only.
A program may use at most 128 MiB of HBM per device.

```python
import math
import jax
import jax.numpy as jnp
import numpy as np
from jax import lax

D = 768
FF = 3072
KERNEL = 7
PATCH = 8
COLS = 8
P_AVG = 2
ITERS_NS = 2
P_MOST = 4
TILE_ROWS = 32
ROWS = 512
PATCH_ROWS = 64
IMG_ROWS = 256
MUON_COLS = 1536
N_TILE = 16
N_OWN = 2


def plant(entries, stream_key, smallest, top_value):
    spot = [jax.random.randint(jax.random.fold_in(stream_key, axis), (), 0, length) for axis, length in enumerate(entries.shape)]
    widest = entries.shape.index(max(entries.shape))
    beside = spot[:widest] + [(spot[widest] + 1) % entries.shape[widest]] + spot[widest + 1:]
    return entries.at[tuple(spot)].set(smallest).at[tuple(beside)].set(top_value)


def shard_levels(rng, shape, shards, low, top_value):
    def one(position, blocks):
        heights = jax.random.uniform(jax.random.fold_in(jax.random.fold_in(rng, 6), position), (blocks,), jnp.float32, low / len(shards), top_value / len(shards))
        return jnp.repeat(jnp.exp(heights), shape[position] // blocks).reshape((-1,) + (1,) * (len(shape) - position - 1))

    level = one(*shards[0])
    for cut in shards[1:]:
        level = level * one(*cut)
    return level


def split_up(amount, total, bound, lean):
    portions = [(1 << 20) // math.isqrt(rank ** lean) + 1 for rank in range(2, amount + 1)]
    spare, holding = total - bound - (amount - 1), [1] * (amount - 1)
    while spare > 0:
        free = [i for i in range(amount - 1) if holding[i] < bound]
        whole, left = sum([portions[i] for i in free]), spare
        for i in free:
            more = min(bound - holding[i], max(1, left * portions[i] // whole), spare)
            holding[i] = holding[i] + more
            spare = spare - more
    return np.array([bound] + holding)


def ragged_sizes(rng, count, total, bound, lean):
    if count == 2:
        one = jax.random.randint(rng, (), max(1, total - bound), min(bound, total - 1) + 1)
        return jnp.stack([one, total - one])
    tallies = jnp.asarray(split_up(count, total, bound, lean), jnp.int32)
    pairs = (count - 1) // 2
    giver, taker = tallies[1:1 + 2 * pairs:2], tallies[2:2 + 2 * pairs:2]
    slack = jnp.minimum(giver - 1, bound - taker)
    passed = jax.random.randint(jax.random.fold_in(rng, 1), (pairs,), 0, 1 << 20) % (slack + 1)
    tallies = tallies.at[1:1 + 2 * pairs:2].set(giver - passed).at[2:2 + 2 * pairs:2].set(taker + passed)
    return tallies[jax.random.permutation(jax.random.fold_in(rng, 2), count)]


def gaussian(stream_key, extent, width, limit, split=(), held_as=jnp.bfloat16):
    entries = width * jax.random.normal(stream_key, extent, jnp.float32)
    if split:
        entries = entries * shard_levels(stream_key, extent, split, -0.22, 0.18)
    return jnp.clip(entries, -limit, limit).astype(held_as)


def setup_inputs(seed: int = 0) -> dict:
    streams_of = jax.random.split(jax.random.key(seed), 11)
    return {
        "features": gaussian(streams_of[0], (ROWS, COLS, D), 1.0, 6.0, ((0, 16),)),
        "cotangent": gaussian(streams_of[1], (ROWS, COLS, D), 1.0, 6.0, ((0, 16),)),
        "depth_kernel": gaussian(streams_of[2], (KERNEL, KERNEL, D), (KERNEL * KERNEL) ** -0.5, 0.875, (), jnp.float32),
        "ln_gain": jnp.clip(1.0 + 0.18 * jax.random.normal(streams_of[3], (D,), jnp.float32), 0.1, 1.9),
        "weight_up": gaussian(streams_of[4], (D, FF), D ** -0.5, 0.21875, ((0, 16), (1, 2))),
        "bias_up": gaussian(streams_of[5], (FF,), 0.5, 3.0, ((0, 2),), jnp.float32),
        "weight_down": gaussian(streams_of[6], (FF, D), FF ** -0.5, 0.109375, ((0, 2), (1, 16))),
        "layer_scale": jnp.clip(jnp.exp(jax.random.uniform(streams_of[7], (D,), jnp.float32, math.log(0.3), math.log(3.0))), 0.3, 3.0),
        "tissue": plant((jax.random.randint(streams_of[8], (PATCH_ROWS, COLS // PATCH), 0, 4) < 3).astype(jnp.int32), jax.random.fold_in(streams_of[8], 1), 0, 1),
        "lengths": ragged_sizes(streams_of[9], N_TILE, N_TILE * P_AVG, P_MOST, 2).astype(jnp.int32),
    }


INV_ROOT_TWO = 0.7071067811865476
INV_ROOT_TAU = 0.3989422804014327
NS_A = 3.4445
NS_B = -4.775
NS_C = 2.0315
EPS_NORM = 1e-06
HIGHEST_PREC = lax.Precision.HIGHEST

def gelu_exact(hidden):
    return 0.5 * hidden * (1.0 + lax.erf(hidden * INV_ROOT_TWO))

def gelu_slope(hidden):
    return 0.5 * (1.0 + lax.erf(hidden * INV_ROOT_TWO)) + hidden * jnp.exp(-0.5 * hidden * hidden) * INV_ROOT_TAU

def depthwise(framed, kernel):
    margin = kernel.shape[0] // 2
    padded = jnp.pad(framed, ((0, 0), (margin, margin), (0, 0)))
    row_count = framed.shape[0] - 2 * margin
    col_count = framed.shape[1]
    totals = jnp.zeros((row_count, col_count, framed.shape[2]), jnp.float32)
    for row_tap in range(kernel.shape[0]):
        for col_tap in range(kernel.shape[1]):
            totals = totals + kernel[row_tap, col_tap] * padded[row_tap:row_tap + row_count, col_tap:col_tap + col_count]
    return totals

def layer_norm(mixed, ln_gain):
    average = lax.optimization_barrier(jnp.mean(mixed, axis=-1, keepdims=True))
    shifted = mixed - average
    variance = lax.optimization_barrier(jnp.mean(shifted * shifted, axis=-1, keepdims=True))
    inv_std = lax.rsqrt(variance + 1e-06)
    centred = shifted * inv_std
    return (centred, inv_std, (centred * ln_gain).astype(jnp.bfloat16))

def norm_back(grad_normed, centred, inv_std, ln_gain):
    scaled_grad = grad_normed * ln_gain
    first_mean = lax.optimization_barrier(jnp.mean(scaled_grad, axis=-1, keepdims=True))
    second_mean = lax.optimization_barrier(jnp.mean(scaled_grad * centred, axis=-1, keepdims=True))
    return inv_std * (scaled_grad - first_mean - centred * second_mean)

def blockwise_sum(left, right, right_rows):
    block_width = left.shape[1] // N_OWN
    total = jnp.zeros((left.shape[0], right.shape[1] if right_rows else right.shape[0]), jnp.float32)
    for block_index in range(N_OWN):
        lo_col = block_index * block_width
        piece = left[:, lo_col:lo_col + block_width]
        if right_rows:
            term = jnp.dot(piece, right[lo_col:lo_col + block_width], preferred_element_type=jnp.float32)
        else:
            term = lax.dot_general(piece, right[:, lo_col:lo_col + block_width], (((1,), (1,)), ((), ())), preferred_element_type=jnp.float32)
        rounded = lax.optimization_barrier(term.astype(jnp.bfloat16))
        total = total + rounded.astype(jnp.float32)
    return total

def branch_pass(normed_rows, grad_branch, up_full, bias_up, down_full):
    hidden = jnp.dot(normed_rows, up_full, preferred_element_type=jnp.float32) + bias_up
    activation = gelu_exact(hidden).astype(jnp.bfloat16)
    branch = blockwise_sum(activation, down_full, True)
    grad_act = lax.dot_general(grad_branch, down_full, (((1,), (1,)), ((), ())), preferred_element_type=jnp.float32)
    grad_hidden = (grad_act * gelu_slope(hidden)).astype(jnp.bfloat16)
    grad_normed = blockwise_sum(grad_hidden, up_full, False)
    grad_up = lax.dot_general(normed_rows, grad_hidden, (((0,), (0,)), ((), ())), preferred_element_type=jnp.float32)
    grad_down_t = lax.dot_general(grad_branch, activation, (((0,), (0,)), ((), ())), preferred_element_type=jnp.float32)
    return (branch, grad_normed, grad_up, grad_down_t)

def ns_update(block, gram_matrix):
    polynomial = NS_B * gram_matrix + NS_C * jnp.dot(gram_matrix, gram_matrix, precision=HIGHEST_PREC, preferred_element_type=jnp.float32)
    return NS_A * block + jnp.dot(block, polynomial, precision=HIGHEST_PREC, preferred_element_type=jnp.float32)

def newton_schulz(gradient):
    scaled = gradient * lax.rsqrt(jnp.sum(gradient * gradient) + EPS_NORM)
    for sweep_index in range(ITERS_NS):
        gram_matrix = lax.dot_general(scaled, scaled, (((0,), (0,)), ((), ())), precision=HIGHEST_PREC, preferred_element_type=jnp.float32)
        scaled = ns_update(scaled, gram_matrix)
    return scaled

def reference(features, cotangent, depth_kernel, ln_gain, weight_up, bias_up, weight_down, layer_scale, tissue, lengths):
    margin = KERNEL // 2
    row_counts = (PATCH * lengths).astype(jnp.int32)
    row_starts = (jnp.cumsum(row_counts) - row_counts).astype(jnp.int32)
    buffer_row = jnp.arange(ROWS, dtype=jnp.int32)
    strip_owner = buffer_row // TILE_ROWS
    inner_row = buffer_row % TILE_ROWS
    row_live = inner_row < row_counts[strip_owner]
    target = jnp.where(row_live, row_starts[strip_owner] + inner_row, IMG_ROWS).astype(jnp.int32)
    source = jnp.minimum(target, IMG_ROWS - 1).astype(jnp.int32)
    patch_mask = jnp.repeat(jnp.repeat(tissue, PATCH, axis=0), PATCH, axis=1)

    def place(buffer_field):
        blank_field = jnp.zeros((IMG_ROWS,) + buffer_field.shape[1:], buffer_field.dtype)
        return blank_field.at[target].set(buffer_field, mode='drop')

    def pick(image_field):
        return jnp.where(row_live[:, None, None], image_field[source], jnp.zeros((), image_field.dtype))
    image = place(features).astype(jnp.float32)
    cot_image = place(cotangent).astype(jnp.float32)
    keep_mask = place(patch_mask).astype(jnp.float32)[:, :, None]
    mixed = depthwise(jnp.pad(image, ((margin, margin), (0, 0), (0, 0))), depth_kernel)
    centred, inv_std, normed = layer_norm(mixed, ln_gain)
    grad_branch = (keep_mask * layer_scale * cot_image).astype(jnp.bfloat16)
    branch, grad_normed, grad_up, grad_down_t = branch_pass(normed.reshape(-1, D), grad_branch.reshape(-1, D), weight_up, bias_up, weight_down)
    out_image = (image + keep_mask * layer_scale * branch.reshape(image.shape)).astype(jnp.bfloat16)
    grad_mixed = norm_back(grad_normed.reshape(image.shape), centred, inv_std, ln_gain)
    spread = depthwise(jnp.pad(grad_mixed, ((margin, margin), (0, 0), (0, 0))), depth_kernel[::-1, ::-1])
    grad_image = (cot_image + spread).astype(jnp.bfloat16)
    blocks_up = grad_up.reshape(D, N_OWN, MUON_COLS).transpose(1, 0, 2)
    blocks_down = grad_down_t.reshape(D, N_OWN, MUON_COLS).transpose(1, 0, 2)
    ortho_up = lax.map(newton_schulz, blocks_up).transpose(1, 0, 2).reshape(D, FF)
    ortho_down = lax.map(newton_schulz, blocks_down).transpose(1, 0, 2).reshape(D, FF)
    return (pick(out_image), pick(grad_image), ortho_up, ortho_down.T)
```

```python
import jax
import jax.numpy as jnp
from jax import lax
from jax.sharding import PartitionSpec as P

KERNEL = 7
PATCH = 8
PLANE = 4

INV_ROOT_TWO = 0.7071067811865476
INV_ROOT_TAU = 0.3989422804014327
NS_A = 3.4445
NS_B = -4.775
NS_C = 2.0315
EPS_NORM = 1e-06
F32 = jnp.float32
BF16 = jnp.bfloat16


def swap(value, axis, bit):
    return lax.ppermute(value, axis, [(i, i ^ bit) for i in range(lax.axis_size(axis))])


def neighbours(first, last):
    devices = lax.axis_size("tile")
    up = [(i, i + 1) for i in range(devices - 1)]
    down = [(i + 1, i) for i in range(devices - 1)]
    return lax.ppermute(last, "tile", up), lax.ppermute(first, "tile", down)


def in_order(blocks, index):
    bit = 1
    while bit < len(blocks):
        odd = (index // bit) % 2 == 1
        blocks = [jnp.where(odd, blocks[s ^ bit], blocks[s]) for s in range(len(blocks))]
        bit *= 2
    return blocks


def depthwise(framed, kernel):
    margin = kernel.shape[0] // 2
    padded = jnp.pad(framed, ((0, 0), (margin, margin), (0, 0)))
    row_count = framed.shape[0] - 2 * margin
    col_count = framed.shape[1]
    totals = jnp.zeros((row_count, col_count, framed.shape[2]), F32)
    for row_tap in range(kernel.shape[0]):
        for col_tap in range(kernel.shape[1]):
            totals = (
                totals
                + kernel[row_tap, col_tap]
                * padded[row_tap : row_tap + row_count, col_tap : col_tap + col_count]
            )
    return totals


def layer_norm(mixed, ln_gain):
    average = jnp.mean(mixed, axis=-1, keepdims=True)
    shifted = mixed - average
    variance = jnp.mean(shifted * shifted, axis=-1, keepdims=True)
    inv_std = lax.rsqrt(variance + 1e-06)
    centred = shifted * inv_std
    return (centred, inv_std, (centred * ln_gain).astype(BF16))


def norm_back(grad_normed, centred, inv_std, ln_gain):
    scaled_grad = grad_normed * ln_gain
    first_mean = jnp.mean(scaled_grad, axis=-1, keepdims=True)
    second_mean = jnp.mean(scaled_grad * centred, axis=-1, keepdims=True)
    return inv_std * (scaled_grad - first_mean - centred * second_mean)


def framed_share(field, live_rows, offset, share, margin):
    tail_rows = lax.dynamic_slice_in_dim(field, live_rows - margin, margin, 0)
    before, after = neighbours(field[:margin], tail_rows)
    blank_rows = jnp.zeros((margin,) + field.shape[1:], field.dtype)
    framed = jnp.concatenate([before, field, blank_rows], 0)
    framed = lax.dynamic_update_slice_in_dim(framed, after, live_rows + margin, 0)
    return lax.dynamic_slice_in_dim(framed, offset, share + 2 * margin, 0).astype(F32)


def dot(left, right, contract, precision=None):
    return lax.dot_general(
        left, right, (contract, ((), ())), precision=precision, preferred_element_type=F32
    )


def orthogonal_rows(grad_t, starts, height):
    high = lax.Precision.HIGH
    plain = ((1,), (0,))
    gram = dot(grad_t, grad_t, ((0,), (0,)))
    channels = gram.shape[0]
    diagonal = lax.broadcasted_iota(jnp.int32, gram.shape, 0) == lax.broadcasted_iota(
        jnp.int32, gram.shape, 1
    )
    scale = lax.rsqrt(jnp.sum(jnp.where(diagonal, gram, 0.0)) + EPS_NORM)
    gram = gram * (scale * scale)
    first = NS_B * gram + NS_C * dot(gram, gram, plain, high)
    half = NS_A * gram + dot(gram, first, plain, high)
    second_gram = NS_A * half + dot(half, first, plain, high)

    def rows(matrix):
        return jnp.concatenate([lax.dynamic_slice_in_dim(matrix, s, height, 0) for s in starts], 0)

    gram_rows = rows(second_gram)
    second = NS_B * gram_rows + NS_C * dot(gram_rows, second_gram, plain, high)
    column = lax.broadcasted_iota(jnp.int32, second.shape, 1)
    row = jnp.concatenate([s + jnp.arange(height) for s in starts])[:, None]
    both = (
        jnp.where(row == column, NS_A * NS_A, 0.0)
        + NS_A * (rows(first) + second)
        + dot(second, first, plain, high)
    ) * scale
    top = both.astype(BF16)
    rest = (both - top.astype(F32)).astype(BF16)
    across = ((1,), (1,))
    return dot(top, grad_t, across) + dot(rest, grad_t, across)


def shards(
    features,
    cotangent,
    depth_kernel,
    ln_gain,
    weight_up,
    bias_up,
    weight_down,
    layer_scale,
    tissue,
    lengths,
):
    tile_rows, columns, channels = features.shape
    margin = KERNEL // 2
    tiles = lax.axis_size("tile")
    owners = lax.axis_size("own")
    lines = tiles // PLANE
    tile = lax.axis_index("tile")
    own = lax.axis_index("own")
    place, line = tile % PLANE, tile // PLANE
    share = tile_rows // owners
    offset = own * share
    tokens = share * columns
    live_rows = PATCH * lengths[tile]
    row_live = jnp.arange(tile_rows) < live_rows
    mine_live = (offset + jnp.arange(share) < live_rows)[:, None, None]
    mine_tissue = jnp.repeat(tissue, PATCH, axis=0)
    mine_tissue = lax.dynamic_slice_in_dim(mine_tissue, offset, share, 0)
    mine_tissue = jnp.repeat(mine_tissue, PATCH, axis=1)[:, :, None]
    keep_scale = jnp.where(mine_live & (mine_tissue > 0), layer_scale, 0.0)
    mine_cot = lax.dynamic_slice_in_dim(cotangent, offset, share, 0).astype(F32)
    mine_inputs = lax.dynamic_slice_in_dim(features, offset, share, 0).astype(F32)

    units = weight_up.shape[1] // PLANE
    both_weights = jnp.stack([weight_up, weight_down.T])
    pieces = []
    for s in range(PLANE):
        piece = lax.dynamic_slice_in_dim(both_weights, (place ^ s) * units, units, 2)
        pieces.append(swap(piece, "tile", s) if s else piece)
    piece = jnp.concatenate(in_order(pieces, place), 1)
    pieces = [swap(piece, "tile", PLANE * s) if s else piece for s in range(lines)]
    weights = jnp.concatenate(in_order(pieces, line), 1)
    up, down_t = weights[0], weights[1]
    bias = lax.dynamic_slice_in_dim(bias_up, place * units, units, 0)

    def gather(mine):
        mine = mine.reshape(tokens, channels)
        mine = jnp.concatenate([mine] + [swap(mine, "tile", s) for s in range(1, PLANE)], 0)
        return jnp.concatenate([mine] + [swap(mine, "own", s) for s in range(1, owners)], 0)

    def scatter(partial):
        partial = partial.reshape(owners, PLANE * tokens, channels)
        total = partial[0]
        for s in range(1, owners):
            total = total + swap(partial[s].astype(BF16), "own", s).astype(F32)
        total = total.reshape(PLANE, tokens, channels)
        mine = total[0]
        for s in range(1, PLANE):
            mine = mine + swap(total[s].astype(BF16), "tile", s).astype(F32)
        return mine.reshape(share, columns, channels)

    grad_branch = gather((keep_scale * mine_cot).astype(BF16))
    inputs_live = jnp.where(row_live[:, None, None], features, jnp.zeros_like(features))
    mixed = depthwise(framed_share(inputs_live, live_rows, offset, share, margin), depth_kernel)
    centred, inv_std, normed = layer_norm(mixed, ln_gain)
    normed = gather(normed)

    plain, across, over_tokens = ((1,), (0,)), ((1,), (1,)), ((0,), (0,))
    hidden = dot(normed, up, plain) + bias
    cdf = 0.5 * (1.0 + lax.erf(hidden * INV_ROOT_TWO))
    act = (hidden * cdf).astype(BF16)
    slope = cdf + hidden * jnp.exp(-0.5 * hidden * hidden) * INV_ROOT_TAU
    grad_hidden = (dot(grad_branch, down_t, plain) * slope).astype(BF16)

    parts = jnp.concatenate(
        [dot(grad_hidden, normed, over_tokens), dot(act, grad_branch, over_tokens)], 0
    ).astype(BF16)
    kept = 2 * units // lines
    grad_t = lax.dynamic_slice_in_dim(parts, line * kept, kept, 0).astype(F32)
    for s in range(1, lines):
        part = lax.dynamic_slice_in_dim(parts, (line ^ s) * kept, kept, 0)
        grad_t = grad_t + swap(part, "tile", PLANE * s).astype(F32)
    grad_t = grad_t.astype(BF16)

    grad_normed = scatter(dot(grad_hidden, up, across))
    branch = scatter(dot(act, down_t, across))
    block_out = jnp.where(mine_live, mine_inputs + keep_scale * branch, 0.0).astype(BF16)

    half_lines = lines // 2
    blocks = [swap(grad_t, "tile", PLANE * s) if s else grad_t for s in range(half_lines)]
    block = jnp.concatenate(in_order(blocks, line % half_lines), 0)
    blocks = [swap(block, "tile", s) if s else block for s in range(PLANE)]
    whole_t = jnp.concatenate(in_order(blocks, place), 0)

    grad_mixed = jnp.where(mine_live, norm_back(grad_normed, centred, inv_std, ln_gain), 0.0)
    grad_mixed = grad_mixed.astype(BF16)
    grad_mixed = [swap(grad_mixed, "own", s) if s else grad_mixed for s in range(owners)]
    grad_mixed = jnp.concatenate(in_order(grad_mixed, own), 0)
    spread = depthwise(
        framed_share(grad_mixed, live_rows, offset, share, margin), depth_kernel[::-1, ::-1]
    )
    grad_features = jnp.where(mine_live, mine_cot + spread, 0.0).astype(BF16)

    height = channels // tiles
    other = tile ^ (PLANE * half_lines)
    ortho = orthogonal_rows(whole_t, (tile * height, other * height), height)
    mine, theirs = ortho[:height], swap(ortho[height:].astype(BF16), "tile", PLANE * half_lines)
    theirs = theirs.astype(F32)
    expands = line < half_lines
    muon_up = jnp.where(expands, mine, theirs)
    muon_down = jnp.where(expands, theirs, mine).T
    return (block_out, grad_features, muon_up, muon_down)


def solution(mesh):
    in_specs = (
        P("tile", None, None),
        P("tile", None, None),
        P(),
        P(),
        P("tile", "own"),
        P("own"),
        P("own", "tile"),
        P(),
        P("tile", None),
        P(),
    )
    out_specs = (
        P(("tile", "own"), None, None),
        P(("tile", "own"), None, None),
        P("tile", "own"),
        P("own", "tile"),
    )
    return jax.shard_map(shards, mesh=mesh, in_specs=in_specs, out_specs=out_specs, check_vma=False)
```

```python
import jax
import jax.numpy as jnp
from jax import lax
from jax.sharding import PartitionSpec as P

KERNEL = 7
PATCH = 8
PLANE = 4

INV_ROOT_TWO = 0.7071067811865476
INV_ROOT_TAU = 0.3989422804014327
NS_A = 3.4445
NS_B = -4.775
NS_C = 2.0315
EPS_NORM = 1e-06
F32 = jnp.float32
BF16 = jnp.bfloat16


def swap(value, axis, bit):
    return lax.ppermute(value, axis, [(i, i ^ bit) for i in range(lax.axis_size(axis))])


def neighbours(first, last):
    devices = lax.axis_size("tile")
    up = [(i, i + 1) for i in range(devices - 1)]
    down = [(i + 1, i) for i in range(devices - 1)]
    return lax.ppermute(last, "tile", up), lax.ppermute(first, "tile", down)


def exchange(blocks, groups):
    return lax.all_to_all(blocks, "tile", 0, 0, axis_index_groups=groups)


def in_order(blocks, index):
    bit = 1
    while bit < len(blocks):
        odd = (index // bit) % 2 == 1
        blocks = [jnp.where(odd, blocks[s ^ bit], blocks[s]) for s in range(len(blocks))]
        bit *= 2
    return blocks


def depthwise(framed, kernel):
    margin = kernel.shape[0] // 2
    padded = jnp.pad(framed, ((0, 0), (margin, margin), (0, 0)))
    row_count = framed.shape[0] - 2 * margin
    col_count = framed.shape[1]
    totals = jnp.zeros((row_count, col_count, framed.shape[2]), F32)
    for row_tap in range(kernel.shape[0]):
        for col_tap in range(kernel.shape[1]):
            totals = (
                totals
                + kernel[row_tap, col_tap]
                * padded[row_tap : row_tap + row_count, col_tap : col_tap + col_count]
            )
    return totals


def layer_norm(mixed, ln_gain):
    average = jnp.mean(mixed, axis=-1, keepdims=True)
    shifted = mixed - average
    variance = jnp.mean(shifted * shifted, axis=-1, keepdims=True)
    inv_std = lax.rsqrt(variance + 1e-06)
    centred = shifted * inv_std
    return (centred, inv_std, (centred * ln_gain).astype(BF16))


def norm_back(grad_normed, centred, inv_std, ln_gain):
    scaled_grad = grad_normed * ln_gain
    first_mean = jnp.mean(scaled_grad, axis=-1, keepdims=True)
    second_mean = jnp.mean(scaled_grad * centred, axis=-1, keepdims=True)
    return inv_std * (scaled_grad - first_mean - centred * second_mean)


def framed_share(field, live_rows, offset, share, margin):
    tail_rows = lax.dynamic_slice_in_dim(field, live_rows - margin, margin, 0)
    before, after = neighbours(field[:margin], tail_rows)
    blank_rows = jnp.zeros((margin,) + field.shape[1:], field.dtype)
    framed = jnp.concatenate([before, field, blank_rows], 0)
    framed = lax.dynamic_update_slice_in_dim(framed, after, live_rows + margin, 0)
    return lax.dynamic_slice_in_dim(framed, offset, share + 2 * margin, 0).astype(F32)


def dot(left, right, contract, precision=None):
    return lax.dot_general(
        left, right, (contract, ((), ())), precision=precision, preferred_element_type=F32
    )


def orthogonal_rows(grad_t, starts, height):
    high = lax.Precision.HIGH
    plain = ((1,), (0,))
    gram = dot(grad_t, grad_t, ((0,), (0,)))
    channels = gram.shape[0]
    diagonal = lax.broadcasted_iota(jnp.int32, gram.shape, 0) == lax.broadcasted_iota(
        jnp.int32, gram.shape, 1
    )
    scale = lax.rsqrt(jnp.sum(jnp.where(diagonal, gram, 0.0)) + EPS_NORM)
    gram = gram * (scale * scale)
    first = NS_B * gram + NS_C * dot(gram, gram, plain, high)
    half = NS_A * gram + dot(gram, first, plain, high)
    second_gram = NS_A * half + dot(half, first, plain, high)

    def rows(matrix):
        return jnp.concatenate([lax.dynamic_slice_in_dim(matrix, s, height, 0) for s in starts], 0)

    gram_rows = rows(second_gram)
    second = NS_B * gram_rows + NS_C * dot(gram_rows, second_gram, plain, high)
    column = lax.broadcasted_iota(jnp.int32, second.shape, 1)
    row = jnp.concatenate([s + jnp.arange(height) for s in starts])[:, None]
    both = (
        jnp.where(row == column, NS_A * NS_A, 0.0)
        + NS_A * (rows(first) + second)
        + dot(second, first, plain, high)
    ) * scale
    top = both.astype(BF16)
    rest = (both - top.astype(F32)).astype(BF16)
    across = ((1,), (1,))
    return dot(top, grad_t, across) + dot(rest, grad_t, across)


def shards(
    features,
    cotangent,
    depth_kernel,
    ln_gain,
    weight_up,
    bias_up,
    weight_down,
    layer_scale,
    tissue,
    lengths,
):
    tile_rows, columns, channels = features.shape
    margin = KERNEL // 2
    tiles = lax.axis_size("tile")
    owners = lax.axis_size("own")
    lines = tiles // PLANE
    tile = lax.axis_index("tile")
    own = lax.axis_index("own")
    place, line = tile % PLANE, tile // PLANE
    share = tile_rows // owners
    offset = own * share
    tokens = share * columns
    live_rows = PATCH * lengths[tile]
    row_live = jnp.arange(tile_rows) < live_rows
    mine_live = (offset + jnp.arange(share) < live_rows)[:, None, None]
    mine_tissue = jnp.repeat(tissue, PATCH, axis=0)
    mine_tissue = lax.dynamic_slice_in_dim(mine_tissue, offset, share, 0)
    mine_tissue = jnp.repeat(mine_tissue, PATCH, axis=1)[:, :, None]
    keep_scale = jnp.where(mine_live & (mine_tissue > 0), layer_scale, 0.0)
    mine_cot = lax.dynamic_slice_in_dim(cotangent, offset, share, 0).astype(F32)
    mine_inputs = lax.dynamic_slice_in_dim(features, offset, share, 0).astype(F32)

    planes = [[i * PLANE + j for j in range(PLANE)] for i in range(lines)]
    columns_z = [[i * PLANE + j for i in range(lines)] for j in range(PLANE)]
    height = channels // tiles
    units = weight_up.shape[1] // PLANE
    both_weights = jnp.stack([weight_up, weight_down.T])
    pieces = both_weights.reshape(2, height, PLANE, units).transpose(2, 0, 1, 3)
    pieces = exchange(pieces, planes)
    pieces = pieces.transpose(1, 0, 2, 3).reshape(2, PLANE * height, units)
    pieces = exchange(jnp.broadcast_to(pieces, (lines,) + pieces.shape), columns_z)
    up = pieces[:, 0].reshape(channels, units)
    down_t = pieces[:, 1].reshape(channels, units)
    bias = lax.dynamic_slice_in_dim(bias_up, place * units, units, 0)

    def gather(mine):
        mine = mine.reshape(tokens, channels)
        mine = exchange(jnp.broadcast_to(mine, (PLANE,) + mine.shape), planes)
        mine = mine.reshape(PLANE * tokens, channels)
        return jnp.concatenate([mine] + [swap(mine, "own", s) for s in range(1, owners)], 0)

    def scatter(partials):
        partials = jnp.stack(partials).reshape(2, owners, PLANE, tokens, channels)
        total = partials[:, 0]
        for s in range(1, owners):
            total = total + swap(partials[:, s].astype(BF16), "own", s).astype(F32)
        total = exchange(total.astype(BF16).transpose(1, 0, 2, 3), planes).astype(F32)
        return jnp.sum(total, 0).reshape(2, share, columns, channels)

    grad_branch = gather((keep_scale * mine_cot).astype(BF16))
    inputs_live = jnp.where(row_live[:, None, None], features, jnp.zeros_like(features))
    mixed = depthwise(framed_share(inputs_live, live_rows, offset, share, margin), depth_kernel)
    centred, inv_std, normed = layer_norm(mixed, ln_gain)
    normed = gather(normed)

    plain, across, over_tokens = ((1,), (0,)), ((1,), (1,)), ((0,), (0,))
    hidden = dot(normed, up, plain) + bias
    cdf = 0.5 * (1.0 + lax.erf(hidden * INV_ROOT_TWO))
    act = (hidden * cdf).astype(BF16)
    slope = cdf + hidden * jnp.exp(-0.5 * hidden * hidden) * INV_ROOT_TAU
    grad_hidden = (dot(grad_branch, down_t, plain) * slope).astype(BF16)

    parts = jnp.concatenate(
        [dot(grad_hidden, normed, over_tokens), dot(act, grad_branch, over_tokens)], 0
    ).astype(BF16)
    kept = 2 * units // lines
    parts = exchange(parts.reshape(lines, kept, channels), columns_z)
    grad_t = jnp.sum(parts.astype(F32), 0).astype(BF16)

    grad_normed, branch = scatter([dot(grad_hidden, up, across), dot(act, down_t, across)])
    block_out = jnp.where(mine_live, mine_inputs + keep_scale * branch, 0.0).astype(BF16)

    half_lines = lines // 2
    blocks = [swap(grad_t, "tile", PLANE * s) if s else grad_t for s in range(half_lines)]
    block = jnp.concatenate(in_order(blocks, line % half_lines), 0)
    blocks = exchange(jnp.broadcast_to(block, (PLANE,) + block.shape), planes)
    whole_t = blocks.reshape(-1, channels)

    grad_mixed = jnp.where(mine_live, norm_back(grad_normed, centred, inv_std, ln_gain), 0.0)
    grad_mixed = grad_mixed.astype(BF16)
    grad_mixed = [swap(grad_mixed, "own", s) if s else grad_mixed for s in range(owners)]
    grad_mixed = jnp.concatenate(in_order(grad_mixed, own), 0)
    spread = depthwise(
        framed_share(grad_mixed, live_rows, offset, share, margin), depth_kernel[::-1, ::-1]
    )
    grad_features = jnp.where(mine_live, mine_cot + spread, 0.0).astype(BF16)

    other = tile ^ (PLANE * half_lines)
    ortho = orthogonal_rows(whole_t, (tile * height, other * height), height)
    mine, theirs = ortho[:height], swap(ortho[height:].astype(BF16), "tile", PLANE * half_lines)
    theirs = theirs.astype(F32)
    expands = line < half_lines
    muon_up = jnp.where(expands, mine, theirs)
    muon_down = jnp.where(expands, theirs, mine).T
    return (block_out, grad_features, muon_up, muon_down)


def solution(mesh):
    in_specs = (
        P("tile", None, None),
        P("tile", None, None),
        P(),
        P(),
        P("tile", "own"),
        P("own"),
        P("own", "tile"),
        P(),
        P("tile", None),
        P(),
    )
    out_specs = (
        P(("tile", "own"), None, None),
        P(("tile", "own"), None, None),
        P("tile", "own"),
        P("own", "tile"),
    )
    return jax.shard_map(shards, mesh=mesh, in_specs=in_specs, out_specs=out_specs, check_vma=False)
```

```python
import jax
import jax.numpy as jnp
from jax import lax
from jax.experimental import pallas as pl
from jax.experimental.pallas import tpu as pltpu
from jax.sharding import PartitionSpec as P

KERNEL = 7
PATCH = 8
COLS = 8
MARGIN = KERNEL // 2
RIM = MARGIN + 1
PLANE = 4
LANES = 128
CHUNK = 8

INV_ROOT_TWO = 0.7071067811865476
INV_ROOT_TAU = 0.3989422804014327
NS_A = 3.4445
NS_B = -4.775
NS_C = 2.0315
EPS_NORM = 1e-06
F32 = jnp.float32
BF16 = jnp.bfloat16


def swap(value, axis, bit):
    return lax.ppermute(value, axis, [(i, i ^ bit) for i in range(lax.axis_size(axis))])


def neighbours(first, last):
    devices = lax.axis_size("tile")
    up = [(i, i + 1) for i in range(devices - 1)]
    down = [(i + 1, i) for i in range(devices - 1)]
    return lax.ppermute(last, "tile", up), lax.ppermute(first, "tile", down)


def in_order(blocks, index):
    bit = 1
    while bit < len(blocks):
        odd = (index & bit) != 0
        blocks = [jnp.where(odd, blocks[s ^ bit], blocks[s]) for s in range(len(blocks))]
        bit *= 2
    return blocks


def call(kernel, out_shape, scratch, flops, *operands, scalars=1):
    smem = pl.BlockSpec(memory_space=pltpu.SMEM)
    vmem = pl.BlockSpec(memory_space=pltpu.VMEM)
    return pl.pallas_call(
        kernel,
        out_shape=out_shape,
        in_specs=[smem] * scalars + [vmem] * (len(operands) - scalars),
        out_specs=[vmem] * len(out_shape),
        scratch_shapes=scratch,
        compiler_params=pltpu.CompilerParams(vmem_limit_bytes=40 * 2**20),
        cost_estimate=pl.CostEstimate(flops=flops, bytes_accessed=2**20, transcendentals=0),
    )(*operands)


def convolve(framed, kernel_ref, offset, out_ref, flipped):
    share, columns, channels = out_ref.shape
    chunk = min(CHUNK, share)
    lane_steps = channels // LANES
    column = lax.broadcasted_iota(jnp.int32, (chunk + 2 * MARGIN, columns, LANES), 1)

    def step(index, carry):
        lanes = pl.ds(pl.multiple_of((index % lane_steps) * LANES, LANES), LANES)
        first = (index // lane_steps) * chunk
        rows = framed[pl.ds(offset + first, chunk + 2 * MARGIN), :, lanes]
        total = jnp.zeros((chunk, columns, LANES), F32)
        for col_tap in range(KERNEL):
            reach = col_tap - MARGIN
            moved = rows
            if reach:
                moved = pltpu.roll(rows, (-reach) % columns, 1)
                inside = (column + reach >= 0) & (column + reach < columns)
                moved = jnp.where(inside, moved, 0.0)
            for row_tap in range(KERNEL):
                tap = row_tap * KERNEL + col_tap
                tap = KERNEL * KERNEL - 1 - tap if flipped else tap
                weight = kernel_ref[pl.ds(tap, 1), lanes][None]
                total = total + weight * moved[row_tap : row_tap + chunk]
        out_ref[pl.ds(first, chunk), :, lanes] = total
        return carry

    lax.fori_loop(0, lane_steps * (share // chunk), step, 0)


def place_strip(framed, pieces, before_ref, after_ref, live_rows):
    columns, channels = framed.shape[1:]

    def rows_of(ref):
        value = ref[...].astype(F32)
        return value.reshape(value.shape[0] // columns, columns, channels)

    for start, ref in pieces:
        rows = rows_of(ref)
        framed[pl.ds(start + MARGIN, rows.shape[0])] = rows
    framed[pl.ds(framed.shape[0] - MARGIN, MARGIN)] = jnp.zeros((MARGIN, columns, channels), F32)
    framed[pl.ds(0, MARGIN)] = rows_of(before_ref)[RIM - MARGIN :]
    framed[pl.ds(live_rows + MARGIN, MARGIN)] = rows_of(after_ref)[:MARGIN]


def forward_kernel(
    scalars, strip, before, after, taps, gain, normed, centred_out, inverse, framed, mixed
):
    place_strip(framed, [(0, strip)], before, after, scalars[0])
    convolve(framed, taps, scalars[1], mixed, False)
    value = mixed[...].reshape(normed.shape)
    channels = value.shape[1]
    shifted = value - jnp.sum(value, 1, keepdims=True) / channels
    variance = jnp.sum(shifted * shifted, 1, keepdims=True) / channels
    inv_std = lax.rsqrt(variance + 1e-06)
    centred = shifted * inv_std
    centred_out[...] = centred
    inverse[...] = jnp.broadcast_to(inv_std, inverse.shape)
    normed[...] = (centred * gain[...]).astype(BF16)


def middle_kernel(
    scalars, strip, total, one, two, three, centred, inverse, gain, layer_scale, grad_mixed, block_out
):
    tokens, channels = grad_mixed.shape
    start = pl.multiple_of(scalars[1] * COLS, 16)
    row = scalars[1] + lax.broadcasted_iota(jnp.int32, (tokens, 1), 0) // COLS
    keep = jnp.zeros((tokens, 1), F32)
    for patch in range(strip.shape[0] // (COLS * PATCH)):
        keep = jnp.where(row // PATCH == patch, scalars[2 + patch].astype(F32), keep)
    live = row < scalars[0]

    def summed(which):
        value = total[which].astype(F32)
        for ref in (one, two, three):
            value = value + ref[which].astype(F32)
        return value

    inputs = strip[pl.ds(start, tokens), :].astype(F32)
    block = inputs + keep * layer_scale[...] * summed(1)
    block_out[...] = jnp.where(live, block, 0.0).astype(BF16)
    scaled_grad = summed(0) * gain[...]
    first_mean = jnp.sum(scaled_grad, 1, keepdims=True) / channels
    second_mean = jnp.sum(scaled_grad * centred[...], 1, keepdims=True) / channels
    value = inverse[:, :1] * (scaled_grad - first_mean - centred[...] * second_mean)
    grad_mixed[...] = jnp.where(live, value, 0.0).astype(BF16)


def weights_kernel(scalars, *refs):
    *pieces, up, down_t = refs
    rows = pieces[0].shape[1]
    for s, piece in enumerate(pieces):
        start = pl.multiple_of((scalars[0] ^ s) * rows, rows)
        up[pl.ds(start, rows), :] = piece[0]
        down_t[pl.ds(start, rows), :] = piece[1]


def backward_kernel(scalars, cotangent, before, after, taps, *rest):
    *pieces, grad_features, framed, spread = rest
    tokens = grad_features.shape[0]
    share = spread.shape[0]
    own = scalars[1] // share
    placed = [((own ^ s) * share, piece) for s, piece in enumerate(pieces)]
    place_strip(framed, placed, before, after, scalars[0])
    convolve(framed, taps, scalars[1], spread, True)
    start = pl.multiple_of(scalars[1] * COLS, 16)
    value = cotangent[pl.ds(start, tokens), :].astype(F32) + spread[...].reshape(grad_features.shape)
    row = scalars[1] + lax.broadcasted_iota(jnp.int32, (tokens, 1), 0) // COLS
    grad_features[...] = jnp.where(row < scalars[0], value, 0.0).astype(BF16)


def dot(left, right, contract, precision=None):
    return lax.dot_general(
        left, right, (contract, ((), ())), precision=precision, preferred_element_type=F32
    )


def member_bits(entry, turn, group):
    bits = group.bit_length() - 1
    return sum(1 << ((i + turn) % bits) for i in range(bits) if entry >> i & 1)


def hidden_block(member, group):
    return (member & (PLANE - 1)) * (group // PLANE) + (member >> (PLANE.bit_length() - 1))


def ortho_kernel(scalars, *refs):
    *gathered, mine, theirs, whole, gram, first, half = refs
    channels = whole.shape[1]
    if len(gathered) == 1:
        whole[...] = gathered[0][...]
    else:
        group, third, _ = gathered[0].shape
        for turn, ref in enumerate(gathered):
            for e in range(group):
                block = hidden_block(scalars[2] ^ member_bits(e, turn, group), group)
                start = pl.multiple_of((block * 3 + turn) * third, third)
                whole[pl.ds(start, third), :] = ref[e]

    plain = ((1,), (0,))
    steps = [pl.ds(i, 256) for i in range(0, channels, 256)]
    value = whole[...]
    squares = jnp.zeros((1, 1), F32)
    for rows in steps:
        product = dot(value[:, rows.start : rows.start + 256], value, ((0,), (0,)))
        row = rows.start + lax.broadcasted_iota(jnp.int32, product.shape, 0)
        column = lax.broadcasted_iota(jnp.int32, product.shape, 1)
        on_diagonal = jnp.where(row == column, product, 0.0)
        squares = squares + jnp.sum(jnp.sum(on_diagonal, 1, keepdims=True), 0, keepdims=True)
        gram[rows, :] = product
    scale = lax.rsqrt(squares + EPS_NORM)
    gram[...] = gram[...] * (scale * scale)

    low = gram[...].astype(BF16)
    for rows in steps:
        first[rows, :] = NS_B * gram[rows, :] + NS_C * dot(low[rows.start : rows.start + 256], low, plain)
    first_low = first[...].astype(BF16)
    for rows in steps:
        product = dot(low[rows.start : rows.start + 256], first_low, plain)
        half[rows, :] = NS_A * gram[rows, :] + product
    half_low = half[...].astype(BF16)
    for rows in steps:
        product = dot(half_low[rows.start : rows.start + 256], first_low, plain)
        gram[rows, :] = NS_A * half[rows, :] + product

    height = mine.shape[0]
    picked = -(-2 * height // 16) * 16
    row = lax.broadcasted_iota(jnp.int32, (picked, channels), 0)
    column = lax.broadcasted_iota(jnp.int32, (picked, channels), 1)
    wanted = jnp.where(row < height, scalars[0] + row, scalars[1] + row - height)
    chosen = (column == wanted) & (row < 2 * height)
    pick = jnp.where(chosen, 1.0, 0.0).astype(BF16)

    def halves(matrix):
        top = matrix.astype(BF16)
        return top, (matrix - top.astype(F32)).astype(BF16)

    def rows_of(matrix):
        top, rest = halves(matrix)
        return dot(pick, top, plain) + dot(pick, rest, plain)

    second_gram = gram[...]
    gram_rows = rows_of(second_gram)
    second = NS_B * gram_rows
    second = second + NS_C * dot(gram_rows.astype(BF16), second_gram.astype(BF16), plain)
    both = (
        jnp.where(chosen, NS_A * NS_A, 0.0)
        + NS_A * (rows_of(first[...]) + second)
        + dot(second.astype(BF16), first_low, plain)
    ) * scale
    top, rest = halves(both)
    across = ((1,), (1,))
    for start in range(0, value.shape[0], 256):
        step = min(256, value.shape[0] - start)
        piece = value[start : start + step]
        out = dot(top, piece, across) + dot(rest, piece, across)
        mine[:, start : start + step] = out[:height]
        theirs[:, start : start + step] = out[height : 2 * height].astype(BF16)


def shards(
    features,
    cotangent,
    depth_kernel,
    ln_gain,
    weight_up,
    bias_up,
    weight_down,
    layer_scale,
    tissue,
    lengths,
):
    tile_rows, columns, channels = features.shape
    tiles = lax.axis_size("tile")
    owners = lax.axis_size("own")
    lines = tiles // PLANE
    half_lines = lines // 2
    tile = lax.axis_index("tile")
    own = lax.axis_index("own")
    place, line = tile & (PLANE - 1), tile >> (PLANE.bit_length() - 1)
    share = tile_rows // owners
    offset = own * share
    tokens = share * columns
    live_rows = PATCH * lengths[tile]
    row = offset + jnp.arange(share)
    keep = jnp.repeat(tissue[:, 0], PATCH, axis=0)
    keep = lax.dynamic_slice_in_dim(keep, offset, share, 0) * (row < live_rows)
    mine_cot = lax.dynamic_slice_in_dim(cotangent, offset, share, 0).astype(F32)
    grad_branch = (keep.astype(F32)[:, None, None] * layer_scale * mine_cot).astype(BF16)
    scalars = jnp.concatenate([jnp.stack([live_rows, offset]), tissue[:, 0]])
    scalars = scalars.astype(jnp.int32)
    strip = features.reshape(tile_rows * columns, channels)
    taps = depth_kernel.reshape(KERNEL * KERNEL, channels)
    gain, scale = ln_gain[None], layer_scale[None]
    frame = pltpu.VMEM((tile_rows + 2 * MARGIN, columns, channels), F32)
    wide = pltpu.VMEM((share, columns, channels), F32)
    rim = RIM * columns

    units = weight_up.shape[1] // PLANE
    both_weights = jnp.stack([weight_up, weight_down.T])
    pieces = []
    for s in range(PLANE):
        piece = lax.dynamic_slice_in_dim(both_weights, (place ^ s) * units, units, 2)
        pieces.append(swap(piece, "tile", s) if s else piece)
    piece = jnp.concatenate(in_order(pieces, place), 1)

    tail = lax.dynamic_slice_in_dim(strip, (live_rows - RIM) * columns, rim, 0)
    before, after = neighbours(strip[:rim], tail)
    piece, before, after = lax.optimization_barrier((piece, before, after))
    pieces = [swap(piece, "tile", PLANE * s) if s else piece for s in range(lines)]
    up, down_t = call(
        weights_kernel,
        [jax.ShapeDtypeStruct((channels, units), BF16)] * 2,
        [],
        10 * 10**9,
        line[None], *pieces,
    )
    bias = lax.dynamic_slice_in_dim(bias_up, place * units, units, 0)

    def gather(mine):
        mine = jnp.concatenate([mine] + [swap(mine, "tile", s) for s in range(1, PLANE)], 0)
        return jnp.concatenate([mine] + [swap(mine, "own", s) for s in range(1, owners)], 0)

    grad_branch = gather(grad_branch.reshape(tokens, channels))
    normed, centred, inverse = call(
        forward_kernel,
        [
            jax.ShapeDtypeStruct((tokens, channels), BF16),
            jax.ShapeDtypeStruct((tokens, channels), F32),
            jax.ShapeDtypeStruct((tokens, LANES), F32),
        ],
        [frame, wide],
        10**6,
        scalars, strip, before, after, taps, gain,
    )
    normed = gather(normed)

    plain, across, over_tokens = ((1,), (0,)), ((1,), (1,)), ((0,), (0,))
    hidden = dot(normed, up, plain) + bias
    cdf = 0.5 * (1.0 + lax.erf(hidden * INV_ROOT_TWO))
    act = (hidden * cdf).astype(BF16)
    slope = cdf + hidden * jnp.exp(-0.5 * hidden * hidden) * INV_ROOT_TAU
    grad_hidden = (dot(grad_branch, down_t, plain) * slope).astype(BF16)

    parts = jnp.concatenate(
        [dot(grad_hidden, normed, over_tokens), dot(act, grad_branch, over_tokens)], 0
    ).astype(BF16)
    parts, grad_hidden, act = lax.optimization_barrier((parts, grad_hidden, act))
    kept = 2 * units // lines
    grad_t = lax.dynamic_slice_in_dim(parts, line * kept, kept, 0).astype(F32)
    arrived = []
    for s in range(1, lines):
        part = lax.dynamic_slice_in_dim(parts, (line ^ s) * kept, kept, 0)
        arrived.append(swap(part, "tile", PLANE * s))

    partial = jnp.stack([dot(grad_hidden, up, across), dot(act, down_t, across)])
    partial = partial.reshape(2, owners, PLANE, tokens, channels)
    total = partial[:, 0]
    for s in range(1, owners):
        total = total + swap(partial[:, s].astype(BF16), "own", s).astype(F32)
    total = total.astype(BF16)
    moved = [swap(total[:, s], "tile", s) for s in range(1, PLANE)]
    grad_mixed, block_out = call(
        middle_kernel,
        [jax.ShapeDtypeStruct((tokens, channels), BF16)] * 2,
        [],
        10**6,
        scalars, strip, total[:, 0], *moved, centred, inverse, gain, scale,
    )

    grad_t = (grad_t + sum(part.astype(F32) for part in arrived)).astype(BF16)
    group = PLANE * half_lines
    bits = [1 << i for i in range(group.bit_length() - 1)]
    third = kept // 3
    thirds = []
    for turn in range(3):
        held = grad_t[turn * third : (turn + 1) * third][None]
        order = bits[turn:] + bits[:turn]
        for bit in order:
            held = jnp.concatenate([held, swap(held, "tile", bit)], 0)
        thirds.append(held)

    halves = [grad_mixed] + [swap(grad_mixed, "own", s) for s in range(1, owners)]
    stacked = jnp.stack(halves)
    head = lax.dynamic_slice_in_dim(stacked, own, 1, 0)[0, :rim]
    last = live_rows - RIM
    tail = lax.dynamic_slice(
        stacked, ((last >> (share.bit_length() - 1)) ^ own, (last & (share - 1)) * columns, 0), (1, rim, channels)
    )[0]
    before, after = neighbours(head, tail)
    (grad_features,) = call(
        backward_kernel,
        [jax.ShapeDtypeStruct((tokens, channels), BF16)],
        [frame, wide],
        10**6,
        scalars, cotangent.reshape(strip.shape), before, after, taps, *halves,
    )

    height = channels // tiles
    other = tile ^ (PLANE * half_lines)
    square = pltpu.VMEM((channels, channels), F32)
    thirds, grad_features = lax.optimization_barrier((thirds, grad_features))
    if third % 16:
        entries = [(e, turn) for turn in range(3) for e in range(group)]
        slots = [
            hidden_block((tile & (group - 1)) ^ member_bits(e, turn, group), group) * 3 + turn
            for e, turn in entries
        ]
        ordered = jnp.zeros((3 * group, third, channels), BF16)
        ordered = ordered.at[jnp.stack(slots)].set(jnp.concatenate(thirds, 0))
        thirds = [ordered.reshape(-1, channels)]
    mine, theirs = call(
        ortho_kernel,
        [
            jax.ShapeDtypeStruct((height, weight_up.shape[1]), F32),
            jax.ShapeDtypeStruct((height, weight_up.shape[1]), BF16),
        ],
        [pltpu.VMEM((weight_up.shape[1], channels), BF16), square, square, square],
        10 * 10**9,
        jnp.stack([tile * height, other * height, tile & (group - 1)]), *thirds,
    )
    theirs = swap(theirs, "tile", PLANE * half_lines)
    theirs = theirs.astype(F32)
    expands = line < half_lines
    muon_up = jnp.where(expands, mine, theirs)
    muon_down = jnp.where(expands, theirs, mine).T
    shape = (share, columns, channels)
    return (block_out.reshape(shape), grad_features.reshape(shape), muon_up, muon_down)


def solution(mesh):
    in_specs = (
        P("tile", None, None),
        P("tile", None, None),
        P(),
        P(),
        P("tile", "own"),
        P("own"),
        P("own", "tile"),
        P(),
        P("tile", None),
        P(),
    )
    out_specs = (
        P(("tile", "own"), None, None),
        P(("tile", "own"), None, None),
        P("tile", "own"),
        P("own", "tile"),
    )
    return jax.shard_map(shards, mesh=mesh, in_specs=in_specs, out_specs=out_specs, check_vma=False)
```

```python
import jax
import jax.numpy as jnp
from jax import lax
from jax.experimental import pallas as pl
from jax.experimental.pallas import tpu as pltpu
from jax.sharding import PartitionSpec as P

KERNEL = 7
PATCH = 8
COLS = 8
MARGIN = KERNEL // 2
RIM = MARGIN + 1
PLANE = 4
LANES = 128
CHUNK = 8

INV_ROOT_TWO = 0.7071067811865476
INV_ROOT_TAU = 0.3989422804014327
NS_A = 3.4445
NS_B = -4.775
NS_C = 2.0315
EPS_NORM = 1e-06
F32 = jnp.float32
BF16 = jnp.bfloat16


def swap(value, axis, bit):
    return lax.ppermute(value, axis, [(i, i ^ bit) for i in range(lax.axis_size(axis))])


def neighbours(first, last):
    devices = lax.axis_size("tile")
    up = [(i, i + 1) for i in range(devices - 1)]
    down = [(i + 1, i) for i in range(devices - 1)]
    return lax.ppermute(last, "tile", up), lax.ppermute(first, "tile", down)


def in_order(blocks, index):
    bit = 1
    while bit < len(blocks):
        odd = (index & bit) != 0
        blocks = [jnp.where(odd, blocks[s ^ bit], blocks[s]) for s in range(len(blocks))]
        bit *= 2
    return blocks


def call(kernel, out_shape, scratch, flops, *operands, scalars=1):
    smem = pl.BlockSpec(memory_space=pltpu.SMEM)
    vmem = pl.BlockSpec(memory_space=pltpu.VMEM)
    return pl.pallas_call(
        kernel,
        out_shape=out_shape,
        in_specs=[smem] * scalars + [vmem] * (len(operands) - scalars),
        out_specs=[vmem] * len(out_shape),
        scratch_shapes=scratch,
        compiler_params=pltpu.CompilerParams(vmem_limit_bytes=40 * 2**20),
        cost_estimate=pl.CostEstimate(flops=flops, bytes_accessed=2**20, transcendentals=0),
    )(*operands)


def convolve(framed, kernel_ref, offset, out_ref, flipped):
    share, columns, channels = out_ref.shape
    chunk = min(CHUNK, share)
    lane_steps = channels // LANES
    column = lax.broadcasted_iota(jnp.int32, (chunk + 2 * MARGIN, columns, LANES), 1)

    def step(index, carry):
        lanes = pl.ds(pl.multiple_of((index % lane_steps) * LANES, LANES), LANES)
        first = (index // lane_steps) * chunk
        rows = framed[pl.ds(offset + first, chunk + 2 * MARGIN), :, lanes]
        total = jnp.zeros((chunk, columns, LANES), F32)
        for col_tap in range(KERNEL):
            reach = col_tap - MARGIN
            moved = rows
            if reach:
                moved = pltpu.roll(rows, (-reach) % columns, 1)
                inside = (column + reach >= 0) & (column + reach < columns)
                moved = jnp.where(inside, moved, 0.0)
            for row_tap in range(KERNEL):
                tap = row_tap * KERNEL + col_tap
                tap = KERNEL * KERNEL - 1 - tap if flipped else tap
                weight = kernel_ref[pl.ds(tap, 1), lanes][None]
                total = total + weight * moved[row_tap : row_tap + chunk]
        out_ref[pl.ds(first, chunk), :, lanes] = total
        return carry

    lax.fori_loop(0, lane_steps * (share // chunk), step, 0)


def place_strip(framed, pieces, before_ref, after_ref, live_rows):
    columns, channels = framed.shape[1:]

    def rows_of(ref):
        value = ref[...].astype(F32)
        return value.reshape(value.shape[0] // columns, columns, channels)

    for start, ref in pieces:
        rows = rows_of(ref)
        framed[pl.ds(start + MARGIN, rows.shape[0])] = rows
    framed[pl.ds(framed.shape[0] - MARGIN, MARGIN)] = jnp.zeros((MARGIN, columns, channels), F32)
    framed[pl.ds(0, MARGIN)] = rows_of(before_ref)[RIM - MARGIN :]
    framed[pl.ds(live_rows + MARGIN, MARGIN)] = rows_of(after_ref)[:MARGIN]


def kept_rows(scalars, tokens, patches):
    row = scalars[1] + lax.broadcasted_iota(jnp.int32, (tokens, 1), 0) // COLS
    keep = jnp.zeros((tokens, 1), F32)
    for patch in range(patches):
        keep = jnp.where(row // PATCH == patch, scalars[2 + patch].astype(F32), keep)
    live = row < scalars[0]
    return live, jnp.where(live, keep, 0.0)


def forward_kernel(
    scalars,
    strip,
    cotangent,
    before,
    after,
    taps,
    gain,
    layer_scale,
    sent,
    centred_out,
    inverse,
    framed,
    mixed,
):
    place_strip(framed, [(0, strip)], before, after, scalars[0])
    convolve(framed, taps, scalars[1], mixed, False)
    tokens, channels = centred_out.shape
    value = mixed[...].reshape(tokens, channels)
    shifted = value - jnp.sum(value, 1, keepdims=True) / channels
    variance = jnp.sum(shifted * shifted, 1, keepdims=True) / channels
    inv_std = lax.rsqrt(variance + 1e-06)
    centred = shifted * inv_std
    centred_out[...] = centred
    inverse[...] = jnp.broadcast_to(inv_std, inverse.shape)
    sent[0] = (centred * gain[...]).astype(BF16)
    _, keep = kept_rows(scalars, tokens, strip.shape[0] // (COLS * PATCH))
    start = pl.multiple_of(scalars[1] * COLS, 16)
    grad_out = cotangent[pl.ds(start, tokens), :].astype(F32)
    sent[1] = (keep * layer_scale[...] * grad_out).astype(BF16)


def middle_kernel(
    scalars, strip, total, one, two, three, centred, inverse, gain, layer_scale, grad_mixed, block_out
):
    tokens, channels = grad_mixed.shape
    start = pl.multiple_of(scalars[1] * COLS, 16)
    live, keep = kept_rows(scalars, tokens, strip.shape[0] // (COLS * PATCH))

    def summed(which):
        value = total[which].astype(F32)
        for ref in (one, two, three):
            value = value + ref[which].astype(F32)
        return value

    inputs = strip[pl.ds(start, tokens), :].astype(F32)
    block = inputs + keep * layer_scale[...] * summed(1)
    block_out[...] = jnp.where(live, block, 0.0).astype(BF16)
    scaled_grad = summed(0) * gain[...]
    first_mean = jnp.sum(scaled_grad, 1, keepdims=True) / channels
    second_mean = jnp.sum(scaled_grad * centred[...], 1, keepdims=True) / channels
    value = inverse[:, :1] * (scaled_grad - first_mean - centred[...] * second_mean)
    grad_mixed[...] = jnp.where(live, value, 0.0).astype(BF16)


def weights_kernel(scalars, held, up, down_t):
    lines, _, rows, _ = held.shape
    bits = lines.bit_length() - 1
    for e in range(lines):
        apart = sum(lines >> (i + 1) for i in range(bits) if e >> i & 1)
        start = pl.multiple_of((scalars[0] ^ apart) * rows, rows)
        up[pl.ds(start, rows), :] = held[e, 0]
        down_t[pl.ds(start, rows), :] = held[e, 1]


def backward_kernel(scalars, cotangent, before, after, taps, *rest):
    *pieces, grad_features, framed, spread = rest
    tokens = grad_features.shape[0]
    share = spread.shape[0]
    own = scalars[1] // share
    placed = [((own ^ s) * share, piece) for s, piece in enumerate(pieces)]
    place_strip(framed, placed, before, after, scalars[0])
    convolve(framed, taps, scalars[1], spread, True)
    start = pl.multiple_of(scalars[1] * COLS, 16)
    value = cotangent[pl.ds(start, tokens), :].astype(F32) + spread[...].reshape(grad_features.shape)
    row = scalars[1] + lax.broadcasted_iota(jnp.int32, (tokens, 1), 0) // COLS
    grad_features[...] = jnp.where(row < scalars[0], value, 0.0).astype(BF16)


def dot(left, right, contract, precision=None):
    return lax.dot_general(
        left, right, (contract, ((), ())), precision=precision, preferred_element_type=F32
    )


def member_bits(entry, turn, group):
    bits = group.bit_length() - 1
    return sum(1 << ((i + turn) % bits) for i in range(bits) if entry >> i & 1)


def hidden_block(member, group):
    return (member & (PLANE - 1)) * (group // PLANE) + (member >> (PLANE.bit_length() - 1))


def ortho_kernel(scalars, *refs):
    *gathered, mine, theirs, whole, gram, first, half = refs
    channels = whole.shape[1]
    if len(gathered) == 1:
        whole[...] = gathered[0][...]
    else:
        group, third, _ = gathered[0].shape
        group *= 2
        for turn in range(3):
            for e in range(group):
                block = hidden_block(scalars[2] ^ member_bits(e, turn, group), group)
                start = pl.multiple_of((block * 3 + turn) * third, third)
                later, entry = divmod(e, group // 2)
                whole[pl.ds(start, third), :] = gathered[2 * turn + later][entry]

    plain = ((1,), (0,))
    steps = [pl.ds(i, 256) for i in range(0, channels, 256)]
    value = whole[...]
    squares = jnp.zeros((1, 1), F32)
    for rows in steps:
        product = dot(value[:, rows.start : rows.start + 256], value, ((0,), (0,)))
        row = rows.start + lax.broadcasted_iota(jnp.int32, product.shape, 0)
        column = lax.broadcasted_iota(jnp.int32, product.shape, 1)
        on_diagonal = jnp.where(row == column, product, 0.0)
        squares = squares + jnp.sum(jnp.sum(on_diagonal, 1, keepdims=True), 0, keepdims=True)
        gram[rows, :] = product
    scale = lax.rsqrt(squares + EPS_NORM)
    gram[...] = gram[...] * (scale * scale)

    low = gram[...].astype(BF16)
    for rows in steps:
        first[rows, :] = NS_B * gram[rows, :] + NS_C * dot(low[rows.start : rows.start + 256], low, plain)
    first_low = first[...].astype(BF16)
    for rows in steps:
        product = dot(low[rows.start : rows.start + 256], first_low, plain)
        half[rows, :] = NS_A * gram[rows, :] + product
    half_low = half[...].astype(BF16)
    for rows in steps:
        product = dot(half_low[rows.start : rows.start + 256], first_low, plain)
        gram[rows, :] = NS_A * half[rows, :] + product

    height = mine.shape[0]
    picked = -(-2 * height // 16) * 16
    row = lax.broadcasted_iota(jnp.int32, (picked, channels), 0)
    column = lax.broadcasted_iota(jnp.int32, (picked, channels), 1)
    wanted = jnp.where(row < height, scalars[0] + row, scalars[1] + row - height)
    chosen = (column == wanted) & (row < 2 * height)
    pick = jnp.where(chosen, 1.0, 0.0).astype(BF16)

    def halves(matrix):
        top = matrix.astype(BF16)
        return top, (matrix - top.astype(F32)).astype(BF16)

    def rows_of(matrix):
        top, rest = halves(matrix)
        return dot(pick, top, plain) + dot(pick, rest, plain)

    second_gram = gram[...]
    gram_rows = rows_of(second_gram)
    second = NS_B * gram_rows
    second = second + NS_C * dot(gram_rows.astype(BF16), second_gram.astype(BF16), plain)
    both = (
        jnp.where(chosen, NS_A * NS_A, 0.0)
        + NS_A * (rows_of(first[...]) + second)
        + dot(second.astype(BF16), first_low, plain)
    ) * scale
    top, rest = halves(both)
    across = ((1,), (1,))
    for start in range(0, value.shape[0], 256):
        step = min(256, value.shape[0] - start)
        piece = value[start : start + step]
        out = dot(top, piece, across) + dot(rest, piece, across)
        mine[:, start : start + step] = out[:height]
        theirs[:, start : start + step] = out[height : 2 * height].astype(BF16)


def shards(
    features,
    cotangent,
    depth_kernel,
    ln_gain,
    weight_up,
    bias_up,
    weight_down,
    layer_scale,
    tissue,
    lengths,
):
    tile_rows, columns, channels = features.shape
    tiles = lax.axis_size("tile")
    owners = lax.axis_size("own")
    lines = tiles // PLANE
    half_lines = lines // 2
    line_bits = [1 << i for i in range(lines.bit_length() - 1)]
    tile = lax.axis_index("tile")
    own = lax.axis_index("own")
    place, line = tile & (PLANE - 1), tile >> (PLANE.bit_length() - 1)
    share = tile_rows // owners
    offset = own * share
    tokens = share * columns
    live_rows = PATCH * lengths[tile]
    scalars = jnp.concatenate([jnp.stack([live_rows, offset]), tissue[:, 0]])
    scalars = scalars.astype(jnp.int32)
    strip = features.reshape(tile_rows * columns, channels)
    taps = depth_kernel.reshape(KERNEL * KERNEL, channels)
    gain, scale = ln_gain[None], layer_scale[None]
    frame = pltpu.VMEM((tile_rows + 2 * MARGIN, columns, channels), F32)
    wide = pltpu.VMEM((share, columns, channels), F32)
    rim = RIM * columns

    units = weight_up.shape[1] // PLANE
    both_weights = jnp.stack([weight_up, weight_down.T])
    pieces = []
    for s in range(PLANE):
        piece = lax.dynamic_slice_in_dim(both_weights, (place ^ s) * units, units, 2)
        pieces.append(swap(piece, "tile", s) if s else piece)
    piece = jnp.concatenate(in_order(pieces, place), 1)

    tail = lax.dynamic_slice_in_dim(strip, (live_rows - RIM) * columns, rim, 0)
    before, after = neighbours(strip[:rim], tail)
    piece, before, after = lax.optimization_barrier((piece, before, after))
    held = piece[None]
    for bit in line_bits[::-1]:
        held = jnp.concatenate([held, swap(held, "tile", PLANE * bit)], 0)
    up, down_t = call(
        weights_kernel,
        [jax.ShapeDtypeStruct((channels, units), BF16)] * 2,
        [],
        10 * 10**9,
        line[None], held,
    )
    bias = lax.dynamic_slice_in_dim(bias_up, place * units, units, 0)

    sent, centred, inverse = call(
        forward_kernel,
        [
            jax.ShapeDtypeStruct((2, tokens, channels), BF16),
            jax.ShapeDtypeStruct((tokens, channels), F32),
            jax.ShapeDtypeStruct((tokens, LANES), F32),
        ],
        [frame, wide],
        10**6,
        scalars, strip, cotangent.reshape(strip.shape), before, after, taps, gain, scale,
    )
    mine = jnp.concatenate([sent] + [swap(sent, "tile", s) for s in range(1, PLANE)], 1)
    both = jnp.concatenate([mine] + [swap(mine, "own", s) for s in range(1, owners)], 1)
    normed, grad_branch = both[0], both[1]

    plain, across, over_tokens = ((1,), (0,)), ((1,), (1,)), ((0,), (0,))
    hidden = dot(normed, up, plain) + bias
    cdf = 0.5 * (1.0 + lax.erf(hidden * INV_ROOT_TWO))
    act = (hidden * cdf).astype(BF16)
    slope = cdf + hidden * jnp.exp(-0.5 * hidden * hidden) * INV_ROOT_TAU
    grad_hidden = (dot(grad_branch, down_t, plain) * slope).astype(BF16)

    parts = jnp.concatenate(
        [dot(grad_hidden, normed, over_tokens), dot(act, grad_branch, over_tokens)], 0
    ).astype(BF16)
    parts, grad_hidden, act = lax.optimization_barrier((parts, grad_hidden, act))
    kept = 2 * units // lines
    reduced = parts.reshape(lines, kept, channels)

    def split(blocks, bit):
        blocks = blocks.reshape(-1, 2, kept, channels)
        which = jnp.where((line & bit) != 0, 1, 0)
        mine = lax.dynamic_slice_in_dim(blocks, which, 1, 1)
        other = lax.dynamic_slice_in_dim(blocks, 1 - which, 1, 1)
        return mine[:, 0].astype(F32), other[:, 0].astype(BF16)

    for bit in line_bits[:-1]:
        reduced, other = split(reduced, bit)
        reduced = reduced + swap(other, "tile", PLANE * bit).astype(F32)
    reduced, other = split(reduced, line_bits[-1])
    arrived = swap(other, "tile", PLANE * line_bits[-1])

    partial = jnp.stack([dot(grad_hidden, up, across), dot(act, down_t, across)])
    partial = partial.reshape(2, owners, PLANE, tokens, channels)
    total = partial[:, 0]
    for s in range(1, owners):
        total = total + swap(partial[:, s].astype(BF16), "own", s).astype(F32)
    total = total.astype(BF16)
    moved = [swap(total[:, s], "tile", s) for s in range(1, PLANE)]
    grad_mixed, block_out = call(
        middle_kernel,
        [jax.ShapeDtypeStruct((tokens, channels), BF16)] * 2,
        [],
        10**6,
        scalars, strip, total[:, 0], *moved, centred, inverse, gain, scale,
    )

    arrived, grad_mixed = lax.optimization_barrier((arrived, grad_mixed))
    grad_t = (reduced + arrived.astype(F32)).astype(BF16)[0]
    group = PLANE * half_lines
    bits = [1 << i for i in range(group.bit_length() - 1)]
    third = kept // 3
    thirds = []
    for turn in range(3):
        held = grad_t[turn * third : (turn + 1) * third][None]
        order = bits[turn:] + bits[:turn]
        for bit in order[:-1]:
            held = jnp.concatenate([held, swap(held, "tile", bit)], 0)
        thirds += [held, swap(held, "tile", order[-1])]

    halves = [grad_mixed] + [swap(grad_mixed, "own", s) for s in range(1, owners)]
    stacked = jnp.stack(halves)
    head = lax.dynamic_slice_in_dim(stacked, own, 1, 0)[0, :rim]
    last = live_rows - RIM
    tail = lax.dynamic_slice(
        stacked, ((last >> (share.bit_length() - 1)) ^ own, (last & (share - 1)) * columns, 0), (1, rim, channels)
    )[0]
    before, after = neighbours(head, tail)
    (grad_features,) = call(
        backward_kernel,
        [jax.ShapeDtypeStruct((tokens, channels), BF16)],
        [frame, wide],
        10**6,
        scalars, cotangent.reshape(strip.shape), before, after, taps, *halves,
    )

    height = channels // tiles
    other = tile ^ (PLANE * half_lines)
    square = pltpu.VMEM((channels, channels), F32)
    thirds, grad_features = lax.optimization_barrier((thirds, grad_features))
    if third % 16:
        entries = [(e, turn) for turn in range(3) for e in range(group)]
        slots = [
            hidden_block((tile & (group - 1)) ^ member_bits(e, turn, group), group) * 3 + turn
            for e, turn in entries
        ]
        ordered = jnp.zeros((3 * group, third, channels), BF16)
        ordered = ordered.at[jnp.stack(slots)].set(jnp.concatenate(thirds, 0))
        thirds = [ordered.reshape(-1, channels)]
    mine, theirs = call(
        ortho_kernel,
        [
            jax.ShapeDtypeStruct((height, weight_up.shape[1]), F32),
            jax.ShapeDtypeStruct((height, weight_up.shape[1]), BF16),
        ],
        [pltpu.VMEM((weight_up.shape[1], channels), BF16), square, square, square],
        10 * 10**9,
        jnp.stack([tile * height, other * height, tile & (group - 1)]), *thirds,
    )
    theirs = swap(theirs, "tile", PLANE * half_lines)
    theirs = theirs.astype(F32)
    expands = line < half_lines
    muon_up = jnp.where(expands, mine, theirs)
    muon_down = jnp.where(expands, theirs, mine).T
    shape = (share, columns, channels)
    return (block_out.reshape(shape), grad_features.reshape(shape), muon_up, muon_down)


def solution(mesh):
    in_specs = (
        P("tile", None, None),
        P("tile", None, None),
        P(),
        P(),
        P("tile", "own"),
        P("own"),
        P("own", "tile"),
        P(),
        P("tile", None),
        P(),
    )
    out_specs = (
        P(("tile", "own"), None, None),
        P(("tile", "own"), None, None),
        P("tile", "own"),
        P("own", "tile"),
    )
    return jax.shard_map(shards, mesh=mesh, in_specs=in_specs, out_specs=out_specs, check_vma=False)
```

```python
import functools

import jax
import jax.numpy as jnp
from jax import lax
from jax.experimental import pallas as pl
from jax.experimental.pallas import tpu as pltpu
from jax.sharding import PartitionSpec as P

KERNEL = 7
PATCH = 8
COLS = 8
MARGIN = KERNEL // 2
RIM = MARGIN + 1
PLANE = 4
LANES = 128
CHUNK = 8

INV_ROOT_TWO = 0.7071067811865476
INV_ROOT_TAU = 0.3989422804014327
NS_A = 3.4445
NS_B = -4.775
NS_C = 2.0315
EPS_NORM = 1e-06
F32 = jnp.float32
BF16 = jnp.bfloat16


def swap(value, axis, bit):
    return lax.ppermute(value, axis, [(i, i ^ bit) for i in range(lax.axis_size(axis))])


def neighbours(first, last):
    devices = lax.axis_size("tile")
    up = [(i, i + 1) for i in range(devices - 1)]
    down = [(i + 1, i) for i in range(devices - 1)]
    return lax.ppermute(last, "tile", up), lax.ppermute(first, "tile", down)


def in_order(blocks, index):
    bit = 1
    while bit < len(blocks):
        odd = (index & bit) != 0
        blocks = [jnp.where(odd, blocks[s ^ bit], blocks[s]) for s in range(len(blocks))]
        bit *= 2
    return blocks


def call(kernel, out_shape, scratch, flops, *operands, scalars=1):
    smem = pl.BlockSpec(memory_space=pltpu.SMEM)
    vmem = pl.BlockSpec(memory_space=pltpu.VMEM)
    return pl.pallas_call(
        kernel,
        out_shape=out_shape,
        in_specs=[smem] * scalars + [vmem] * (len(operands) - scalars),
        out_specs=[vmem] * len(out_shape),
        scratch_shapes=scratch,
        compiler_params=pltpu.CompilerParams(vmem_limit_bytes=40 * 2**20),
        cost_estimate=pl.CostEstimate(flops=flops, bytes_accessed=2**20, transcendentals=0),
    )(*operands)


def convolve(framed, kernel_ref, offset, out_ref, flipped):
    share, columns, channels = out_ref.shape
    chunk = min(CHUNK, share)
    lane_steps = channels // LANES
    column = lax.broadcasted_iota(jnp.int32, (chunk + 2 * MARGIN, columns, LANES), 1)

    def step(index, carry):
        lanes = pl.ds(pl.multiple_of((index % lane_steps) * LANES, LANES), LANES)
        first = (index // lane_steps) * chunk
        rows = framed[pl.ds(offset + first, chunk + 2 * MARGIN), :, lanes]
        total = jnp.zeros((chunk, columns, LANES), F32)
        for col_tap in range(KERNEL):
            reach = col_tap - MARGIN
            moved = rows
            if reach:
                moved = pltpu.roll(rows, (-reach) % columns, 1)
                inside = (column + reach >= 0) & (column + reach < columns)
                moved = jnp.where(inside, moved, 0.0)
            for row_tap in range(KERNEL):
                tap = row_tap * KERNEL + col_tap
                tap = KERNEL * KERNEL - 1 - tap if flipped else tap
                weight = kernel_ref[pl.ds(tap, 1), lanes][None]
                total = total + weight * moved[row_tap : row_tap + chunk]
        out_ref[pl.ds(first, chunk), :, lanes] = total
        return carry

    lax.fori_loop(0, lane_steps * (share // chunk), step, 0)


def place_strip(framed, pieces, before_ref, after_ref, live_rows):
    columns, channels = framed.shape[1:]

    def rows_of(ref):
        value = ref[...].astype(F32)
        return value.reshape(value.shape[0] // columns, columns, channels)

    for start, ref in pieces:
        rows = rows_of(ref)
        framed[pl.ds(start + MARGIN, rows.shape[0])] = rows
    framed[pl.ds(framed.shape[0] - MARGIN, MARGIN)] = jnp.zeros((MARGIN, columns, channels), F32)
    framed[pl.ds(0, MARGIN)] = rows_of(before_ref)[RIM - MARGIN :]
    framed[pl.ds(live_rows + MARGIN, MARGIN)] = rows_of(after_ref)[:MARGIN]


def kept_rows(scalars, tokens, patches):
    row = scalars[1] + lax.broadcasted_iota(jnp.int32, (tokens, 1), 0) // COLS
    keep = jnp.zeros((tokens, 1), F32)
    for patch in range(patches):
        keep = jnp.where(row // PATCH == patch, scalars[2 + patch].astype(F32), keep)
    live = row < scalars[0]
    return live, jnp.where(live, keep, 0.0)


def forward_kernel(
    scalars,
    strip,
    cotangent,
    before,
    after,
    taps,
    gain,
    layer_scale,
    sent,
    centred_out,
    inverse,
    framed,
    mixed,
):
    place_strip(framed, [(0, strip)], before, after, scalars[0])
    convolve(framed, taps, scalars[1], mixed, False)
    tokens, channels = centred_out.shape
    value = mixed[...].reshape(tokens, channels)
    shifted = value - jnp.sum(value, 1, keepdims=True) / channels
    variance = jnp.sum(shifted * shifted, 1, keepdims=True) / channels
    inv_std = lax.rsqrt(variance + 1e-06)
    centred = shifted * inv_std
    centred_out[...] = centred
    inverse[...] = jnp.broadcast_to(inv_std, inverse.shape)
    sent[0] = (centred * gain[...]).astype(BF16)
    _, keep = kept_rows(scalars, tokens, strip.shape[0] // (COLS * PATCH))
    start = pl.multiple_of(scalars[1] * COLS, 16)
    grad_out = cotangent[pl.ds(start, tokens), :].astype(F32)
    sent[1] = (keep * layer_scale[...] * grad_out).astype(BF16)


def middle_kernel(
    scalars, strip, total, one, two, three, centred, inverse, gain, layer_scale, grad_mixed, block_out
):
    tokens, channels = grad_mixed.shape
    start = pl.multiple_of(scalars[1] * COLS, 16)
    live, keep = kept_rows(scalars, tokens, strip.shape[0] // (COLS * PATCH))

    def summed(which):
        value = total[which].astype(F32)
        for ref in (one, two, three):
            value = value + ref[which].astype(F32)
        return value

    inputs = strip[pl.ds(start, tokens), :].astype(F32)
    block = inputs + keep * layer_scale[...] * summed(1)
    block_out[...] = jnp.where(live, block, 0.0).astype(BF16)
    scaled_grad = summed(0) * gain[...]
    first_mean = jnp.sum(scaled_grad, 1, keepdims=True) / channels
    second_mean = jnp.sum(scaled_grad * centred[...], 1, keepdims=True) / channels
    value = inverse[:, :1] * (scaled_grad - first_mean - centred[...] * second_mean)
    grad_mixed[...] = jnp.where(live, value, 0.0).astype(BF16)


def join_kernel(*refs):
    *blocks, out = refs
    start = 0
    for ref in blocks:
        out[:, start : start + ref.shape[1], :] = ref[...]
        start += ref.shape[1]


def double_kernel(*refs):
    count = len(refs) // 3
    for held, came, out in zip(refs[:count], refs[count : 2 * count], refs[2 * count :]):
        out[: held.shape[0]] = held[...]
        out[held.shape[0] :] = came[...]


def piece_kernel(scalars, *refs):
    *blocks, out = refs
    rows = blocks[0].shape[1]
    for s, block in enumerate(blocks):
        start = pl.multiple_of((scalars[0] ^ s) * rows, rows)
        out[:, pl.ds(start, rows), :] = block[...]


def weights_kernel(scalars, early, late, up, down_t):
    lines, rows = 2 * early.shape[0], early.shape[2]
    bits = lines.bit_length() - 1
    for e in range(lines):
        apart = sum(lines >> (i + 1) for i in range(bits) if e >> i & 1)
        start = pl.multiple_of((scalars[0] ^ apart) * rows, rows)
        later, entry = divmod(e, lines // 2)
        piece = (early, late)[later]
        up[pl.ds(start, rows), :] = piece[entry, 0]
        down_t[pl.ds(start, rows), :] = piece[entry, 1]


def mlp_kernel(scalars, up, down_t, bias, *refs, owners):
    tokens_of = refs[:owners]
    kept, sent, act_out, grad_out, parts = refs[owners:]
    lines = 2 * kept.shape[0]
    plain, over_tokens = ((1,), (0,)), ((0,), (0,))
    count = tokens_of[0].shape[1]
    step = min(256, count)
    for index, ref in enumerate(tokens_of):
        for start in range(0, count, step):
            hidden = dot(ref[0, start : start + step, :], up[...], plain) + bias[...]
            cdf = 0.5 * (1.0 + lax.erf(hidden * INV_ROOT_TWO))
            slope = cdf + hidden * jnp.exp(-0.5 * hidden * hidden) * INV_ROOT_TAU
            grad_act = dot(ref[1, start : start + step, :], down_t[...], plain)
            rows_out = pl.ds(index * count + start, step)
            act_out[rows_out, :] = (hidden * cdf).astype(BF16)
            grad_out[rows_out, :] = (grad_act * slope).astype(BF16)

    units = act_out.shape[1]
    for half, (hidden_side, which) in enumerate(((grad_out, 0), (act_out, 1))):
        total = jnp.zeros((units, parts.shape[1]), F32)
        for index, ref in enumerate(tokens_of):
            rows_in = slice(index * count, (index + 1) * count)
            total = total + dot(hidden_side[rows_in, :], ref[which], over_tokens)
        parts[half * units : (half + 1) * units, :] = total
    width = kept.shape[1]
    for q in range(lines):
        block = parts[q * width : (q + 1) * width, :].astype(BF16)
        same = scalars[0] == q % 2

        @pl.when(same)
        def _():
            kept[q // 2] = block

        @pl.when(jnp.logical_not(same))
        def _():
            sent[q // 2] = block


def partial_kernel(act, grad_hidden, up, down_t, mine, *others):
    across = ((1,), (1,))
    count = mine.shape[1]
    step = min(256, count)
    for index, ref in enumerate((mine,) + others):
        for start in range(0, count, step):
            rows_in = slice(index * count + start, index * count + start + step)
            rows_out = slice(start, start + step)
            ref[0, rows_out, :] = dot(grad_hidden[rows_in, :], up[...], across).astype(ref.dtype)
            ref[1, rows_out, :] = dot(act[rows_in, :], down_t[...], across).astype(ref.dtype)


def add_kernel(mine, *refs):
    others, outs = refs[:-PLANE], refs[-PLANE:]
    tokens = outs[0].shape[1]
    for strip, out in enumerate(outs):
        rows_in = slice(strip * tokens, (strip + 1) * tokens)
        total = mine[:, rows_in, :]
        for other in others:
            total = total + other[:, rows_in, :].astype(F32)
        out[...] = total.astype(BF16)


def backward_kernel(scalars, cotangent, before, after, taps, *rest):
    *pieces, grad_features, framed, spread = rest
    tokens = grad_features.shape[0]
    share = spread.shape[0]
    own = scalars[1] // share
    placed = [((own ^ s) * share, piece) for s, piece in enumerate(pieces)]
    place_strip(framed, placed, before, after, scalars[0])
    convolve(framed, taps, scalars[1], spread, True)
    start = pl.multiple_of(scalars[1] * COLS, 16)
    value = cotangent[pl.ds(start, tokens), :].astype(F32) + spread[...].reshape(grad_features.shape)
    row = scalars[1] + lax.broadcasted_iota(jnp.int32, (tokens, 1), 0) // COLS
    grad_features[...] = jnp.where(row < scalars[0], value, 0.0).astype(BF16)


def dot(left, right, contract, precision=None):
    return lax.dot_general(
        left, right, (contract, ((), ())), precision=precision, preferred_element_type=F32
    )


def member_bits(entry, turn, group):
    bits = group.bit_length() - 1
    return sum(1 << ((i + turn) % bits) for i in range(bits) if entry >> i & 1)


def hidden_block(member, group):
    return (member & (PLANE - 1)) * (group // PLANE) + (member >> (PLANE.bit_length() - 1))


def ortho_kernel(scalars, *refs):
    *gathered, mine, theirs, whole, gram, first, half = refs
    channels = whole.shape[1]
    if len(gathered) == 1:
        whole[...] = gathered[0][...]
    else:
        group, third, _ = gathered[0].shape
        group *= 2
        for turn in range(3):
            for e in range(group):
                block = hidden_block(scalars[2] ^ member_bits(e, turn, group), group)
                start = pl.multiple_of((block * 3 + turn) * third, third)
                later, entry = divmod(e, group // 2)
                whole[pl.ds(start, third), :] = gathered[2 * turn + later][entry]

    plain = ((1,), (0,))
    steps = [pl.ds(i, 256) for i in range(0, channels, 256)]
    value = whole[...]
    squares = jnp.zeros((1, 1), F32)
    for rows in steps:
        product = dot(value[:, rows.start : rows.start + 256], value, ((0,), (0,)))
        row = rows.start + lax.broadcasted_iota(jnp.int32, product.shape, 0)
        column = lax.broadcasted_iota(jnp.int32, product.shape, 1)
        on_diagonal = jnp.where(row == column, product, 0.0)
        squares = squares + jnp.sum(jnp.sum(on_diagonal, 1, keepdims=True), 0, keepdims=True)
        gram[rows, :] = product
    scale = lax.rsqrt(squares + EPS_NORM)
    gram[...] = gram[...] * (scale * scale)

    low = gram[...].astype(BF16)
    for rows in steps:
        first[rows, :] = NS_B * gram[rows, :] + NS_C * dot(low[rows.start : rows.start + 256], low, plain)
    first_low = first[...].astype(BF16)
    for rows in steps:
        product = dot(low[rows.start : rows.start + 256], first_low, plain)
        half[rows, :] = NS_A * gram[rows, :] + product
    half_low = half[...].astype(BF16)
    for rows in steps:
        product = dot(half_low[rows.start : rows.start + 256], first_low, plain)
        gram[rows, :] = NS_A * half[rows, :] + product

    height = mine.shape[0]
    picked = -(-2 * height // 16) * 16
    row = lax.broadcasted_iota(jnp.int32, (picked, channels), 0)
    column = lax.broadcasted_iota(jnp.int32, (picked, channels), 1)
    wanted = jnp.where(row < height, scalars[0] + row, scalars[1] + row - height)
    chosen = (column == wanted) & (row < 2 * height)
    pick = jnp.where(chosen, 1.0, 0.0).astype(BF16)

    def halves(matrix):
        top = matrix.astype(BF16)
        return top, (matrix - top.astype(F32)).astype(BF16)

    def rows_of(matrix):
        top, rest = halves(matrix)
        return dot(pick, top, plain) + dot(pick, rest, plain)

    second_gram = gram[...]
    gram_rows = rows_of(second_gram)
    second = NS_B * gram_rows
    second = second + NS_C * dot(gram_rows.astype(BF16), second_gram.astype(BF16), plain)
    both = (
        jnp.where(chosen, NS_A * NS_A, 0.0)
        + NS_A * (rows_of(first[...]) + second)
        + dot(second.astype(BF16), first_low, plain)
    ) * scale
    top, rest = halves(both)
    across = ((1,), (1,))
    for start in range(0, value.shape[0], 256):
        step = min(256, value.shape[0] - start)
        piece = value[start : start + step]
        out = dot(top, piece, across) + dot(rest, piece, across)
        mine[:, start : start + step] = out[:height]
        theirs[:, start : start + step] = out[height : 2 * height].astype(BF16)


def shards(
    features,
    cotangent,
    depth_kernel,
    ln_gain,
    weight_up,
    bias_up,
    weight_down,
    layer_scale,
    tissue,
    lengths,
):
    tile_rows, columns, channels = features.shape
    tiles = lax.axis_size("tile")
    owners = lax.axis_size("own")
    lines = tiles // PLANE
    half_lines = lines // 2
    line_bits = [1 << i for i in range(lines.bit_length() - 1)]
    tile = lax.axis_index("tile")
    own = lax.axis_index("own")
    place, line = tile & (PLANE - 1), tile >> (PLANE.bit_length() - 1)
    share = tile_rows // owners
    offset = own * share
    tokens = share * columns
    live_rows = PATCH * lengths[tile]
    scalars = jnp.concatenate([jnp.stack([live_rows, offset]), tissue[:, 0]])
    scalars = scalars.astype(jnp.int32)
    strip = features.reshape(tile_rows * columns, channels)
    taps = depth_kernel.reshape(KERNEL * KERNEL, channels)
    gain, scale = ln_gain[None], layer_scale[None]
    frame = pltpu.VMEM((tile_rows + 2 * MARGIN, columns, channels), F32)
    wide = pltpu.VMEM((share, columns, channels), F32)
    rim = RIM * columns

    height = channels // tiles
    units = weight_up.shape[1] // PLANE
    both_weights = jnp.stack([weight_up, weight_down.T])
    pieces = []
    for s in range(PLANE):
        piece = lax.dynamic_slice_in_dim(both_weights, (place ^ s) * units, units, 2)
        pieces.append(swap(piece, "tile", s) if s else piece)
    if height % 16:
        piece = jnp.concatenate(in_order(pieces, place), 1)
    else:
        (piece,) = call(
            piece_kernel,
            [jax.ShapeDtypeStruct((2, PLANE * height, units), BF16)],
            [],
            10**6,
            place[None], *pieces,
        )

    tail = lax.dynamic_slice_in_dim(strip, (live_rows - RIM) * columns, rim, 0)
    before, after = neighbours(strip[:rim], tail)
    piece, before, after = lax.optimization_barrier((piece, before, after))
    bias = lax.dynamic_slice_in_dim(bias_up, place * units, units, 0)

    sent, centred, inverse = call(
        forward_kernel,
        [
            jax.ShapeDtypeStruct((2, tokens, channels), BF16),
            jax.ShapeDtypeStruct((tokens, channels), F32),
            jax.ShapeDtypeStruct((tokens, LANES), F32),
        ],
        [frame, wide],
        10**6,
        scalars, strip, cotangent.reshape(strip.shape), before, after, taps, gain, scale,
    )
    held = piece[None]
    for bit in line_bits[:0:-1]:
        shape = jax.ShapeDtypeStruct((2 * held.shape[0],) + held.shape[1:], BF16)
        came = swap(held, "tile", PLANE * bit)
        (held,) = call(double_kernel, [shape], [], 10**6, held, came, scalars=0)
    late = swap(held, "tile", PLANE)
    (mine,) = call(
        join_kernel,
        [jax.ShapeDtypeStruct((2, PLANE * tokens, channels), BF16)],
        [],
        10**6,
        sent, *[swap(sent, "tile", s) for s in range(1, PLANE)],
        scalars=0,
    )
    shares = [mine] + [swap(mine, "own", s) for s in range(1, owners)]

    kept = 2 * units // lines
    total_tokens = owners * PLANE * tokens
    half_parts = jax.ShapeDtypeStruct((lines // 2, kept, channels), BF16)
    hidden_shape = jax.ShapeDtypeStruct((total_tokens, units), BF16)
    weight_shape = jax.ShapeDtypeStruct((channels, units), BF16)
    up, down_t = call(
        weights_kernel, [weight_shape, weight_shape], [], 13 * 10**9, line[None], held, late
    )
    reduced, other, act, grad_hidden = call(
        functools.partial(mlp_kernel, owners=owners),
        [half_parts, half_parts, hidden_shape, hidden_shape],
        [pltpu.VMEM((2 * units, channels), F32)],
        5 * 10**9,
        (line & 1)[None], up, down_t, bias[None], *shares,
    )

    def split(blocks, bit):
        blocks = blocks.reshape(-1, 2, kept, channels)
        which = jnp.where((line & bit) != 0, 1, 0)
        mine = lax.dynamic_slice_in_dim(blocks, which, 1, 1)
        other = lax.dynamic_slice_in_dim(blocks, 1 - which, 1, 1)
        return mine[:, 0], other[:, 0].astype(BF16)

    arrived = swap(other, "tile", PLANE)

    part_shape = (2, PLANE * tokens, channels)
    mine, *others = call(
        partial_kernel,
        [jax.ShapeDtypeStruct(part_shape, F32)]
        + [jax.ShapeDtypeStruct(part_shape, BF16)] * (owners - 1),
        [],
        10**9,
        act, grad_hidden, up, down_t,
        scalars=0,
    )
    others = [swap(value, "own", s + 1) for s, value in enumerate(others)]
    total, *moved = call(
        add_kernel,
        [jax.ShapeDtypeStruct((2, tokens, channels), BF16)] * PLANE,
        [],
        10**6,
        mine, *others,
        scalars=0,
    )
    moved = [swap(value, "tile", s + 1) for s, value in enumerate(moved)]
    arrived, moved[0] = lax.optimization_barrier((arrived, moved[0]))
    reduced = reduced.astype(F32) + arrived.astype(F32)
    for bit in line_bits[1:-1]:
        reduced, other = split(reduced, bit)
        reduced = reduced + swap(other, "tile", PLANE * bit).astype(F32)
    reduced, other = split(reduced, line_bits[-1])
    arrived = swap(other, "tile", PLANE * line_bits[-1])

    grad_mixed, block_out = call(
        middle_kernel,
        [jax.ShapeDtypeStruct((tokens, channels), BF16)] * 2,
        [],
        10**6,
        scalars, strip, total, *moved, centred, inverse, gain, scale,
    )

    arrived, grad_mixed = lax.optimization_barrier((arrived, grad_mixed))
    grad_t = (reduced + arrived.astype(F32)).astype(BF16)[0]
    group = PLANE * half_lines
    bits = [1 << i for i in range(group.bit_length() - 1)]
    third = kept // 3
    helds = [grad_t[turn * third : (turn + 1) * third][None] for turn in range(3)]
    orders = [bits[turn:] + bits[:turn] for turn in range(3)]
    for stage in range(len(bits)):
        came = [swap(held, "tile", order[stage]) for held, order in zip(helds, orders)]
        if stage + 1 < len(bits):
            shape = jax.ShapeDtypeStruct((2 << stage, third, channels), BF16)
            helds = call(double_kernel, [shape] * 3, [], 10**6, *helds, *came, scalars=0)
    thirds = [half for pair in zip(helds, came) for half in pair]

    halves = [grad_mixed] + [swap(grad_mixed, "own", s) for s in range(1, owners)]
    stacked = jnp.stack(halves)
    head = lax.dynamic_slice_in_dim(stacked, own, 1, 0)[0, :rim]
    last = live_rows - RIM
    tail = lax.dynamic_slice(
        stacked, ((last >> (share.bit_length() - 1)) ^ own, (last & (share - 1)) * columns, 0), (1, rim, channels)
    )[0]
    before, after = neighbours(head, tail)
    (grad_features,) = call(
        backward_kernel,
        [jax.ShapeDtypeStruct((tokens, channels), BF16)],
        [frame, wide],
        10**6,
        scalars, cotangent.reshape(strip.shape), before, after, taps, *halves,
    )

    other = tile ^ (PLANE * half_lines)
    square = pltpu.VMEM((channels, channels), F32)
    thirds, grad_features = lax.optimization_barrier((thirds, grad_features))
    if third % 16:
        entries = [(e, turn) for turn in range(3) for e in range(group)]
        slots = [
            hidden_block((tile & (group - 1)) ^ member_bits(e, turn, group), group) * 3 + turn
            for e, turn in entries
        ]
        ordered = jnp.zeros((3 * group, third, channels), BF16)
        ordered = ordered.at[jnp.stack(slots)].set(jnp.concatenate(thirds, 0))
        thirds = [ordered.reshape(-1, channels)]
    mine, theirs = call(
        ortho_kernel,
        [
            jax.ShapeDtypeStruct((height, weight_up.shape[1]), F32),
            jax.ShapeDtypeStruct((height, weight_up.shape[1]), BF16),
        ],
        [pltpu.VMEM((weight_up.shape[1], channels), BF16), square, square, square],
        10 * 10**9,
        jnp.stack([tile * height, other * height, tile & (group - 1)]), *thirds,
    )
    theirs = swap(theirs, "tile", PLANE * half_lines)
    theirs = theirs.astype(F32)
    expands = line < half_lines
    muon_up = jnp.where(expands, mine, theirs)
    muon_down = jnp.where(expands, theirs, mine).T
    shape = (share, columns, channels)
    return (block_out.reshape(shape), grad_features.reshape(shape), muon_up, muon_down)


def solution(mesh):
    in_specs = (
        P("tile", None, None),
        P("tile", None, None),
        P(),
        P(),
        P("tile", "own"),
        P("own"),
        P("own", "tile"),
        P(),
        P("tile", None),
        P(),
    )
    out_specs = (
        P(("tile", "own"), None, None),
        P(("tile", "own"), None, None),
        P("tile", "own"),
        P("own", "tile"),
    )
    return jax.shard_map(shards, mesh=mesh, in_specs=in_specs, out_specs=out_specs, check_vma=False)
```

```python
import functools

import jax
import jax.numpy as jnp
from jax import lax
from jax.experimental import pallas as pl
from jax.experimental.pallas import tpu as pltpu
from jax.sharding import PartitionSpec as P

KERNEL = 7
PATCH = 8
COLS = 8
MARGIN = KERNEL // 2
RIM = MARGIN + 1
PLANE = 4
LANES = 128
CHUNK = 8

INV_ROOT_TWO = 0.7071067811865476
INV_ROOT_TAU = 0.3989422804014327
NS_A = 3.4445
NS_B = -4.775
NS_C = 2.0315
EPS_NORM = 1e-06
F32 = jnp.float32
BF16 = jnp.bfloat16


def swap(value, axis, bit):
    return lax.ppermute(value, axis, [(i, i ^ bit) for i in range(lax.axis_size(axis))])


def neighbours(first, last):
    devices = lax.axis_size("tile")
    up = [(i, i + 1) for i in range(devices - 1)]
    down = [(i + 1, i) for i in range(devices - 1)]
    return lax.ppermute(last, "tile", up), lax.ppermute(first, "tile", down)


def in_order(blocks, index):
    bit = 1
    while bit < len(blocks):
        odd = (index & bit) != 0
        blocks = [jnp.where(odd, blocks[s ^ bit], blocks[s]) for s in range(len(blocks))]
        bit *= 2
    return blocks


def call(kernel, out_shape, scratch, flops, *operands, scalars=1):
    smem = pl.BlockSpec(memory_space=pltpu.SMEM)
    vmem = pl.BlockSpec(memory_space=pltpu.VMEM)
    return pl.pallas_call(
        kernel,
        out_shape=out_shape,
        in_specs=[smem] * scalars + [vmem] * (len(operands) - scalars),
        out_specs=[vmem] * len(out_shape),
        scratch_shapes=scratch,
        compiler_params=pltpu.CompilerParams(vmem_limit_bytes=40 * 2**20),
        cost_estimate=pl.CostEstimate(flops=flops, bytes_accessed=2**20, transcendentals=0),
    )(*operands)


def convolve(framed, kernel_ref, offset, out_ref, flipped):
    share, columns, channels = out_ref.shape
    chunk = min(CHUNK, share)
    lane_steps = channels // LANES
    column = lax.broadcasted_iota(jnp.int32, (chunk + 2 * MARGIN, columns, LANES), 1)

    def step(index, carry):
        lanes = pl.ds(pl.multiple_of((index % lane_steps) * LANES, LANES), LANES)
        first = (index // lane_steps) * chunk
        rows = framed[pl.ds(offset + first, chunk + 2 * MARGIN), :, lanes]
        total = jnp.zeros((chunk, columns, LANES), F32)
        for col_tap in range(KERNEL):
            reach = col_tap - MARGIN
            moved = rows
            if reach:
                moved = pltpu.roll(rows, (-reach) % columns, 1)
                inside = (column + reach >= 0) & (column + reach < columns)
                moved = jnp.where(inside, moved, 0.0)
            for row_tap in range(KERNEL):
                tap = row_tap * KERNEL + col_tap
                tap = KERNEL * KERNEL - 1 - tap if flipped else tap
                weight = kernel_ref[pl.ds(tap, 1), lanes][None]
                total = total + weight * moved[row_tap : row_tap + chunk]
        out_ref[pl.ds(first, chunk), :, lanes] = total
        return carry

    lax.fori_loop(0, lane_steps * (share // chunk), step, 0)


def place_strip(framed, pieces, before_ref, after_ref, live_rows):
    columns, channels = framed.shape[1:]

    def rows_of(ref):
        value = ref[...].astype(F32)
        return value.reshape(value.shape[0] // columns, columns, channels)

    for start, ref in pieces:
        rows = rows_of(ref)
        framed[pl.ds(start + MARGIN, rows.shape[0])] = rows
    framed[pl.ds(framed.shape[0] - MARGIN, MARGIN)] = jnp.zeros((MARGIN, columns, channels), F32)
    framed[pl.ds(0, MARGIN)] = rows_of(before_ref)[RIM - MARGIN :]
    framed[pl.ds(live_rows + MARGIN, MARGIN)] = rows_of(after_ref)[:MARGIN]


def live_rows(ids, lengths):
    return PATCH * lengths[ids[0]]


def kept_rows(ids, lengths, tissue, tokens):
    row = ids[1] + lax.broadcasted_iota(jnp.int32, (tokens, 1), 0) // COLS
    keep = jnp.zeros((tokens, 1), F32)
    for patch in range(tissue.shape[0]):
        keep = jnp.where(row // PATCH == patch, tissue[patch].astype(F32), keep)
    live = row < live_rows(ids, lengths)
    return live, jnp.where(live, keep, 0.0)


def rims_kernel(ids, lengths, *refs):
    *shares, head, tail = refs
    tokens = shares[0].shape[0]
    last = (live_rows(ids, lengths) - RIM) * COLS
    for s, share in enumerate(shares):

        @pl.when(ids[2] == s)
        def _():
            head[...] = share[: head.shape[0], :]

        @pl.when((last // tokens) ^ ids[2] == s)
        def _():
            start = pl.multiple_of(lax.rem(last, tokens), RIM * COLS)
            tail[...] = share[pl.ds(start, tail.shape[0]), :]


def forward_kernel(
    ids,
    lengths,
    tissue,
    strip,
    cotangent,
    before,
    after,
    taps,
    gain,
    layer_scale,
    sent,
    centred_out,
    inverse,
    framed,
    mixed,
):
    place_strip(framed, [(0, strip)], before, after, live_rows(ids, lengths))
    convolve(framed, taps, ids[1], mixed, False)
    tokens, channels = centred_out.shape
    value = mixed[...].reshape(tokens, channels)
    shifted = value - jnp.sum(value, 1, keepdims=True) / channels
    variance = jnp.sum(shifted * shifted, 1, keepdims=True) / channels
    inv_std = lax.rsqrt(variance + 1e-06)
    centred = shifted * inv_std
    centred_out[...] = centred
    inverse[...] = jnp.broadcast_to(inv_std, inverse.shape)
    sent[0] = (centred * gain[...]).astype(BF16)
    _, keep = kept_rows(ids, lengths, tissue, tokens)
    start = pl.multiple_of(ids[1] * COLS, 16)
    grad_out = cotangent[pl.ds(start, tokens), :].astype(F32)
    sent[1] = (keep * layer_scale[...] * grad_out).astype(BF16)


def middle_kernel(
    ids,
    lengths,
    tissue,
    strip,
    total,
    one,
    two,
    three,
    centred,
    inverse,
    gain,
    layer_scale,
    grad_mixed,
    block_out,
):
    tokens, channels = grad_mixed.shape
    start = pl.multiple_of(ids[1] * COLS, 16)
    live, keep = kept_rows(ids, lengths, tissue, tokens)

    def summed(which):
        value = total[which].astype(F32)
        for ref in (one, two, three):
            value = value + ref[which].astype(F32)
        return value

    inputs = strip[pl.ds(start, tokens), :].astype(F32)
    block = inputs + keep * layer_scale[...] * summed(1)
    block_out[...] = jnp.where(live, block, 0.0).astype(BF16)
    scaled_grad = summed(0) * gain[...]
    first_mean = jnp.sum(scaled_grad, 1, keepdims=True) / channels
    second_mean = jnp.sum(scaled_grad * centred[...], 1, keepdims=True) / channels
    value = inverse[:, :1] * (scaled_grad - first_mean - centred[...] * second_mean)
    grad_mixed[...] = jnp.where(live, value, 0.0).astype(BF16)


def join_kernel(*refs):
    *blocks, out = refs
    start = 0
    for ref in blocks:
        out[:, start : start + ref.shape[1], :] = ref[...]
        start += ref.shape[1]


def double_kernel(*refs):
    count = len(refs) // 3
    for held, came, out in zip(refs[:count], refs[count : 2 * count], refs[2 * count :]):
        out[: held.shape[0]] = held[...]
        out[held.shape[0] :] = came[...]


def piece_kernel(scalars, *refs):
    *blocks, out = refs
    rows = blocks[0].shape[1]
    for s, block in enumerate(blocks):
        start = pl.multiple_of((scalars[0] ^ s) * rows, rows)
        out[:, pl.ds(start, rows), :] = block[...]


def weights_kernel(scalars, early, late, up, down_t):
    lines, rows = 2 * early.shape[0], early.shape[2]
    bits = lines.bit_length() - 1
    for e in range(lines):
        apart = sum(lines >> (i + 1) for i in range(bits) if e >> i & 1)
        start = pl.multiple_of((scalars[0] ^ apart) * rows, rows)
        later, entry = divmod(e, lines // 2)
        piece = (early, late)[later]
        up[pl.ds(start, rows), :] = piece[entry, 0]
        down_t[pl.ds(start, rows), :] = piece[entry, 1]


def mlp_kernel(scalars, up, down_t, bias, *refs, owners):
    tokens_of = refs[:owners]
    kept, sent, act_out, grad_out, parts = refs[owners:]
    lines = 2 * kept.shape[0]
    plain, over_tokens = ((1,), (0,)), ((0,), (0,))
    count = tokens_of[0].shape[1]
    step = min(256, count)
    for index, ref in enumerate(tokens_of):
        for start in range(0, count, step):
            hidden = dot(ref[0, start : start + step, :], up[...], plain) + bias[...]
            cdf = 0.5 * (1.0 + lax.erf(hidden * INV_ROOT_TWO))
            slope = cdf + hidden * jnp.exp(-0.5 * hidden * hidden) * INV_ROOT_TAU
            grad_act = dot(ref[1, start : start + step, :], down_t[...], plain)
            rows_out = pl.ds(index * count + start, step)
            act_out[rows_out, :] = (hidden * cdf).astype(BF16)
            grad_out[rows_out, :] = (grad_act * slope).astype(BF16)

    units = act_out.shape[1]
    for half, (hidden_side, which) in enumerate(((grad_out, 0), (act_out, 1))):
        total = jnp.zeros((units, parts.shape[1]), F32)
        for index, ref in enumerate(tokens_of):
            rows_in = slice(index * count, (index + 1) * count)
            total = total + dot(hidden_side[rows_in, :], ref[which], over_tokens)
        parts[half * units : (half + 1) * units, :] = total
    width = kept.shape[1]
    for q in range(lines):
        block = parts[q * width : (q + 1) * width, :].astype(BF16)
        same = scalars[0] == q % 2

        @pl.when(same)
        def _():
            kept[q // 2] = block

        @pl.when(jnp.logical_not(same))
        def _():
            sent[q // 2] = block


def partial_kernel(act, grad_hidden, up, down_t, mine, *others):
    across = ((1,), (1,))
    count = mine.shape[1]
    step = min(256, count)
    for index, ref in enumerate((mine,) + others):
        for start in range(0, count, step):
            rows_in = slice(index * count + start, index * count + start + step)
            rows_out = slice(start, start + step)
            ref[0, rows_out, :] = dot(grad_hidden[rows_in, :], up[...], across).astype(ref.dtype)
            ref[1, rows_out, :] = dot(act[rows_in, :], down_t[...], across).astype(ref.dtype)


def add_kernel(mine, *refs):
    others, outs = refs[:-PLANE], refs[-PLANE:]
    tokens = outs[0].shape[1]
    for strip, out in enumerate(outs):
        rows_in = slice(strip * tokens, (strip + 1) * tokens)
        total = mine[:, rows_in, :]
        for other in others:
            total = total + other[:, rows_in, :].astype(F32)
        out[...] = total.astype(BF16)


def backward_kernel(ids, lengths, cotangent, before, after, taps, *rest):
    *pieces, grad_features, framed, spread = rest
    tokens = grad_features.shape[0]
    share = spread.shape[0]
    placed = [((ids[2] ^ s) * share, piece) for s, piece in enumerate(pieces)]
    place_strip(framed, placed, before, after, live_rows(ids, lengths))
    convolve(framed, taps, ids[1], spread, True)
    start = pl.multiple_of(ids[1] * COLS, 16)
    value = cotangent[pl.ds(start, tokens), :].astype(F32) + spread[...].reshape(grad_features.shape)
    row = ids[1] + lax.broadcasted_iota(jnp.int32, (tokens, 1), 0) // COLS
    grad_features[...] = jnp.where(row < live_rows(ids, lengths), value, 0.0).astype(BF16)


def dot(left, right, contract, precision=None):
    return lax.dot_general(
        left, right, (contract, ((), ())), precision=precision, preferred_element_type=F32
    )


def member_bits(entry, turn, group):
    bits = group.bit_length() - 1
    return sum(1 << ((i + turn) % bits) for i in range(bits) if entry >> i & 1)


def hidden_block(member, group):
    return (member & (PLANE - 1)) * (group // PLANE) + (member >> (PLANE.bit_length() - 1))


def ortho_kernel(scalars, *refs):
    *gathered, mine, theirs, whole, gram, first, half = refs
    channels = whole.shape[1]
    if len(gathered) == 1:
        whole[...] = gathered[0][...]
    else:
        group, third, _ = gathered[0].shape
        group *= 2
        for turn in range(3):
            for e in range(group):
                block = hidden_block(scalars[2] ^ member_bits(e, turn, group), group)
                start = pl.multiple_of((block * 3 + turn) * third, third)
                later, entry = divmod(e, group // 2)
                whole[pl.ds(start, third), :] = gathered[2 * turn + later][entry]

    plain = ((1,), (0,))
    steps = [pl.ds(i, 256) for i in range(0, channels, 256)]
    value = whole[...]
    squares = jnp.zeros((1, 1), F32)
    for rows in steps:
        product = dot(value[:, rows.start : rows.start + 256], value, ((0,), (0,)))
        row = rows.start + lax.broadcasted_iota(jnp.int32, product.shape, 0)
        column = lax.broadcasted_iota(jnp.int32, product.shape, 1)
        on_diagonal = jnp.where(row == column, product, 0.0)
        squares = squares + jnp.sum(jnp.sum(on_diagonal, 1, keepdims=True), 0, keepdims=True)
        gram[rows, :] = product
    scale = lax.rsqrt(squares + EPS_NORM)
    gram[...] = gram[...] * (scale * scale)

    low = gram[...].astype(BF16)
    for rows in steps:
        first[rows, :] = NS_B * gram[rows, :] + NS_C * dot(low[rows.start : rows.start + 256], low, plain)
    first_low = first[...].astype(BF16)
    for rows in steps:
        product = dot(low[rows.start : rows.start + 256], first_low, plain)
        half[rows, :] = NS_A * gram[rows, :] + product
    half_low = half[...].astype(BF16)
    for rows in steps:
        product = dot(half_low[rows.start : rows.start + 256], first_low, plain)
        gram[rows, :] = NS_A * half[rows, :] + product

    height = mine.shape[0]
    picked = -(-2 * height // 16) * 16
    row = lax.broadcasted_iota(jnp.int32, (picked, channels), 0)
    column = lax.broadcasted_iota(jnp.int32, (picked, channels), 1)
    wanted = jnp.where(row < height, scalars[0] + row, scalars[1] + row - height)
    chosen = (column == wanted) & (row < 2 * height)

    def halves(matrix):
        top = matrix.astype(BF16)
        return top, (matrix - top.astype(F32)).astype(BF16)

    def rows_of(ref):
        if height % 8 == 0:
            starts = [pl.multiple_of(scalars[i], 8) for i in range(2)]
            return jnp.concatenate([ref[pl.ds(start, height), :] for start in starts], 0)
        pick = jnp.where(chosen, 1.0, 0.0).astype(BF16)
        top, rest = halves(ref[...])
        return dot(pick, top, plain) + dot(pick, rest, plain)

    gram_rows = rows_of(gram)
    second = NS_B * gram_rows
    second = second + NS_C * dot(gram_rows.astype(BF16), gram[...].astype(BF16), plain)
    both = (
        jnp.where(chosen, NS_A * NS_A, 0.0)
        + NS_A * (rows_of(first) + second)
        + dot(second.astype(BF16), first_low, plain)
    ) * scale
    both = jnp.concatenate(halves(both), 0)
    across = ((1,), (1,))
    for start in range(0, value.shape[0], 256):
        step = min(256, value.shape[0] - start)
        out = dot(both, value[start : start + step], across)
        out = out[:picked] + out[picked:]
        mine[:, start : start + step] = out[:height]
        theirs[:, start : start + step] = out[height : 2 * height].astype(BF16)


def shards(
    features,
    cotangent,
    depth_kernel,
    ln_gain,
    weight_up,
    bias_up,
    weight_down,
    layer_scale,
    tissue,
    lengths,
):
    tile_rows, columns, channels = features.shape
    tiles = lax.axis_size("tile")
    owners = lax.axis_size("own")
    lines = tiles // PLANE
    half_lines = lines // 2
    line_bits = [1 << i for i in range(lines.bit_length() - 1)]
    tile = lax.axis_index("tile")
    own = lax.axis_index("own")
    place, line = tile & (PLANE - 1), tile >> (PLANE.bit_length() - 1)
    share = tile_rows // owners
    offset = own * share
    tokens = share * columns
    ids = jnp.stack([tile, offset, own]).astype(jnp.int32)
    flags = tissue.reshape(-1)
    strip = features.reshape(tile_rows * columns, channels)
    taps = depth_kernel.reshape(KERNEL * KERNEL, channels)
    gain, scale = ln_gain[None], layer_scale[None]
    frame = pltpu.VMEM((tile_rows + 2 * MARGIN, columns, channels), F32)
    wide = pltpu.VMEM((share, columns, channels), F32)
    rims = [jax.ShapeDtypeStruct((RIM * columns, channels), BF16)] * 2

    height = channels // tiles
    units = weight_up.shape[1] // PLANE
    both_weights = jnp.stack([weight_up, weight_down.T])
    pieces = []
    for s in range(PLANE):
        piece = lax.dynamic_slice_in_dim(both_weights, (place ^ s) * units, units, 2)
        pieces.append(swap(piece, "tile", s) if s else piece)
    if height % 16:
        piece = jnp.concatenate(in_order(pieces, place), 1)
    else:
        (piece,) = call(
            piece_kernel,
            [jax.ShapeDtypeStruct((2, PLANE * height, units), BF16)],
            [],
            10**6,
            place[None], *pieces,
        )

    place_ids = jnp.stack([tile, 0 * tile, 0 * tile]).astype(jnp.int32)
    head, tail = call(rims_kernel, rims, [], 10**6, place_ids, lengths, strip, scalars=2)
    before, after = neighbours(head, tail)
    piece, before, after = lax.optimization_barrier((piece, before, after))
    bias = lax.dynamic_slice_in_dim(bias_up, place * units, units, 0)

    sent, centred, inverse = call(
        forward_kernel,
        [
            jax.ShapeDtypeStruct((2, tokens, channels), BF16),
            jax.ShapeDtypeStruct((tokens, channels), F32),
            jax.ShapeDtypeStruct((tokens, LANES), F32),
        ],
        [frame, wide],
        10**6,
        ids, lengths, flags, strip, cotangent.reshape(strip.shape),
        before, after, taps, gain, scale,
        scalars=3,
    )
    held = piece[None]
    for bit in line_bits[:0:-1]:
        shape = jax.ShapeDtypeStruct((2 * held.shape[0],) + held.shape[1:], BF16)
        came = swap(held, "tile", PLANE * bit)
        (held,) = call(double_kernel, [shape], [], 10**6, held, came, scalars=0)
    late = swap(held, "tile", PLANE)
    (mine,) = call(
        join_kernel,
        [jax.ShapeDtypeStruct((2, PLANE * tokens, channels), BF16)],
        [],
        10**6,
        sent, *[swap(sent, "tile", s) for s in range(1, PLANE)],
        scalars=0,
    )
    shares = [mine] + [swap(mine, "own", s) for s in range(1, owners)]

    kept = 2 * units // lines
    total_tokens = owners * PLANE * tokens
    half_parts = jax.ShapeDtypeStruct((lines // 2, kept, channels), BF16)
    hidden_shape = jax.ShapeDtypeStruct((total_tokens, units), BF16)
    weight_shape = jax.ShapeDtypeStruct((channels, units), BF16)
    up, down_t = call(
        weights_kernel, [weight_shape, weight_shape], [], 13 * 10**9, line[None], held, late
    )
    reduced, other, act, grad_hidden = call(
        functools.partial(mlp_kernel, owners=owners),
        [half_parts, half_parts, hidden_shape, hidden_shape],
        [pltpu.VMEM((2 * units, channels), F32)],
        5 * 10**9,
        (line & 1)[None], up, down_t, bias[None], *shares,
    )

    def split(blocks, bit):
        blocks = blocks.reshape(-1, 2, kept, channels)
        which = jnp.where((line & bit) != 0, 1, 0)
        mine = lax.dynamic_slice_in_dim(blocks, which, 1, 1)
        other = lax.dynamic_slice_in_dim(blocks, 1 - which, 1, 1)
        return mine[:, 0], other[:, 0].astype(BF16)

    arrived = swap(other, "tile", PLANE)

    part_shape = (2, PLANE * tokens, channels)
    mine, *others = call(
        partial_kernel,
        [jax.ShapeDtypeStruct(part_shape, F32)]
        + [jax.ShapeDtypeStruct(part_shape, BF16)] * (owners - 1),
        [],
        10**9,
        act, grad_hidden, up, down_t,
        scalars=0,
    )
    others = [swap(value, "own", s + 1) for s, value in enumerate(others)]
    total, *moved = call(
        add_kernel,
        [jax.ShapeDtypeStruct((2, tokens, channels), BF16)] * PLANE,
        [],
        10**6,
        mine, *others,
        scalars=0,
    )
    moved = [swap(value, "tile", s + 1) for s, value in enumerate(moved)]
    arrived, moved[0] = lax.optimization_barrier((arrived, moved[0]))
    reduced = reduced.astype(F32) + arrived.astype(F32)
    for bit in line_bits[1:-1]:
        reduced, other = split(reduced, bit)
        reduced = reduced + swap(other, "tile", PLANE * bit).astype(F32)
    reduced, other = split(reduced, line_bits[-1])
    arrived = swap(other, "tile", PLANE * line_bits[-1])

    grad_mixed, block_out = call(
        middle_kernel,
        [jax.ShapeDtypeStruct((tokens, channels), BF16)] * 2,
        [],
        10**6,
        ids, lengths, flags, strip, total, *moved, centred, inverse, gain, scale,
        scalars=3,
    )

    halves = [grad_mixed] + [swap(grad_mixed, "own", s) for s in range(1, owners)]
    arrived, halves = lax.optimization_barrier((arrived, halves))
    head, tail = call(rims_kernel, rims, [], 10**6, ids, lengths, *halves, scalars=2)
    before, after = neighbours(head, tail)
    grad_t = (reduced + arrived.astype(F32)).astype(BF16)[0]
    group = PLANE * half_lines
    bits = [1 << i for i in range(group.bit_length() - 1)]
    third = kept // 3
    helds = [grad_t[turn * third : (turn + 1) * third][None] for turn in range(3)]
    orders = [bits[turn:] + bits[:turn] for turn in range(3)]
    for stage in range(len(bits)):
        came = [swap(held, "tile", order[stage]) for held, order in zip(helds, orders)]
        if stage + 2 == len(bits):
            came, before, after = lax.optimization_barrier((came, before, after))
        if stage + 1 < len(bits):
            shape = jax.ShapeDtypeStruct((2 << stage, third, channels), BF16)
            helds = call(double_kernel, [shape] * 3, [], 10**6, *helds, *came, scalars=0)
    thirds = [half for pair in zip(helds, came) for half in pair]

    (grad_features,) = call(
        backward_kernel,
        [jax.ShapeDtypeStruct((tokens, channels), BF16)],
        [frame, wide],
        10**6,
        ids, lengths, cotangent.reshape(strip.shape), before, after, taps, *halves,
        scalars=2,
    )

    other = tile ^ (PLANE * half_lines)
    square = pltpu.VMEM((channels, channels), F32)
    thirds, grad_features = lax.optimization_barrier((thirds, grad_features))
    if third % 16:
        entries = [(e, turn) for turn in range(3) for e in range(group)]
        slots = [
            hidden_block((tile & (group - 1)) ^ member_bits(e, turn, group), group) * 3 + turn
            for e, turn in entries
        ]
        ordered = jnp.zeros((3 * group, third, channels), BF16)
        ordered = ordered.at[jnp.stack(slots)].set(jnp.concatenate(thirds, 0))
        thirds = [ordered.reshape(-1, channels)]
    mine, theirs = call(
        ortho_kernel,
        [
            jax.ShapeDtypeStruct((height, weight_up.shape[1]), F32),
            jax.ShapeDtypeStruct((height, weight_up.shape[1]), BF16),
        ],
        [pltpu.VMEM((weight_up.shape[1], channels), BF16), square, square, square],
        10 * 10**9,
        jnp.stack([tile * height, other * height, tile & (group - 1)]), *thirds,
    )
    theirs = swap(theirs, "tile", PLANE * half_lines)
    theirs = theirs.astype(F32)
    expands = line < half_lines
    muon_up = jnp.where(expands, mine, theirs)
    muon_down = jnp.where(expands, theirs, mine).T
    shape = (share, columns, channels)
    return (block_out.reshape(shape), grad_features.reshape(shape), muon_up, muon_down)


def solution(mesh):
    in_specs = (
        P("tile", None, None),
        P("tile", None, None),
        P(),
        P(),
        P("tile", "own"),
        P("own"),
        P("own", "tile"),
        P(),
        P("tile", None),
        P(),
    )
    out_specs = (
        P(("tile", "own"), None, None),
        P(("tile", "own"), None, None),
        P("tile", "own"),
        P("own", "tile"),
    )
    return jax.shard_map(shards, mesh=mesh, in_specs=in_specs, out_specs=out_specs, check_vma=False)
```

```python
import functools

import jax
import jax.numpy as jnp
from jax import lax
from jax.experimental import pallas as pl
from jax.experimental.pallas import tpu as pltpu
from jax.sharding import PartitionSpec as P

KERNEL = 7
PATCH = 8
COLS = 8
MARGIN = KERNEL // 2
RIM = MARGIN + 1
PLANE = 4
LANES = 128
CHUNK = 8

INV_ROOT_TWO = 0.7071067811865476
INV_ROOT_TAU = 0.3989422804014327
NS_A = 3.4445
NS_B = -4.775
NS_C = 2.0315
EPS_NORM = 1e-06
F32 = jnp.float32
BF16 = jnp.bfloat16


def swap(value, axis, bit):
    return lax.ppermute(value, axis, [(i, i ^ bit) for i in range(lax.axis_size(axis))])


def neighbours(first, last):
    devices = lax.axis_size("tile")
    up = [(i, i + 1) for i in range(devices - 1)]
    down = [(i + 1, i) for i in range(devices - 1)]
    return lax.ppermute(last, "tile", up), lax.ppermute(first, "tile", down)


def in_order(blocks, index):
    bit = 1
    while bit < len(blocks):
        odd = (index & bit) != 0
        blocks = [jnp.where(odd, blocks[s ^ bit], blocks[s]) for s in range(len(blocks))]
        bit *= 2
    return blocks


def call(kernel, out_shape, scratch, flops, *operands, scalars=1, apart=0):
    smem = pl.BlockSpec(memory_space=pltpu.SMEM)
    vmem = pl.BlockSpec(memory_space=pltpu.VMEM)
    return pl.pallas_call(
        kernel,
        out_shape=out_shape,
        in_specs=[smem] * scalars
        + [vmem] * (len(operands) - scalars - apart)
        + [pl.BlockSpec(memory_space=pl.ANY)] * apart,
        out_specs=[vmem] * len(out_shape),
        scratch_shapes=scratch,
        compiler_params=pltpu.CompilerParams(vmem_limit_bytes=40 * 2**20),
        cost_estimate=pl.CostEstimate(flops=flops, bytes_accessed=2**20, transcendentals=0),
    )(*operands)


def convolve(framed, kernel_ref, offset, out_ref, flipped):
    share, columns, channels = out_ref.shape
    chunk = min(CHUNK, share)
    lane_steps = channels // LANES
    column = lax.broadcasted_iota(jnp.int32, (chunk + 2 * MARGIN, columns, LANES), 1)

    def step(index, carry):
        lanes = pl.ds(pl.multiple_of((index % lane_steps) * LANES, LANES), LANES)
        first = (index // lane_steps) * chunk
        rows = framed[pl.ds(offset + first, chunk + 2 * MARGIN), :, lanes]
        total = jnp.zeros((chunk, columns, LANES), F32)
        for col_tap in range(KERNEL):
            reach = col_tap - MARGIN
            moved = rows
            if reach:
                moved = pltpu.roll(rows, (-reach) % columns, 1)
                inside = (column + reach >= 0) & (column + reach < columns)
                moved = jnp.where(inside, moved, 0.0)
            for row_tap in range(KERNEL):
                tap = row_tap * KERNEL + col_tap
                tap = KERNEL * KERNEL - 1 - tap if flipped else tap
                weight = kernel_ref[pl.ds(tap, 1), lanes][None]
                total = total + weight * moved[row_tap : row_tap + chunk]
        out_ref[pl.ds(first, chunk), :, lanes] = total
        return carry

    lax.fori_loop(0, lane_steps * (share // chunk), step, 0)


def place_strip(framed, pieces, before_ref, after_ref, live_rows):
    columns, channels = framed.shape[1:]

    def rows_of(ref):
        value = ref[...].astype(F32)
        return value.reshape(value.shape[0] // columns, columns, channels)

    for start, ref in pieces:
        rows = rows_of(ref)
        framed[pl.ds(start + MARGIN, rows.shape[0])] = rows
    framed[pl.ds(framed.shape[0] - MARGIN, MARGIN)] = jnp.zeros((MARGIN, columns, channels), F32)
    framed[pl.ds(0, MARGIN)] = rows_of(before_ref)[RIM - MARGIN :]
    framed[pl.ds(live_rows + MARGIN, MARGIN)] = rows_of(after_ref)[:MARGIN]


def live_rows(ids, lengths):
    return PATCH * lengths[ids[0]]


def kept_rows(ids, lengths, tissue, tokens):
    row = ids[1] + lax.broadcasted_iota(jnp.int32, (tokens, 1), 0) // COLS
    keep = jnp.zeros((tokens, 1), F32)
    for patch in range(tissue.shape[0]):
        keep = jnp.where(row // PATCH == patch, tissue[patch].astype(F32), keep)
    live = row < live_rows(ids, lengths)
    return live, jnp.where(live, keep, 0.0)


def rims_kernel(ids, lengths, *refs):
    *shares, head, tail = refs
    tokens = shares[0].shape[0]
    last = (live_rows(ids, lengths) - RIM) * COLS
    for s, share in enumerate(shares):

        @pl.when(ids[2] == s)
        def _():
            head[...] = share[: head.shape[0], :]

        @pl.when((last // tokens) ^ ids[2] == s)
        def _():
            start = pl.multiple_of(lax.rem(last, tokens), RIM * COLS)
            tail[...] = share[pl.ds(start, tail.shape[0]), :]


def edges_kernel(ids, lengths, strip, head, tail, first_sem, last_sem):
    rows = head.shape[0]
    last = pl.multiple_of((live_rows(ids, lengths) - RIM) * COLS, RIM * COLS)
    copies = [
        pltpu.make_async_copy(strip.at[pl.ds(0, rows)], head, first_sem),
        pltpu.make_async_copy(strip.at[pl.ds(last, rows)], tail, last_sem),
    ]
    for copy in copies:
        copy.start()
    for copy in copies:
        copy.wait()


def forward_kernel(
    ids,
    lengths,
    tissue,
    strip,
    cotangent,
    before,
    after,
    taps,
    gain,
    layer_scale,
    sent,
    centred_out,
    inverse,
    framed,
    mixed,
):
    place_strip(framed, [(0, strip)], before, after, live_rows(ids, lengths))
    convolve(framed, taps, ids[1], mixed, False)
    tokens, channels = centred_out.shape
    value = mixed[...].reshape(tokens, channels)
    shifted = value - jnp.sum(value, 1, keepdims=True) / channels
    variance = jnp.sum(shifted * shifted, 1, keepdims=True) / channels
    inv_std = lax.rsqrt(variance + 1e-06)
    centred = shifted * inv_std
    centred_out[...] = centred
    inverse[...] = jnp.broadcast_to(inv_std, inverse.shape)
    sent[0] = (centred * gain[...]).astype(BF16)
    _, keep = kept_rows(ids, lengths, tissue, tokens)
    start = pl.multiple_of(ids[1] * COLS, 16)
    grad_out = cotangent[pl.ds(start, tokens), :].astype(F32)
    sent[1] = (keep * layer_scale[...] * grad_out).astype(BF16)


def summed(blocks):
    value = blocks[0][...].astype(F32)
    for ref in blocks[1:]:
        value = value + ref[...].astype(F32)
    return value


def norm_back_kernel(ids, lengths, tissue, centred, inverse, gain, *refs):
    *blocks, grad_mixed = refs
    tokens, channels = grad_mixed.shape
    live, _ = kept_rows(ids, lengths, tissue, tokens)
    scaled_grad = summed(blocks) * gain[...]
    first_mean = jnp.sum(scaled_grad, 1, keepdims=True) / channels
    second_mean = jnp.sum(scaled_grad * centred[...], 1, keepdims=True) / channels
    value = inverse[:, :1] * (scaled_grad - first_mean - centred[...] * second_mean)
    grad_mixed[...] = jnp.where(live, value, 0.0).astype(BF16)


def output_kernel(ids, lengths, tissue, strip, layer_scale, *refs):
    *blocks, block_out = refs
    tokens = block_out.shape[0]
    start = pl.multiple_of(ids[1] * COLS, 16)
    live, keep = kept_rows(ids, lengths, tissue, tokens)
    inputs = strip[pl.ds(start, tokens), :].astype(F32)
    block = inputs + keep * layer_scale[...] * summed(blocks)
    block_out[...] = jnp.where(live, block, 0.0).astype(BF16)


def join_kernel(*refs):
    *blocks, out = refs
    start = 0
    for ref in blocks:
        out[:, start : start + ref.shape[1], :] = ref[...]
        start += ref.shape[1]


def double_kernel(*refs):
    count = len(refs) // 3
    for held, came, out in zip(refs[:count], refs[count : 2 * count], refs[2 * count :]):
        out[: held.shape[0]] = held[...]
        out[held.shape[0] :] = came[...]


def piece_kernel(scalars, *refs):
    *blocks, out = refs
    rows = blocks[0].shape[1]
    for s, block in enumerate(blocks):
        start = pl.multiple_of((scalars[0] ^ s) * rows, rows)
        out[:, pl.ds(start, rows), :] = block[...]


def weights_kernel(scalars, early, late, up, down_t):
    lines, rows = 2 * early.shape[0], early.shape[2]
    bits = lines.bit_length() - 1
    for e in range(lines):
        apart = sum(lines >> (i + 1) for i in range(bits) if e >> i & 1)
        start = pl.multiple_of((scalars[0] ^ apart) * rows, rows)
        later, entry = divmod(e, lines // 2)
        piece = (early, late)[later]
        up[pl.ds(start, rows), :] = piece[entry, 0]
        down_t[pl.ds(start, rows), :] = piece[entry, 1]


def mlp_kernel(scalars, up, down_t, bias, *refs, owners):
    tokens_of = refs[:owners]
    kept, sent, act_out, grad_out, parts = refs[owners:]
    lines = 2 * kept.shape[0]
    plain, over_tokens = ((1,), (0,)), ((0,), (0,))
    count = tokens_of[0].shape[1]
    step = min(256, count)
    units = act_out.shape[1]
    bias_row = bias[...]
    if bias.shape[1] != units:
        bias_row = bias[:, pl.ds(pl.multiple_of(scalars[1] * units, LANES), units)]
    for index, ref in enumerate(tokens_of):
        for start in range(0, count, step):
            hidden = dot(ref[0, start : start + step, :], up[...], plain) + bias_row
            cdf = 0.5 * (1.0 + lax.erf(hidden * INV_ROOT_TWO))
            slope = cdf + hidden * jnp.exp(-0.5 * hidden * hidden) * INV_ROOT_TAU
            grad_act = dot(ref[1, start : start + step, :], down_t[...], plain)
            rows_out = pl.ds(index * count + start, step)
            act_out[rows_out, :] = (hidden * cdf).astype(BF16)
            grad_out[rows_out, :] = (grad_act * slope).astype(BF16)

    for half, (hidden_side, which) in enumerate(((grad_out, 0), (act_out, 1))):
        total = jnp.zeros((units, parts.shape[1]), F32)
        for index, ref in enumerate(tokens_of):
            rows_in = slice(index * count, (index + 1) * count)
            total = total + dot(hidden_side[rows_in, :], ref[which], over_tokens)
        parts[half * units : (half + 1) * units, :] = total
    width = kept.shape[1]
    for q in range(lines):
        block = parts[q * width : (q + 1) * width, :].astype(BF16)
        same = scalars[0] == q % 2

        @pl.when(same)
        def _():
            kept[q // 2] = block

        @pl.when(jnp.logical_not(same))
        def _():
            sent[q // 2] = block


def partial_kernel(act, grad_hidden, up, down_t, mine, *others):
    across = ((1,), (1,))
    count = mine.shape[1]
    step = min(256, count)
    for index, ref in enumerate((mine,) + others):
        for start in range(0, count, step):
            rows_in = slice(index * count + start, index * count + start + step)
            rows_out = slice(start, start + step)
            ref[0, rows_out, :] = dot(grad_hidden[rows_in, :], up[...], across).astype(ref.dtype)
            ref[1, rows_out, :] = dot(act[rows_in, :], down_t[...], across).astype(ref.dtype)


def add_kernel(mine, *refs):
    others, outs = refs[: -2 * PLANE], refs[-2 * PLANE :]
    tokens = outs[0].shape[0]
    for index, out in enumerate(outs):
        which, strip = divmod(index, PLANE)
        rows_in = slice(strip * tokens, (strip + 1) * tokens)
        total = mine[which, rows_in, :]
        for other in others:
            total = total + other[which, rows_in, :].astype(F32)
        out[...] = total.astype(BF16)


def backward_kernel(ids, lengths, cotangent, before, after, taps, *rest):
    *pieces, grad_features, framed, spread = rest
    tokens = grad_features.shape[0]
    share = spread.shape[0]
    placed = [((ids[2] ^ s) * share, piece) for s, piece in enumerate(pieces)]
    place_strip(framed, placed, before, after, live_rows(ids, lengths))
    convolve(framed, taps, ids[1], spread, True)
    start = pl.multiple_of(ids[1] * COLS, 16)
    value = cotangent[pl.ds(start, tokens), :].astype(F32) + spread[...].reshape(grad_features.shape)
    row = ids[1] + lax.broadcasted_iota(jnp.int32, (tokens, 1), 0) // COLS
    grad_features[...] = jnp.where(row < live_rows(ids, lengths), value, 0.0).astype(BF16)


def dot(left, right, contract, precision=None):
    return lax.dot_general(
        left, right, (contract, ((), ())), precision=precision, preferred_element_type=F32
    )


def member_bits(entry, turn, group):
    bits = group.bit_length() - 1
    return sum(1 << ((i + turn) % bits) for i in range(bits) if entry >> i & 1)


def hidden_block(member, group):
    return (member & (PLANE - 1)) * (group // PLANE) + (member >> (PLANE.bit_length() - 1))


def ortho_kernel(scalars, *refs):
    *gathered, mine, theirs, whole, gram, first, half = refs
    channels = whole.shape[1]
    if len(gathered) == 1:
        whole[...] = gathered[0][...]
    else:
        group, third, _ = gathered[0].shape
        group *= 2
        for turn in range(3):
            for e in range(group):
                block = hidden_block(scalars[2] ^ member_bits(e, turn, group), group)
                start = pl.multiple_of((block * 3 + turn) * third, third)
                later, entry = divmod(e, group // 2)
                whole[pl.ds(start, third), :] = gathered[2 * turn + later][entry]

    plain = ((1,), (0,))
    steps = [pl.ds(i, 256) for i in range(0, channels, 256)]
    value = whole[...]
    squares = jnp.zeros((1, 1), F32)
    for rows in steps:
        product = dot(value[:, rows.start : rows.start + 256], value, ((0,), (0,)))
        row = rows.start + lax.broadcasted_iota(jnp.int32, product.shape, 0)
        column = lax.broadcasted_iota(jnp.int32, product.shape, 1)
        on_diagonal = jnp.where(row == column, product, 0.0)
        squares = squares + jnp.sum(jnp.sum(on_diagonal, 1, keepdims=True), 0, keepdims=True)
        gram[rows, :] = product
    scale = lax.rsqrt(squares + EPS_NORM)
    gram[...] = gram[...] * (scale * scale)

    low = gram[...].astype(BF16)
    for rows in steps:
        first[rows, :] = NS_B * gram[rows, :] + NS_C * dot(low[rows.start : rows.start + 256], low, plain)
    first_low = first[...].astype(BF16)
    for rows in steps:
        product = dot(low[rows.start : rows.start + 256], first_low, plain)
        half[rows, :] = NS_A * gram[rows, :] + product
    half_low = half[...].astype(BF16)
    for rows in steps:
        product = dot(half_low[rows.start : rows.start + 256], first_low, plain)
        gram[rows, :] = NS_A * half[rows, :] + product

    height = mine.shape[0]
    picked = -(-2 * height // 16) * 16
    row = lax.broadcasted_iota(jnp.int32, (picked, channels), 0)
    column = lax.broadcasted_iota(jnp.int32, (picked, channels), 1)
    wanted = jnp.where(row < height, scalars[0] + row, scalars[1] + row - height)
    chosen = (column == wanted) & (row < 2 * height)

    def halves(matrix):
        top = matrix.astype(BF16)
        return top, (matrix - top.astype(F32)).astype(BF16)

    def rows_of(ref):
        if height % 8 == 0:
            starts = [pl.multiple_of(scalars[i], 8) for i in range(2)]
            return jnp.concatenate([ref[pl.ds(start, height), :] for start in starts], 0)
        pick = jnp.where(chosen, 1.0, 0.0).astype(BF16)
        top, rest = halves(ref[...])
        return dot(pick, top, plain) + dot(pick, rest, plain)

    gram_rows = rows_of(gram)
    second = NS_B * gram_rows
    second = second + NS_C * dot(gram_rows.astype(BF16), gram[...].astype(BF16), plain)
    both = (
        jnp.where(chosen, NS_A * NS_A, 0.0)
        + NS_A * (rows_of(first) + second)
        + dot(second.astype(BF16), first_low, plain)
    ) * scale
    both = jnp.concatenate(halves(both), 0)
    across = ((1,), (1,))
    for start in range(0, value.shape[0], 256):
        step = min(256, value.shape[0] - start)
        out = dot(both, value[start : start + step], across)
        out = out[:picked] + out[picked:]
        mine[:, start : start + step] = out[:height]
        theirs[:, start : start + step] = out[height : 2 * height].astype(BF16)


def shards(
    features,
    cotangent,
    depth_kernel,
    ln_gain,
    weight_up,
    bias_up,
    weight_down,
    layer_scale,
    tissue,
    lengths,
):
    tile_rows, columns, channels = features.shape
    tiles = lax.axis_size("tile")
    owners = lax.axis_size("own")
    lines = tiles // PLANE
    half_lines = lines // 2
    line_bits = [1 << i for i in range(lines.bit_length() - 1)]
    tile = lax.axis_index("tile")
    own = lax.axis_index("own")
    place, line = tile & (PLANE - 1), tile >> (PLANE.bit_length() - 1)
    share = tile_rows // owners
    offset = own * share
    tokens = share * columns
    ids = jnp.stack([tile, offset, own]).astype(jnp.int32)
    flags = tissue.reshape(-1)
    strip = features.reshape(tile_rows * columns, channels)
    taps = depth_kernel.reshape(KERNEL * KERNEL, channels)
    gain, scale = ln_gain[None], layer_scale[None]
    frame = pltpu.VMEM((tile_rows + 2 * MARGIN, columns, channels), F32)
    wide = pltpu.VMEM((share, columns, channels), F32)
    rims = [jax.ShapeDtypeStruct((RIM * columns, channels), BF16)] * 2

    height = channels // tiles
    units = weight_up.shape[1] // PLANE
    both_weights = jnp.stack([weight_up, weight_down.T])
    pieces = []
    for s in range(PLANE):
        piece = lax.dynamic_slice_in_dim(both_weights, (place ^ s) * units, units, 2)
        pieces.append(swap(piece, "tile", s) if s else piece)
    if height % 16:
        piece = jnp.concatenate(in_order(pieces, place), 1)
    else:
        (piece,) = call(
            piece_kernel,
            [jax.ShapeDtypeStruct((2, PLANE * height, units), BF16)],
            [],
            10**6,
            place[None], *pieces,
        )

    head, tail = call(
        edges_kernel,
        rims,
        [pltpu.SemaphoreType.DMA] * 2,
        10**6,
        tile[None], lengths, strip,
        scalars=2, apart=1,
    )
    before, after = neighbours(head, tail)
    _, before, after = lax.optimization_barrier((piece, before, after))
    bias = bias_up[None]
    if units % LANES:
        bias = lax.dynamic_slice_in_dim(bias, place * units, units, 1)

    sent, centred, inverse = call(
        forward_kernel,
        [
            jax.ShapeDtypeStruct((2, tokens, channels), BF16),
            jax.ShapeDtypeStruct((tokens, channels), F32),
            jax.ShapeDtypeStruct((tokens, LANES), F32),
        ],
        [frame, wide],
        10**6,
        ids, lengths, flags, strip, cotangent.reshape(strip.shape),
        before, after, taps, gain, scale,
        scalars=3,
    )
    held = piece[None]
    for bit in line_bits[:0:-1]:
        shape = jax.ShapeDtypeStruct((2 * held.shape[0],) + held.shape[1:], BF16)
        came = swap(held, "tile", PLANE * bit)
        (held,) = call(double_kernel, [shape], [], 10**6, held, came, scalars=0)
    late = swap(held, "tile", PLANE)
    (mine,) = call(
        join_kernel,
        [jax.ShapeDtypeStruct((2, PLANE * tokens, channels), BF16)],
        [],
        10**6,
        sent, *[swap(sent, "tile", s) for s in range(1, PLANE)],
        scalars=0,
    )
    shares = [mine] + [swap(mine, "own", s) for s in range(1, owners)]

    kept = 2 * units // lines
    total_tokens = owners * PLANE * tokens
    half_parts = jax.ShapeDtypeStruct((lines // 2, kept, channels), BF16)
    hidden_shape = jax.ShapeDtypeStruct((total_tokens, units), BF16)
    weight_shape = jax.ShapeDtypeStruct((channels, units), BF16)
    up, down_t = call(
        weights_kernel, [weight_shape, weight_shape], [], 13 * 10**9, line[None], held, late
    )
    reduced, other, act, grad_hidden = call(
        functools.partial(mlp_kernel, owners=owners),
        [half_parts, half_parts, hidden_shape, hidden_shape],
        [pltpu.VMEM((2 * units, channels), F32)],
        5 * 10**9,
        jnp.stack([line & 1, place]), up, down_t, bias, *shares,
    )

    def split(blocks, bit):
        blocks = blocks.reshape(-1, 2, kept, channels)
        which = jnp.where((line & bit) != 0, 1, 0)
        mine = lax.dynamic_slice_in_dim(blocks, which, 1, 1)
        other = lax.dynamic_slice_in_dim(blocks, 1 - which, 1, 1)
        return mine[:, 0], other[:, 0].astype(BF16)

    arrived = swap(other, "tile", PLANE)

    part_shape = (2, PLANE * tokens, channels)
    mine, *others = call(
        partial_kernel,
        [jax.ShapeDtypeStruct(part_shape, F32)]
        + [jax.ShapeDtypeStruct(part_shape, BF16)] * (owners - 1),
        [],
        10**9,
        act, grad_hidden, up, down_t,
        scalars=0,
    )
    others = [swap(value, "own", s + 1) for s, value in enumerate(others)]
    flat = jax.ShapeDtypeStruct((tokens, channels), BF16)
    blocks = call(add_kernel, [flat] * (2 * PLANE), [], 10**6, mine, *others, scalars=0)
    blocks = [
        swap(value, "tile", i % PLANE) if i % PLANE else value for i, value in enumerate(blocks)
    ]
    for_norm, for_output = blocks[:PLANE], blocks[PLANE:]
    arrived, for_norm[1] = lax.optimization_barrier((arrived, for_norm[1]))
    reduced = reduced.astype(F32) + arrived.astype(F32)
    for bit in line_bits[1:-1]:
        reduced, other = split(reduced, bit)
        reduced = reduced + swap(other, "tile", PLANE * bit).astype(F32)
    reduced, other = split(reduced, line_bits[-1])
    arrived = swap(other, "tile", PLANE * line_bits[-1])

    (grad_mixed,) = call(
        norm_back_kernel,
        [flat],
        [],
        10**6,
        ids, lengths, flags, centred, inverse, gain, *for_norm,
        scalars=3,
    )
    (block_out,) = call(
        output_kernel,
        [flat],
        [],
        10**6,
        ids, lengths, flags, strip, scale, *for_output,
        scalars=3,
    )
    halves = [grad_mixed] + [swap(grad_mixed, "own", s) for s in range(1, owners)]
    head, tail = call(rims_kernel, rims, [], 10**6, ids, lengths, *halves, scalars=2)
    before, after = neighbours(head, tail)
    arrived, before, after, block_out = lax.optimization_barrier(
        (arrived, before, after, block_out)
    )
    grad_t = (reduced + arrived.astype(F32)).astype(BF16)[0]
    group = PLANE * half_lines
    bits = [1 << i for i in range(group.bit_length() - 1)]
    third = kept // 3
    helds = [grad_t[turn * third : (turn + 1) * third][None] for turn in range(3)]
    orders = [bits[turn:] + bits[:turn] for turn in range(3)]
    for stage in range(len(bits)):
        came = [swap(held, "tile", order[stage]) for held, order in zip(helds, orders)]
        if stage + 1 < len(bits):
            shape = jax.ShapeDtypeStruct((2 << stage, third, channels), BF16)
            helds = call(double_kernel, [shape] * 3, [], 10**6, *helds, *came, scalars=0)
    thirds = [half for pair in zip(helds, came) for half in pair]

    (grad_features,) = call(
        backward_kernel,
        [flat],
        [frame, wide],
        10**6,
        ids, lengths, cotangent.reshape(strip.shape), before, after, taps, *halves,
        scalars=2,
    )

    other = tile ^ (PLANE * half_lines)
    square = pltpu.VMEM((channels, channels), F32)
    thirds, grad_features = lax.optimization_barrier((thirds, grad_features))
    if third % 16:
        entries = [(e, turn) for turn in range(3) for e in range(group)]
        slots = [
            hidden_block((tile & (group - 1)) ^ member_bits(e, turn, group), group) * 3 + turn
            for e, turn in entries
        ]
        ordered = jnp.zeros((3 * group, third, channels), BF16)
        ordered = ordered.at[jnp.stack(slots)].set(jnp.concatenate(thirds, 0))
        thirds = [ordered.reshape(-1, channels)]
    mine, theirs = call(
        ortho_kernel,
        [
            jax.ShapeDtypeStruct((height, weight_up.shape[1]), F32),
            jax.ShapeDtypeStruct((height, weight_up.shape[1]), BF16),
        ],
        [pltpu.VMEM((weight_up.shape[1], channels), BF16), square, square, square],
        10 * 10**9,
        jnp.stack([tile * height, other * height, tile & (group - 1)]), *thirds,
    )
    theirs = swap(theirs, "tile", PLANE * half_lines)
    theirs = theirs.astype(F32)
    expands = line < half_lines
    muon_up = jnp.where(expands, mine, theirs)
    muon_down = jnp.where(expands, theirs, mine).T
    shape = (share, columns, channels)
    return (block_out.reshape(shape), grad_features.reshape(shape), muon_up, muon_down)


def solution(mesh):
    in_specs = (
        P("tile", None, None),
        P("tile", None, None),
        P(),
        P(),
        P("tile", "own"),
        P("own"),
        P("own", "tile"),
        P(),
        P("tile", None),
        P(),
    )
    out_specs = (
        P(("tile", "own"), None, None),
        P(("tile", "own"), None, None),
        P("tile", "own"),
        P("own", "tile"),
    )
    return jax.shard_map(shards, mesh=mesh, in_specs=in_specs, out_specs=out_specs, check_vma=False)
```

```python
import functools

import jax
import jax.numpy as jnp
from jax import lax
from jax.experimental import pallas as pl
from jax.experimental.pallas import tpu as pltpu
from jax.sharding import PartitionSpec as P

KERNEL = 7
PATCH = 8
COLS = 8
MARGIN = KERNEL // 2
RIM = MARGIN + 1
PLANE = 4
LANES = 128
CHUNK = 8

INV_ROOT_TWO = 0.7071067811865476
INV_ROOT_TAU = 0.3989422804014327
NS_A = 3.4445
NS_B = -4.775
NS_C = 2.0315
EPS_NORM = 1e-06
F32 = jnp.float32
BF16 = jnp.bfloat16


def swap(value, axis, bit):
    return lax.ppermute(value, axis, [(i, i ^ bit) for i in range(lax.axis_size(axis))])


def neighbours(first, last):
    devices = lax.axis_size("tile")
    up = [(i, i + 1) for i in range(devices - 1)]
    down = [(i + 1, i) for i in range(devices - 1)]
    return lax.ppermute(last, "tile", up), lax.ppermute(first, "tile", down)


def in_order(blocks, index):
    bit = 1
    while bit < len(blocks):
        odd = (index & bit) != 0
        blocks = [jnp.where(odd, blocks[s ^ bit], blocks[s]) for s in range(len(blocks))]
        bit *= 2
    return blocks


def call(
    kernel, out_shape, scratch, flops, *operands, scalars=1, apart=0, out_space=pltpu.VMEM
):
    smem = pl.BlockSpec(memory_space=pltpu.SMEM)
    vmem = pl.BlockSpec(memory_space=pltpu.VMEM)
    return pl.pallas_call(
        kernel,
        out_shape=out_shape,
        in_specs=[smem] * scalars
        + [vmem] * (len(operands) - scalars - apart)
        + [pl.BlockSpec(memory_space=pl.ANY)] * apart,
        out_specs=[pl.BlockSpec(memory_space=out_space)] * len(out_shape),
        scratch_shapes=scratch,
        compiler_params=pltpu.CompilerParams(vmem_limit_bytes=40 * 2**20),
        cost_estimate=pl.CostEstimate(flops=flops, bytes_accessed=2**20, transcendentals=0),
    )(*operands)


def convolve(framed, kernel_ref, offset, out_ref, flipped):
    share, columns, channels = out_ref.shape
    chunk = min(CHUNK, share)
    lane_steps = channels // LANES
    column = lax.broadcasted_iota(jnp.int32, (chunk + 2 * MARGIN, columns, LANES), 1)

    def step(index, carry):
        lanes = pl.ds(pl.multiple_of((index % lane_steps) * LANES, LANES), LANES)
        first = (index // lane_steps) * chunk
        rows = framed[pl.ds(offset + first, chunk + 2 * MARGIN), :, lanes]
        total = jnp.zeros((chunk, columns, LANES), F32)
        for col_tap in range(KERNEL):
            reach = col_tap - MARGIN
            moved = rows
            if reach:
                moved = pltpu.roll(rows, (-reach) % columns, 1)
                inside = (column + reach >= 0) & (column + reach < columns)
                moved = jnp.where(inside, moved, 0.0)
            for row_tap in range(KERNEL):
                tap = row_tap * KERNEL + col_tap
                tap = KERNEL * KERNEL - 1 - tap if flipped else tap
                weight = kernel_ref[pl.ds(tap, 1), lanes][None]
                total = total + weight * moved[row_tap : row_tap + chunk]
        out_ref[pl.ds(first, chunk), :, lanes] = total
        return carry

    lax.fori_loop(0, lane_steps * (share // chunk), step, 0)


def place_strip(framed, pieces, before_ref, after_ref, live_rows):
    columns, channels = framed.shape[1:]

    def rows_of(ref):
        value = ref[...].astype(F32)
        return value.reshape(value.shape[0] // columns, columns, channels)

    for start, ref in pieces:
        rows = rows_of(ref)
        framed[pl.ds(start + MARGIN, rows.shape[0])] = rows
    framed[pl.ds(framed.shape[0] - MARGIN, MARGIN)] = jnp.zeros((MARGIN, columns, channels), F32)
    framed[pl.ds(0, MARGIN)] = rows_of(before_ref)[RIM - MARGIN :]
    framed[pl.ds(live_rows + MARGIN, MARGIN)] = rows_of(after_ref)[:MARGIN]


def live_rows(ids, lengths):
    return PATCH * lengths[ids[0]]


def kept_rows(ids, lengths, tissue, tokens):
    row = ids[1] + lax.broadcasted_iota(jnp.int32, (tokens, 1), 0) // COLS
    keep = jnp.zeros((tokens, 1), F32)
    for patch in range(tissue.shape[0]):
        keep = jnp.where(row // PATCH == patch, tissue[patch].astype(F32), keep)
    live = row < live_rows(ids, lengths)
    return live, jnp.where(live, keep, 0.0)


def rims_kernel(ids, lengths, *refs):
    *shares, head, tail = refs
    tokens = shares[0].shape[0]
    last = (live_rows(ids, lengths) - RIM) * COLS
    for s, share in enumerate(shares):

        @pl.when(ids[2] == s)
        def _():
            head[...] = share[: head.shape[0], :]

        @pl.when((last // tokens) ^ ids[2] == s)
        def _():
            start = pl.multiple_of(lax.rem(last, tokens), RIM * COLS)
            tail[...] = share[pl.ds(start, tail.shape[0]), :]


def edges_kernel(ids, lengths, strip, head, tail, first_sem, last_sem):
    rows = head.shape[0]
    last = pl.multiple_of((live_rows(ids, lengths) - RIM) * COLS, RIM * COLS)
    copies = [
        pltpu.make_async_copy(strip.at[pl.ds(0, rows)], head, first_sem),
        pltpu.make_async_copy(strip.at[pl.ds(last, rows)], tail, last_sem),
    ]
    for copy in copies:
        copy.start()
    for copy in copies:
        copy.wait()


def forward_kernel(
    ids,
    lengths,
    tissue,
    strip,
    cotangent,
    before,
    after,
    taps,
    gain,
    layer_scale,
    sent,
    centred_out,
    inverse,
    framed,
    mixed,
):
    place_strip(framed, [(0, strip)], before, after, live_rows(ids, lengths))
    convolve(framed, taps, ids[1], mixed, False)
    tokens, channels = centred_out.shape
    value = mixed[...].reshape(tokens, channels)
    shifted = value - jnp.sum(value, 1, keepdims=True) / channels
    variance = jnp.sum(shifted * shifted, 1, keepdims=True) / channels
    inv_std = lax.rsqrt(variance + 1e-06)
    centred = shifted * inv_std
    centred_out[...] = centred
    inverse[...] = jnp.broadcast_to(inv_std, inverse.shape)
    sent[0] = (centred * gain[...]).astype(BF16)
    _, keep = kept_rows(ids, lengths, tissue, tokens)
    start = pl.multiple_of(ids[1] * COLS, 16)
    grad_out = cotangent[pl.ds(start, tokens), :].astype(F32)
    sent[1] = (keep * layer_scale[...] * grad_out).astype(BF16)


def summed(blocks):
    value = blocks[0][...].astype(F32)
    for ref in blocks[1:]:
        value = value + ref[...].astype(F32)
    return value


def norm_back_kernel(ids, lengths, tissue, centred, inverse, gain, *refs):
    *blocks, grad_mixed = refs
    tokens, channels = grad_mixed.shape
    live, _ = kept_rows(ids, lengths, tissue, tokens)
    scaled_grad = summed(blocks) * gain[...]
    first_mean = jnp.sum(scaled_grad, 1, keepdims=True) / channels
    second_mean = jnp.sum(scaled_grad * centred[...], 1, keepdims=True) / channels
    value = inverse[:, :1] * (scaled_grad - first_mean - centred[...] * second_mean)
    grad_mixed[...] = jnp.where(live, value, 0.0).astype(BF16)


def output_kernel(ids, lengths, tissue, strip, layer_scale, *refs):
    *blocks, block_out = refs
    tokens = block_out.shape[0]
    start = pl.multiple_of(ids[1] * COLS, 16)
    live, keep = kept_rows(ids, lengths, tissue, tokens)
    inputs = strip[pl.ds(start, tokens), :].astype(F32)
    block = inputs + keep * layer_scale[...] * summed(blocks)
    block_out[...] = jnp.where(live, block, 0.0).astype(BF16)


def join_kernel(*refs):
    *blocks, out = refs
    start = 0
    for ref in blocks:
        out[:, start : start + ref.shape[1], :] = ref[...]
        start += ref.shape[1]


def double_kernel(*refs):
    count = len(refs) // 3
    for held, came, out in zip(refs[:count], refs[count : 2 * count], refs[2 * count :]):
        out[: held.shape[0]] = held[...]
        out[held.shape[0] :] = came[...]


def piece_kernel(scalars, *refs):
    *blocks, out = refs
    rows = blocks[0].shape[1]
    for s, block in enumerate(blocks):
        start = pl.multiple_of((scalars[0] ^ s) * rows, rows)
        out[:, pl.ds(start, rows), :] = block[...]


def weights_kernel(scalars, early, late, up, down_t):
    lines, rows = 2 * early.shape[0], early.shape[2]
    bits = lines.bit_length() - 1
    for e in range(lines):
        apart = sum(lines >> (i + 1) for i in range(bits) if e >> i & 1)
        start = pl.multiple_of((scalars[0] ^ apart) * rows, rows)
        later, entry = divmod(e, lines // 2)
        piece = (early, late)[later]
        up[pl.ds(start, rows), :] = piece[entry, 0]
        down_t[pl.ds(start, rows), :] = piece[entry, 1]


def mlp_kernel(scalars, up, down_t, bias, *refs, owners):
    tokens_of = refs[:owners]
    kept, sent, act_out, grad_out, parts = refs[owners:]
    lines = 2 * kept.shape[0]
    plain, over_tokens = ((1,), (0,)), ((0,), (0,))
    count = tokens_of[0].shape[1]
    step = min(256, count)
    units = act_out.shape[1]
    bias_row = bias[...]
    if bias.shape[1] != units:
        bias_row = bias[:, pl.ds(pl.multiple_of(scalars[1] * units, LANES), units)]
    for index, ref in enumerate(tokens_of):
        for start in range(0, count, step):
            hidden = dot(ref[0, start : start + step, :], up[...], plain) + bias_row
            cdf = 0.5 * (1.0 + lax.erf(hidden * INV_ROOT_TWO))
            slope = cdf + hidden * jnp.exp(-0.5 * hidden * hidden) * INV_ROOT_TAU
            grad_act = dot(ref[1, start : start + step, :], down_t[...], plain)
            rows_out = pl.ds(index * count + start, step)
            act_out[rows_out, :] = (hidden * cdf).astype(BF16)
            grad_out[rows_out, :] = (grad_act * slope).astype(BF16)

    for half, (hidden_side, which) in enumerate(((grad_out, 0), (act_out, 1))):
        total = jnp.zeros((units, parts.shape[1]), F32)
        for index, ref in enumerate(tokens_of):
            rows_in = slice(index * count, (index + 1) * count)
            total = total + dot(hidden_side[rows_in, :], ref[which], over_tokens)
        parts[half * units : (half + 1) * units, :] = total
    width = kept.shape[1]
    for q in range(lines):
        block = parts[q * width : (q + 1) * width, :].astype(BF16)
        same = scalars[0] == q % 2

        @pl.when(same)
        def _():
            kept[q // 2] = block

        @pl.when(jnp.logical_not(same))
        def _():
            sent[q // 2] = block


def partial_kernel(act, grad_hidden, up, down_t, mine, *others):
    across = ((1,), (1,))
    count = mine.shape[1]
    step = min(256, count)
    for index, ref in enumerate((mine,) + others):
        for start in range(0, count, step):
            rows_in = slice(index * count + start, index * count + start + step)
            rows_out = slice(start, start + step)
            ref[0, rows_out, :] = dot(grad_hidden[rows_in, :], up[...], across).astype(ref.dtype)
            ref[1, rows_out, :] = dot(act[rows_in, :], down_t[...], across).astype(ref.dtype)


def add_kernel(mine, *refs):
    *refs, staged, sems = refs
    others, outs = refs[: -2 * PLANE], refs[-2 * PLANE :]
    tokens = outs[0].shape[0]
    copies = []
    for index, out in enumerate(outs):
        which, strip = divmod(index, PLANE)
        rows_in = slice(strip * tokens, (strip + 1) * tokens)
        total = mine[which, rows_in, :]
        for other in others:
            total = total + other[which, rows_in, :].astype(F32)
        staged[index] = total.astype(BF16)
        copies.append(pltpu.make_async_copy(staged.at[index], out, sems.at[index]))
        copies[-1].start()
    for copy in copies:
        copy.wait()


def backward_kernel(ids, lengths, cotangent, before, after, taps, *rest):
    *pieces, grad_features, framed, spread = rest
    tokens = grad_features.shape[0]
    share = spread.shape[0]
    placed = [((ids[2] ^ s) * share, piece) for s, piece in enumerate(pieces)]
    place_strip(framed, placed, before, after, live_rows(ids, lengths))
    convolve(framed, taps, ids[1], spread, True)
    start = pl.multiple_of(ids[1] * COLS, 16)
    value = cotangent[pl.ds(start, tokens), :].astype(F32) + spread[...].reshape(grad_features.shape)
    row = ids[1] + lax.broadcasted_iota(jnp.int32, (tokens, 1), 0) // COLS
    grad_features[...] = jnp.where(row < live_rows(ids, lengths), value, 0.0).astype(BF16)


def dot(left, right, contract, precision=None):
    return lax.dot_general(
        left, right, (contract, ((), ())), precision=precision, preferred_element_type=F32
    )


def hidden_block(member, group):
    return (member & (PLANE - 1)) * (group // PLANE) + (member >> (PLANE.bit_length() - 1))


def ortho_kernel(scalars, *refs):
    *gathered, mine, theirs, whole, gram, first, half = refs
    channels = whole.shape[1]
    if len(gathered) == 1:
        whole[...] = gathered[0][...]
    else:
        rows = gathered[0].shape[0]
        for e, ref in enumerate(gathered):
            block = hidden_block(scalars[2] ^ e, len(gathered))
            whole[pl.ds(pl.multiple_of(block * rows, rows), rows), :] = ref[...]

    plain = ((1,), (0,))
    steps = [pl.ds(i, 256) for i in range(0, channels, 256)]
    value = whole[...]
    squares = jnp.zeros((1, 1), F32)
    for rows in steps:
        product = dot(value[:, rows.start : rows.start + 256], value, ((0,), (0,)))
        row = rows.start + lax.broadcasted_iota(jnp.int32, product.shape, 0)
        column = lax.broadcasted_iota(jnp.int32, product.shape, 1)
        on_diagonal = jnp.where(row == column, product, 0.0)
        squares = squares + jnp.sum(jnp.sum(on_diagonal, 1, keepdims=True), 0, keepdims=True)
        gram[rows, :] = product
    scale = lax.rsqrt(squares + EPS_NORM)
    gram[...] = gram[...] * (scale * scale)

    low = gram[...].astype(BF16)
    for rows in steps:
        first[rows, :] = NS_B * gram[rows, :] + NS_C * dot(low[rows.start : rows.start + 256], low, plain)
    first_low = first[...].astype(BF16)
    for rows in steps:
        product = dot(low[rows.start : rows.start + 256], first_low, plain)
        half[rows, :] = NS_A * gram[rows, :] + product
    half_low = half[...].astype(BF16)
    for rows in steps:
        product = dot(half_low[rows.start : rows.start + 256], first_low, plain)
        gram[rows, :] = NS_A * half[rows, :] + product

    height = mine.shape[0]
    picked = -(-2 * height // 16) * 16
    row = lax.broadcasted_iota(jnp.int32, (picked, channels), 0)
    column = lax.broadcasted_iota(jnp.int32, (picked, channels), 1)
    wanted = jnp.where(row < height, scalars[0] + row, scalars[1] + row - height)
    chosen = (column == wanted) & (row < 2 * height)

    def halves(matrix):
        top = matrix.astype(BF16)
        return top, (matrix - top.astype(F32)).astype(BF16)

    def rows_of(ref):
        if height % 8 == 0:
            starts = [pl.multiple_of(scalars[i], 8) for i in range(2)]
            return jnp.concatenate([ref[pl.ds(start, height), :] for start in starts], 0)
        pick = jnp.where(chosen, 1.0, 0.0).astype(BF16)
        top, rest = halves(ref[...])
        return dot(pick, top, plain) + dot(pick, rest, plain)

    gram_rows = rows_of(gram)
    second = NS_B * gram_rows
    second = second + NS_C * dot(gram_rows.astype(BF16), gram[...].astype(BF16), plain)
    both = (
        jnp.where(chosen, NS_A * NS_A, 0.0)
        + NS_A * (rows_of(first) + second)
        + dot(second.astype(BF16), first_low, plain)
    ) * scale
    both = jnp.concatenate(halves(both), 0)
    across = ((1,), (1,))
    for start in range(0, value.shape[0], 256):
        step = min(256, value.shape[0] - start)
        out = dot(both, value[start : start + step], across)
        out = out[:picked] + out[picked:]
        mine[:, start : start + step] = out[:height]
        theirs[:, start : start + step] = out[height : 2 * height].astype(BF16)


def shards(
    features,
    cotangent,
    depth_kernel,
    ln_gain,
    weight_up,
    bias_up,
    weight_down,
    layer_scale,
    tissue,
    lengths,
):
    tile_rows, columns, channels = features.shape
    tiles = lax.axis_size("tile")
    owners = lax.axis_size("own")
    lines = tiles // PLANE
    half_lines = lines // 2
    line_bits = [1 << i for i in range(lines.bit_length() - 1)]
    tile = lax.axis_index("tile")
    own = lax.axis_index("own")
    place, line = tile & (PLANE - 1), tile >> (PLANE.bit_length() - 1)
    share = tile_rows // owners
    offset = own * share
    tokens = share * columns
    ids = jnp.stack([tile, offset, own]).astype(jnp.int32)
    flags = tissue.reshape(-1)
    strip = features.reshape(tile_rows * columns, channels)
    taps = depth_kernel.reshape(KERNEL * KERNEL, channels)
    gain, scale = ln_gain[None], layer_scale[None]
    frame = pltpu.VMEM((tile_rows + 2 * MARGIN, columns, channels), F32)
    wide = pltpu.VMEM((share, columns, channels), F32)
    rims = [jax.ShapeDtypeStruct((RIM * columns, channels), BF16)] * 2

    height = channels // tiles
    units = weight_up.shape[1] // PLANE
    both_weights = jnp.stack([weight_up, weight_down.T])
    pieces = []
    for s in range(PLANE):
        piece = lax.dynamic_slice_in_dim(both_weights, (place ^ s) * units, units, 2)
        pieces.append(swap(piece, "tile", s) if s else piece)
    if height % 16:
        piece = jnp.concatenate(in_order(pieces, place), 1)
    else:
        (piece,) = call(
            piece_kernel,
            [jax.ShapeDtypeStruct((2, PLANE * height, units), BF16)],
            [],
            10**6,
            place[None], *pieces,
        )

    head, tail = call(
        edges_kernel,
        rims,
        [pltpu.SemaphoreType.DMA] * 2,
        10**6,
        tile[None], lengths, strip,
        scalars=2, apart=1,
    )
    before, after = neighbours(head, tail)
    piece, before, after = lax.optimization_barrier((piece, before, after))
    bias = bias_up[None]
    if units % LANES:
        bias = lax.dynamic_slice_in_dim(bias, place * units, units, 1)

    sent, centred, inverse = call(
        forward_kernel,
        [
            jax.ShapeDtypeStruct((2, tokens, channels), BF16),
            jax.ShapeDtypeStruct((tokens, channels), F32),
            jax.ShapeDtypeStruct((tokens, LANES), F32),
        ],
        [frame, wide],
        10**6,
        ids, lengths, flags, strip, cotangent.reshape(strip.shape),
        before, after, taps, gain, scale,
        scalars=3,
    )
    held = piece[None]
    for bit in line_bits[:0:-1]:
        shape = jax.ShapeDtypeStruct((2 * held.shape[0],) + held.shape[1:], BF16)
        came = swap(held, "tile", PLANE * bit)
        (held,) = call(double_kernel, [shape], [], 10**6, held, came, scalars=0)
    late = swap(held, "tile", PLANE)
    (mine,) = call(
        join_kernel,
        [jax.ShapeDtypeStruct((2, PLANE * tokens, channels), BF16)],
        [],
        10**6,
        sent, *[swap(sent, "tile", s) for s in range(1, PLANE)],
        scalars=0,
    )
    shares = [mine] + [swap(mine, "own", s) for s in range(1, owners)]

    kept = 2 * units // lines
    total_tokens = owners * PLANE * tokens
    half_parts = jax.ShapeDtypeStruct((lines // 2, kept, channels), BF16)
    hidden_shape = jax.ShapeDtypeStruct((total_tokens, units), BF16)
    weight_shape = jax.ShapeDtypeStruct((channels, units), BF16)
    up, down_t = call(
        weights_kernel, [weight_shape, weight_shape], [], 13 * 10**9, line[None], held, late
    )
    reduced, other, act, grad_hidden = call(
        functools.partial(mlp_kernel, owners=owners),
        [half_parts, half_parts, hidden_shape, hidden_shape],
        [pltpu.VMEM((2 * units, channels), F32)],
        5 * 10**9,
        jnp.stack([line & 1, place]), up, down_t, bias, *shares,
    )

    def split(blocks, bit):
        blocks = blocks.reshape(-1, 2, kept, channels)
        which = jnp.where((line & bit) != 0, 1, 0)
        mine = lax.dynamic_slice_in_dim(blocks, which, 1, 1)
        other = lax.dynamic_slice_in_dim(blocks, 1 - which, 1, 1)
        return mine[:, 0], other[:, 0].astype(BF16)

    arrived = swap(other, "tile", PLANE)

    part_shape = (2, PLANE * tokens, channels)
    mine, *others = call(
        partial_kernel,
        [jax.ShapeDtypeStruct(part_shape, F32)]
        + [jax.ShapeDtypeStruct(part_shape, BF16)] * (owners - 1),
        [],
        10**9,
        act, grad_hidden, up, down_t,
        scalars=0,
    )
    others = [swap(value, "own", s + 1) for s, value in enumerate(others)]
    flat = jax.ShapeDtypeStruct((tokens, channels), BF16)
    blocks = call(
        add_kernel,
        [flat] * (2 * PLANE),
        [
            pltpu.VMEM((2 * PLANE, tokens, channels), BF16),
            pltpu.SemaphoreType.DMA((2 * PLANE,)),
        ],
        10**6,
        mine, *others,
        scalars=0, out_space=pltpu.HBM,
    )
    blocks = [
        swap(value, "tile", i % PLANE) if i % PLANE else value for i, value in enumerate(blocks)
    ]
    for_norm, for_output = blocks[:PLANE], blocks[PLANE:]
    arrived, for_norm[1] = lax.optimization_barrier((arrived, for_norm[1]))
    reduced = reduced.astype(F32) + arrived.astype(F32)
    for bit in line_bits[1:-1]:
        reduced, other = split(reduced, bit)
        reduced = reduced + swap(other, "tile", PLANE * bit).astype(F32)
    reduced, other = split(reduced, line_bits[-1])
    arrived = swap(other, "tile", PLANE * line_bits[-1])

    (grad_mixed,) = call(
        norm_back_kernel,
        [flat],
        [],
        10**6,
        ids, lengths, flags, centred, inverse, gain, *for_norm,
        scalars=3,
    )
    (block_out,) = call(
        output_kernel,
        [flat],
        [],
        10**6,
        ids, lengths, flags, strip, scale, *for_output,
        scalars=3,
    )
    halves = [grad_mixed] + [swap(grad_mixed, "own", s) for s in range(1, owners)]
    head, tail = call(rims_kernel, rims, [], 10**6, ids, lengths, *halves, scalars=2)
    before, after = neighbours(head, tail)
    arrived, before, after, block_out = lax.optimization_barrier(
        (arrived, before, after, block_out)
    )
    grad_t = (reduced + arrived.astype(F32)).astype(BF16)[0]
    group = PLANE * half_lines
    if group == 8:
        near = [swap(grad_t, "tile", bit) for bit in (1, 2, 4)]
        corner = swap(grad_t, "tile", 7)
        far = [swap(near[1], "tile", 1), swap(near[0], "tile", 4), swap(near[2], "tile", 2)]
        gathered = [grad_t, near[0], near[1], far[0], near[2], far[1], far[2], corner]
    else:
        gathered = [swap(grad_t, "tile", e) if e else grad_t for e in range(group)]

    (grad_features,) = call(
        backward_kernel,
        [flat],
        [frame, wide],
        10**6,
        ids, lengths, cotangent.reshape(strip.shape), before, after, taps, *halves,
        scalars=2,
    )

    other = tile ^ (PLANE * half_lines)
    square = pltpu.VMEM((channels, channels), F32)
    gathered, grad_features = lax.optimization_barrier((gathered, grad_features))
    if kept % 16:
        slots = [hidden_block((tile & (group - 1)) ^ e, group) for e in range(group)]
        ordered = jnp.zeros((group, kept, channels), BF16)
        ordered = ordered.at[jnp.stack(slots)].set(jnp.stack(gathered))
        gathered = [ordered.reshape(-1, channels)]
    mine, theirs = call(
        ortho_kernel,
        [
            jax.ShapeDtypeStruct((height, weight_up.shape[1]), F32),
            jax.ShapeDtypeStruct((height, weight_up.shape[1]), BF16),
        ],
        [pltpu.VMEM((weight_up.shape[1], channels), BF16), square, square, square],
        10 * 10**9,
        jnp.stack([tile * height, other * height, tile & (group - 1)]), *gathered,
    )
    theirs = swap(theirs, "tile", PLANE * half_lines)
    theirs = theirs.astype(F32)
    expands = line < half_lines
    muon_up = jnp.where(expands, mine, theirs)
    muon_down = jnp.where(expands, theirs, mine).T
    shape = (share, columns, channels)
    return (block_out.reshape(shape), grad_features.reshape(shape), muon_up, muon_down)


def solution(mesh):
    in_specs = (
        P("tile", None, None),
        P("tile", None, None),
        P(),
        P(),
        P("tile", "own"),
        P("own"),
        P("own", "tile"),
        P(),
        P("tile", None),
        P(),
    )
    out_specs = (
        P(("tile", "own"), None, None),
        P(("tile", "own"), None, None),
        P("tile", "own"),
        P("own", "tile"),
    )
    return jax.shard_map(shards, mesh=mesh, in_specs=in_specs, out_specs=out_specs, check_vma=False)
```

```python
import functools
import math

import jax
import jax.numpy as jnp
from jax import lax
from jax.experimental import pallas as pl
from jax.experimental.pallas import tpu as pltpu
from jax.sharding import PartitionSpec as P

KERNEL = 7
PATCH = 8
COLS = 8
MARGIN = KERNEL // 2
RIM = MARGIN + 1
PLANE = 4
LANES = 128
CHUNK = 8
SLACK = 4 * 2**20

INV_ROOT_TWO = 0.7071067811865476
INV_ROOT_TAU = 0.3989422804014327
NS_A = 3.4445
NS_B = -4.775
NS_C = 2.0315
EPS_NORM = 1e-06
F32 = jnp.float32
BF16 = jnp.bfloat16


def swap(value, axis, bit):
    return lax.ppermute(value, axis, [(i, i ^ bit) for i in range(lax.axis_size(axis))])


def neighbours(first, last):
    devices = lax.axis_size("tile")
    up = [(i, i + 1) for i in range(devices - 1)]
    down = [(i + 1, i) for i in range(devices - 1)]
    return lax.ppermute(last, "tile", up), lax.ppermute(first, "tile", down)


def in_order(blocks, index):
    bit = 1
    while bit < len(blocks):
        odd = (index & bit) != 0
        blocks = [jnp.where(odd, blocks[s ^ bit], blocks[s]) for s in range(len(blocks))]
        bit *= 2
    return blocks


def call(kernel, out_shape, scratch, flops, *operands, scalars=1, apart=0):
    held = sum(a.size * a.dtype.itemsize for a in operands + tuple(out_shape))
    room = sum(math.prod(a.shape) * 4 for a in scratch if hasattr(a, "shape"))
    smem = pl.BlockSpec(memory_space=pltpu.SMEM)
    vmem = pl.BlockSpec(memory_space=pltpu.VMEM)
    return pl.pallas_call(
        kernel,
        out_shape=out_shape,
        in_specs=[smem] * scalars
        + [vmem] * (len(operands) - scalars - apart)
        + [pl.BlockSpec(memory_space=pltpu.HBM)] * apart,
        out_specs=[vmem] * len(out_shape),
        scratch_shapes=scratch,
        compiler_params=pltpu.CompilerParams(vmem_limit_bytes=2 * held + room + SLACK),
        cost_estimate=pl.CostEstimate(flops=flops, bytes_accessed=2**20, transcendentals=0),
    )(*operands)


def convolve(framed, kernel_ref, offset, out_ref, flipped):
    share, columns, channels = out_ref.shape
    chunk = min(CHUNK, share)
    lane_steps = channels // LANES
    column = lax.broadcasted_iota(jnp.int32, (chunk + 2 * MARGIN, columns, LANES), 1)

    def step(index, carry):
        lanes = pl.ds(pl.multiple_of((index % lane_steps) * LANES, LANES), LANES)
        first = (index // lane_steps) * chunk
        rows = framed[pl.ds(offset + first, chunk + 2 * MARGIN), :, lanes]
        total = jnp.zeros((chunk, columns, LANES), F32)
        for col_tap in range(KERNEL):
            reach = col_tap - MARGIN
            moved = rows
            if reach:
                moved = pltpu.roll(rows, (-reach) % columns, 1)
                inside = (column + reach >= 0) & (column + reach < columns)
                moved = jnp.where(inside, moved, 0.0)
            for row_tap in range(KERNEL):
                tap = row_tap * KERNEL + col_tap
                tap = KERNEL * KERNEL - 1 - tap if flipped else tap
                weight = kernel_ref[pl.ds(tap, 1), lanes][None]
                total = total + weight * moved[row_tap : row_tap + chunk]
        out_ref[pl.ds(first, chunk), :, lanes] = total
        return carry

    lax.fori_loop(0, lane_steps * (share // chunk), step, 0)


def place_strip(framed, pieces, before_ref, after_ref, live_rows):
    columns, channels = framed.shape[1:]

    def rows_of(ref):
        value = ref[...].astype(F32)
        return value.reshape(value.shape[0] // columns, columns, channels)

    for start, ref in pieces:
        rows = rows_of(ref)
        framed[pl.ds(start + MARGIN, rows.shape[0])] = rows
    framed[pl.ds(framed.shape[0] - MARGIN, MARGIN)] = jnp.zeros((MARGIN, columns, channels), F32)
    framed[pl.ds(0, MARGIN)] = rows_of(before_ref)[RIM - MARGIN :]
    framed[pl.ds(live_rows + MARGIN, MARGIN)] = rows_of(after_ref)[:MARGIN]


def live_rows(ids, lengths):
    return PATCH * lengths[ids[0]]


def kept_rows(ids, lengths, tissue, tokens):
    row = ids[1] + lax.broadcasted_iota(jnp.int32, (tokens, 1), 0) // COLS
    keep = jnp.zeros((tokens, 1), F32)
    for patch in range(tissue.shape[0]):
        keep = jnp.where(row // PATCH == patch, tissue[patch].astype(F32), keep)
    live = row < live_rows(ids, lengths)
    return live, jnp.where(live, keep, 0.0)


def rims_kernel(ids, lengths, *refs):
    *shares, head, tail = refs
    tokens = shares[0].shape[0]
    last = (live_rows(ids, lengths) - RIM) * COLS
    for s, share in enumerate(shares):

        @pl.when(ids[2] == s)
        def _():
            head[...] = share[: head.shape[0], :]

        @pl.when((last // tokens) ^ ids[2] == s)
        def _():
            start = pl.multiple_of(lax.rem(last, tokens), RIM * COLS)
            tail[...] = share[pl.ds(start, tail.shape[0]), :]


def edges_kernel(ids, lengths, strip, head, tail, first_sem, last_sem):
    rows = head.shape[0]
    last = pl.multiple_of((live_rows(ids, lengths) - RIM) * COLS, RIM * COLS)
    copies = [
        pltpu.make_async_copy(strip.at[pl.ds(0, rows)], head, first_sem),
        pltpu.make_async_copy(strip.at[pl.ds(last, rows)], tail, last_sem),
    ]
    for copy in copies:
        copy.start()
    for copy in copies:
        copy.wait()


def forward_kernel(
    ids,
    lengths,
    tissue,
    strip,
    cotangent,
    before,
    after,
    taps,
    gain,
    layer_scale,
    sent,
    centred_out,
    inverse,
    framed,
    mixed,
):
    place_strip(framed, [(0, strip)], before, after, live_rows(ids, lengths))
    convolve(framed, taps, ids[1], mixed, False)
    tokens, channels = centred_out.shape
    value = mixed[...].reshape(tokens, channels)
    shifted = value - jnp.sum(value, 1, keepdims=True) / channels
    variance = jnp.sum(shifted * shifted, 1, keepdims=True) / channels
    inv_std = lax.rsqrt(variance + 1e-06)
    centred = shifted * inv_std
    centred_out[...] = centred
    inverse[...] = jnp.broadcast_to(inv_std, inverse.shape)
    sent[0] = (centred * gain[...]).astype(BF16)
    _, keep = kept_rows(ids, lengths, tissue, tokens)
    start = pl.multiple_of(ids[1] * COLS, 16)
    grad_out = cotangent[pl.ds(start, tokens), :].astype(F32)
    sent[1] = (keep * layer_scale[...] * grad_out).astype(BF16)


def summed(blocks):
    value = blocks[0][...].astype(F32)
    for ref in blocks[1:]:
        value = value + ref[...].astype(F32)
    return value


def norm_back_kernel(ids, lengths, tissue, centred, inverse, gain, *refs):
    *blocks, grad_mixed = refs
    tokens, channels = grad_mixed.shape
    live, _ = kept_rows(ids, lengths, tissue, tokens)
    scaled_grad = summed(blocks) * gain[...]
    first_mean = jnp.sum(scaled_grad, 1, keepdims=True) / channels
    second_mean = jnp.sum(scaled_grad * centred[...], 1, keepdims=True) / channels
    value = inverse[:, :1] * (scaled_grad - first_mean - centred[...] * second_mean)
    grad_mixed[...] = jnp.where(live, value, 0.0).astype(BF16)


def output_kernel(ids, lengths, tissue, strip, layer_scale, *refs):
    *blocks, block_out = refs
    tokens = block_out.shape[0]
    start = pl.multiple_of(ids[1] * COLS, 16)
    live, keep = kept_rows(ids, lengths, tissue, tokens)
    inputs = strip[pl.ds(start, tokens), :].astype(F32)
    block = inputs + keep * layer_scale[...] * summed(blocks)
    block_out[...] = jnp.where(live, block, 0.0).astype(BF16)


def join_kernel(*refs):
    *blocks, out = refs
    start = 0
    for ref in blocks:
        out[:, start : start + ref.shape[1], :] = ref[...]
        start += ref.shape[1]


def double_kernel(*refs):
    count = len(refs) // 3
    for held, came, out in zip(refs[:count], refs[count : 2 * count], refs[2 * count :]):
        out[: held.shape[0]] = held[...]
        out[held.shape[0] :] = came[...]


def piece_kernel(scalars, *refs):
    *blocks, out = refs
    rows = blocks[0].shape[1]
    for s, block in enumerate(blocks):
        start = pl.multiple_of((scalars[0] ^ s) * rows, rows)
        out[:, pl.ds(start, rows), :] = block[...]


def weights_kernel(scalars, early, late, up, down_t):
    lines, rows = 2 * early.shape[0], early.shape[2]
    bits = lines.bit_length() - 1
    for e in range(lines):
        apart = sum(lines >> (i + 1) for i in range(bits) if e >> i & 1)
        start = pl.multiple_of((scalars[0] ^ apart) * rows, rows)
        later, entry = divmod(e, lines // 2)
        piece = (early, late)[later]
        up[pl.ds(start, rows), :] = piece[entry, 0]
        down_t[pl.ds(start, rows), :] = piece[entry, 1]


def mlp_kernel(scalars, up, down_t, bias, *refs, owners):
    tokens_of = refs[:owners]
    kept, sent, act_out, grad_out, parts = refs[owners:]
    lines = 2 * kept.shape[0]
    plain, over_tokens = ((1,), (0,)), ((0,), (0,))
    count = tokens_of[0].shape[1]
    step = min(256, count)
    units = act_out.shape[1]
    bias_row = bias[...]
    if bias.shape[1] != units:
        bias_row = bias[:, pl.ds(pl.multiple_of(scalars[1] * units, LANES), units)]
    for index, ref in enumerate(tokens_of):
        for start in range(0, count, step):
            hidden = dot(ref[0, start : start + step, :], up[...], plain) + bias_row
            cdf = 0.5 * (1.0 + lax.erf(hidden * INV_ROOT_TWO))
            slope = cdf + hidden * jnp.exp(-0.5 * hidden * hidden) * INV_ROOT_TAU
            grad_act = dot(ref[1, start : start + step, :], down_t[...], plain)
            rows_out = pl.ds(index * count + start, step)
            act_out[rows_out, :] = (hidden * cdf).astype(BF16)
            grad_out[rows_out, :] = (grad_act * slope).astype(BF16)

    for half, (hidden_side, which) in enumerate(((grad_out, 0), (act_out, 1))):
        total = jnp.zeros((units, parts.shape[1]), F32)
        for index, ref in enumerate(tokens_of):
            rows_in = slice(index * count, (index + 1) * count)
            total = total + dot(hidden_side[rows_in, :], ref[which], over_tokens)
        parts[half * units : (half + 1) * units, :] = total
    width = kept.shape[1]
    for q in range(lines):
        block = parts[q * width : (q + 1) * width, :].astype(BF16)
        same = scalars[0] == q % 2

        @pl.when(same)
        def _():
            kept[q // 2] = block

        @pl.when(jnp.logical_not(same))
        def _():
            sent[q // 2] = block


def partial_kernel(act, grad_hidden, up, down_t, mine, *others):
    across = ((1,), (1,))
    count = mine.shape[1]
    step = min(256, count)
    for index, ref in enumerate((mine,) + others):
        for start in range(0, count, step):
            rows_in = slice(index * count + start, index * count + start + step)
            rows_out = slice(start, start + step)
            ref[0, rows_out, :] = dot(grad_hidden[rows_in, :], up[...], across).astype(ref.dtype)
            ref[1, rows_out, :] = dot(act[rows_in, :], down_t[...], across).astype(ref.dtype)


def add_kernel(mine, *refs):
    others, outs = refs[: -2 * PLANE], refs[-2 * PLANE :]
    tokens = outs[0].shape[0]
    for index, out in enumerate(outs):
        which, strip = divmod(index, PLANE)
        rows_in = slice(strip * tokens, (strip + 1) * tokens)
        total = mine[which, rows_in, :]
        for other in others:
            total = total + other[which, rows_in, :].astype(F32)
        out[...] = total.astype(BF16)


def backward_kernel(ids, lengths, cotangent, before, after, taps, *rest):
    *pieces, grad_features, framed, spread = rest
    tokens = grad_features.shape[0]
    share = spread.shape[0]
    placed = [((ids[2] ^ s) * share, piece) for s, piece in enumerate(pieces)]
    place_strip(framed, placed, before, after, live_rows(ids, lengths))
    convolve(framed, taps, ids[1], spread, True)
    start = pl.multiple_of(ids[1] * COLS, 16)
    value = cotangent[pl.ds(start, tokens), :].astype(F32) + spread[...].reshape(grad_features.shape)
    row = ids[1] + lax.broadcasted_iota(jnp.int32, (tokens, 1), 0) // COLS
    grad_features[...] = jnp.where(row < live_rows(ids, lengths), value, 0.0).astype(BF16)


def dot(left, right, contract, precision=None):
    return lax.dot_general(
        left, right, (contract, ((), ())), precision=precision, preferred_element_type=F32
    )


def hidden_block(member, group):
    return (member & (PLANE - 1)) * (group // PLANE) + (member >> (PLANE.bit_length() - 1))


def ortho_kernel(scalars, *refs):
    *gathered, mine, theirs, whole, gram, first, half = refs
    channels = whole.shape[1]
    if len(gathered) == 1:
        whole[...] = gathered[0][...]
    else:
        rows = gathered[0].shape[0]
        for e, ref in enumerate(gathered):
            block = hidden_block(scalars[2] ^ e, len(gathered))
            whole[pl.ds(pl.multiple_of(block * rows, rows), rows), :] = ref[...]

    plain = ((1,), (0,))
    steps = [pl.ds(i, 256) for i in range(0, channels, 256)]
    value = whole[...]
    squares = jnp.zeros((1, 1), F32)
    for rows in steps:
        product = dot(value[:, rows.start : rows.start + 256], value, ((0,), (0,)))
        row = rows.start + lax.broadcasted_iota(jnp.int32, product.shape, 0)
        column = lax.broadcasted_iota(jnp.int32, product.shape, 1)
        on_diagonal = jnp.where(row == column, product, 0.0)
        squares = squares + jnp.sum(jnp.sum(on_diagonal, 1, keepdims=True), 0, keepdims=True)
        gram[rows, :] = product
    scale = lax.rsqrt(squares + EPS_NORM)
    gram[...] = gram[...] * (scale * scale)

    low = gram[...].astype(BF16)
    for rows in steps:
        first[rows, :] = NS_B * gram[rows, :] + NS_C * dot(low[rows.start : rows.start + 256], low, plain)
    first_low = first[...].astype(BF16)
    for rows in steps:
        product = dot(low[rows.start : rows.start + 256], first_low, plain)
        half[rows, :] = NS_A * gram[rows, :] + product
    half_low = half[...].astype(BF16)
    for rows in steps:
        product = dot(half_low[rows.start : rows.start + 256], first_low, plain)
        gram[rows, :] = NS_A * half[rows, :] + product

    height = mine.shape[0]
    picked = -(-2 * height // 16) * 16
    row = lax.broadcasted_iota(jnp.int32, (picked, channels), 0)
    column = lax.broadcasted_iota(jnp.int32, (picked, channels), 1)
    wanted = jnp.where(row < height, scalars[0] + row, scalars[1] + row - height)
    chosen = (column == wanted) & (row < 2 * height)

    def halves(matrix):
        top = matrix.astype(BF16)
        return top, (matrix - top.astype(F32)).astype(BF16)

    def rows_of(ref):
        if height % 8 == 0:
            starts = [pl.multiple_of(scalars[i], 8) for i in range(2)]
            return jnp.concatenate([ref[pl.ds(start, height), :] for start in starts], 0)
        pick = jnp.where(chosen, 1.0, 0.0).astype(BF16)
        top, rest = halves(ref[...])
        return dot(pick, top, plain) + dot(pick, rest, plain)

    gram_rows = rows_of(gram)
    second = NS_B * gram_rows
    second = second + NS_C * dot(gram_rows.astype(BF16), gram[...].astype(BF16), plain)
    both = (
        jnp.where(chosen, NS_A * NS_A, 0.0)
        + NS_A * (rows_of(first) + second)
        + dot(second.astype(BF16), first_low, plain)
    ) * scale
    both = jnp.concatenate(halves(both), 0)
    across = ((1,), (1,))
    for start in range(0, value.shape[0], 256):
        step = min(256, value.shape[0] - start)
        out = dot(both, value[start : start + step], across)
        out = out[:picked] + out[picked:]
        mine[:, start : start + step] = out[:height]
        theirs[:, start : start + step] = out[height : 2 * height].astype(BF16)


def shards(
    features,
    cotangent,
    depth_kernel,
    ln_gain,
    weight_up,
    bias_up,
    weight_down,
    layer_scale,
    tissue,
    lengths,
):
    tile_rows, columns, channels = features.shape
    tiles = lax.axis_size("tile")
    owners = lax.axis_size("own")
    lines = tiles // PLANE
    half_lines = lines // 2
    line_bits = [1 << i for i in range(lines.bit_length() - 1)]
    tile = lax.axis_index("tile")
    own = lax.axis_index("own")
    place, line = tile & (PLANE - 1), tile >> (PLANE.bit_length() - 1)
    share = tile_rows // owners
    offset = own * share
    tokens = share * columns
    ids = jnp.stack([tile, offset, own]).astype(jnp.int32)
    flags = tissue.reshape(-1)
    strip = features.reshape(tile_rows * columns, channels)
    taps = depth_kernel.reshape(KERNEL * KERNEL, channels)
    gain, scale = ln_gain[None], layer_scale[None]
    frame = pltpu.VMEM((tile_rows + 2 * MARGIN, columns, channels), F32)
    wide = pltpu.VMEM((share, columns, channels), F32)
    rims = [jax.ShapeDtypeStruct((RIM * columns, channels), BF16)] * 2

    height = channels // tiles
    units = weight_up.shape[1] // PLANE
    both_weights = jnp.stack([weight_up, weight_down.T])
    pieces = []
    for s in range(PLANE):
        piece = lax.dynamic_slice_in_dim(both_weights, (place ^ s) * units, units, 2)
        pieces.append(swap(piece, "tile", s) if s else piece)
    if height % 16:
        piece = jnp.concatenate(in_order(pieces, place), 1)
    else:
        (piece,) = call(
            piece_kernel,
            [jax.ShapeDtypeStruct((2, PLANE * height, units), BF16)],
            [],
            10**6,
            place[None], *pieces,
        )

    head, tail = call(
        edges_kernel,
        rims,
        [pltpu.SemaphoreType.DMA] * 2,
        10**6,
        tile[None], lengths, strip,
        scalars=2, apart=1,
    )
    before, after = neighbours(head, tail)
    piece, before, after = lax.optimization_barrier((piece, before, after))
    bias = bias_up[None]
    if units % LANES:
        bias = lax.dynamic_slice_in_dim(bias, place * units, units, 1)

    sent, centred, inverse = call(
        forward_kernel,
        [
            jax.ShapeDtypeStruct((2, tokens, channels), BF16),
            jax.ShapeDtypeStruct((tokens, channels), F32),
            jax.ShapeDtypeStruct((tokens, LANES), F32),
        ],
        [frame, wide],
        10**6,
        ids, lengths, flags, strip, cotangent.reshape(strip.shape),
        before, after, taps, gain, scale,
        scalars=3,
    )
    held = piece[None]
    for bit in line_bits[:0:-1]:
        shape = jax.ShapeDtypeStruct((2 * held.shape[0],) + held.shape[1:], BF16)
        came = swap(held, "tile", PLANE * bit)
        (held,) = call(double_kernel, [shape], [], 10**6, held, came, scalars=0)
    late = swap(held, "tile", PLANE)
    (mine,) = call(
        join_kernel,
        [jax.ShapeDtypeStruct((2, PLANE * tokens, channels), BF16)],
        [],
        10**6,
        sent, *[swap(sent, "tile", s) for s in range(1, PLANE)],
        scalars=0,
    )
    shares = [mine] + [swap(mine, "own", s) for s in range(1, owners)]

    kept = 2 * units // lines
    total_tokens = owners * PLANE * tokens
    half_parts = jax.ShapeDtypeStruct((lines // 2, kept, channels), BF16)
    hidden_shape = jax.ShapeDtypeStruct((total_tokens, units), BF16)
    weight_shape = jax.ShapeDtypeStruct((channels, units), BF16)
    up, down_t = call(
        weights_kernel, [weight_shape, weight_shape], [], 13 * 10**9, line[None], held, late
    )
    reduced, other, act, grad_hidden = call(
        functools.partial(mlp_kernel, owners=owners),
        [half_parts, half_parts, hidden_shape, hidden_shape],
        [pltpu.VMEM((2 * units, channels), F32)],
        5 * 10**9,
        jnp.stack([line & 1, place]), up, down_t, bias, *shares,
    )

    def split(blocks, bit):
        blocks = blocks.reshape(-1, 2, kept, channels)
        which = jnp.where((line & bit) != 0, 1, 0)
        mine = lax.dynamic_slice_in_dim(blocks, which, 1, 1)
        other = lax.dynamic_slice_in_dim(blocks, 1 - which, 1, 1)
        return mine[:, 0], other[:, 0].astype(BF16)

    arrived = swap(other, "tile", PLANE)

    part_shape = (2, PLANE * tokens, channels)
    mine, *others = call(
        partial_kernel,
        [jax.ShapeDtypeStruct(part_shape, F32)]
        + [jax.ShapeDtypeStruct(part_shape, BF16)] * (owners - 1),
        [],
        10**9,
        act, grad_hidden, up, down_t,
        scalars=0,
    )
    others = [swap(value, "own", s + 1) for s, value in enumerate(others)]
    flat = jax.ShapeDtypeStruct((tokens, channels), BF16)
    blocks = call(
        add_kernel,
        [flat] * (2 * PLANE),
        [],
        10**6,
        mine, *others,
        scalars=0,
    )
    blocks = [
        swap(value, "tile", i % PLANE) if i % PLANE else value for i, value in enumerate(blocks)
    ]
    for_norm, for_output = blocks[:PLANE], blocks[PLANE:]
    arrived, for_norm[1] = lax.optimization_barrier((arrived, for_norm[1]))
    reduced = reduced.astype(F32) + arrived.astype(F32)
    for bit in line_bits[1:-1]:
        reduced, other = split(reduced, bit)
        reduced = reduced + swap(other, "tile", PLANE * bit).astype(F32)
    reduced, other = split(reduced, line_bits[-1])
    arrived = swap(other, "tile", PLANE * line_bits[-1])

    (grad_mixed,) = call(
        norm_back_kernel,
        [flat],
        [],
        10**6,
        ids, lengths, flags, centred, inverse, gain, *for_norm,
        scalars=3,
    )
    (block_out,) = call(
        output_kernel,
        [flat],
        [],
        10**6,
        ids, lengths, flags, strip, scale, *for_output,
        scalars=3,
    )
    halves = [grad_mixed] + [swap(grad_mixed, "own", s) for s in range(1, owners)]
    head, tail = call(rims_kernel, rims, [], 10**6, ids, lengths, *halves, scalars=2)
    before, after = neighbours(head, tail)
    arrived, before, after, block_out = lax.optimization_barrier(
        (arrived, before, after, block_out)
    )
    grad_t = (reduced + arrived.astype(F32)).astype(BF16)[0]
    group = PLANE * half_lines
    if group == 8:
        near = [swap(grad_t, "tile", bit) for bit in (1, 2, 4)]
        corner = swap(grad_t, "tile", 7)
        far = [swap(near[1], "tile", 1), swap(near[0], "tile", 4), swap(near[2], "tile", 2)]
        gathered = [grad_t, near[0], near[1], far[0], near[2], far[1], far[2], corner]
    else:
        gathered = [swap(grad_t, "tile", e) if e else grad_t for e in range(group)]

    (grad_features,) = call(
        backward_kernel,
        [flat],
        [frame, wide],
        10**6,
        ids, lengths, cotangent.reshape(strip.shape), before, after, taps, *halves,
        scalars=2,
    )

    other = tile ^ (PLANE * half_lines)
    square = pltpu.VMEM((channels, channels), F32)
    gathered, grad_features = lax.optimization_barrier((gathered, grad_features))
    if kept % 16:
        slots = [hidden_block((tile & (group - 1)) ^ e, group) for e in range(group)]
        ordered = jnp.zeros((group, kept, channels), BF16)
        ordered = ordered.at[jnp.stack(slots)].set(jnp.stack(gathered))
        gathered = [ordered.reshape(-1, channels)]
    mine, theirs = call(
        ortho_kernel,
        [
            jax.ShapeDtypeStruct((height, weight_up.shape[1]), F32),
            jax.ShapeDtypeStruct((height, weight_up.shape[1]), BF16),
        ],
        [pltpu.VMEM((weight_up.shape[1], channels), BF16), square, square, square],
        10 * 10**9,
        jnp.stack([tile * height, other * height, tile & (group - 1)]), *gathered,
    )
    theirs = swap(theirs, "tile", PLANE * half_lines)
    theirs = theirs.astype(F32)
    expands = line < half_lines
    muon_up = jnp.where(expands, mine, theirs)
    muon_down = jnp.where(expands, theirs, mine).T
    shape = (share, columns, channels)
    return (block_out.reshape(shape), grad_features.reshape(shape), muon_up, muon_down)


def solution(mesh):
    in_specs = (
        P("tile", None, None),
        P("tile", None, None),
        P(),
        P(),
        P("tile", "own"),
        P("own"),
        P("own", "tile"),
        P(),
        P("tile", None),
        P(),
    )
    out_specs = (
        P(("tile", "own"), None, None),
        P(("tile", "own"), None, None),
        P("tile", "own"),
        P("own", "tile"),
    )
    return jax.shard_map(shards, mesh=mesh, in_specs=in_specs, out_specs=out_specs, check_vma=False)
```

```python
import functools
import math

import jax
import jax.numpy as jnp
from jax import lax
from jax.experimental import pallas as pl
from jax.experimental.pallas import tpu as pltpu
from jax.sharding import PartitionSpec as P

KERNEL = 7
PATCH = 8
COLS = 8
MARGIN = KERNEL // 2
RIM = MARGIN + 1
PLANE = 4
LANES = 128
CHUNK = 8
SLACK = 4 * 2**20

INV_ROOT_TWO = 0.7071067811865476
INV_ROOT_TAU = 0.3989422804014327
NS_A = 3.4445
NS_B = -4.775
NS_C = 2.0315
EPS_NORM = 1e-06
F32 = jnp.float32
BF16 = jnp.bfloat16


def swap(value, axis, bit):
    return lax.ppermute(value, axis, [(i, i ^ bit) for i in range(lax.axis_size(axis))])


def neighbours(first, last):
    devices = lax.axis_size("tile")
    up = [(i, i + 1) for i in range(devices - 1)]
    down = [(i + 1, i) for i in range(devices - 1)]
    return lax.ppermute(last, "tile", up), lax.ppermute(first, "tile", down)


def in_order(blocks, index):
    bit = 1
    while bit < len(blocks):
        odd = (index & bit) != 0
        blocks = [jnp.where(odd, blocks[s ^ bit], blocks[s]) for s in range(len(blocks))]
        bit *= 2
    return blocks


def call(kernel, out_shape, scratch, flops, *operands, scalars=1, apart=0):
    held = sum(a.size * a.dtype.itemsize for a in operands + tuple(out_shape))
    room = sum(math.prod(a.shape) * 4 for a in scratch if hasattr(a, "shape"))
    smem = pl.BlockSpec(memory_space=pltpu.SMEM)
    vmem = pl.BlockSpec(memory_space=pltpu.VMEM)
    return pl.pallas_call(
        kernel,
        out_shape=out_shape,
        in_specs=[smem] * scalars
        + [vmem] * (len(operands) - scalars - apart)
        + [pl.BlockSpec(memory_space=pltpu.HBM)] * apart,
        out_specs=[vmem] * len(out_shape),
        scratch_shapes=scratch,
        compiler_params=pltpu.CompilerParams(vmem_limit_bytes=2 * held + room + SLACK),
        cost_estimate=pl.CostEstimate(flops=flops, bytes_accessed=2**20, transcendentals=0),
    )(*operands)


def convolve(framed, kernel_ref, offset, out_ref, flipped):
    share, columns, channels = out_ref.shape
    chunk = min(CHUNK, share)
    lane_steps = channels // LANES
    column = lax.broadcasted_iota(jnp.int32, (chunk + 2 * MARGIN, columns, LANES), 1)

    def step(index, carry):
        lanes = pl.ds(pl.multiple_of((index % lane_steps) * LANES, LANES), LANES)
        first = (index // lane_steps) * chunk
        rows = framed[pl.ds(offset + first, chunk + 2 * MARGIN), :, lanes]
        total = jnp.zeros((chunk, columns, LANES), F32)
        for col_tap in range(KERNEL):
            reach = col_tap - MARGIN
            moved = rows
            if reach:
                moved = pltpu.roll(rows, (-reach) % columns, 1)
                inside = (column + reach >= 0) & (column + reach < columns)
                moved = jnp.where(inside, moved, 0.0)
            for row_tap in range(KERNEL):
                tap = row_tap * KERNEL + col_tap
                tap = KERNEL * KERNEL - 1 - tap if flipped else tap
                weight = kernel_ref[pl.ds(tap, 1), lanes][None]
                total = total + weight * moved[row_tap : row_tap + chunk]
        out_ref[pl.ds(first, chunk), :, lanes] = total
        return carry

    lax.fori_loop(0, lane_steps * (share // chunk), step, 0)


def place_strip(framed, pieces, before_ref, after_ref, live_rows):
    columns, channels = framed.shape[1:]

    def rows_of(ref):
        value = ref[...].astype(F32)
        return value.reshape(value.shape[0] // columns, columns, channels)

    for start, ref in pieces:
        rows = rows_of(ref)
        framed[pl.ds(start + MARGIN, rows.shape[0])] = rows
    framed[pl.ds(framed.shape[0] - MARGIN, MARGIN)] = jnp.zeros((MARGIN, columns, channels), F32)
    framed[pl.ds(0, MARGIN)] = rows_of(before_ref)[RIM - MARGIN :]
    framed[pl.ds(live_rows + MARGIN, MARGIN)] = rows_of(after_ref)[:MARGIN]


def live_rows(ids, lengths):
    return PATCH * lengths[ids[0]]


def kept_rows(ids, lengths, tissue, tokens):
    row = ids[1] + lax.broadcasted_iota(jnp.int32, (tokens, 1), 0) // COLS
    keep = jnp.zeros((tokens, 1), F32)
    for patch in range(tissue.shape[0]):
        keep = jnp.where(row // PATCH == patch, tissue[patch].astype(F32), keep)
    live = row < live_rows(ids, lengths)
    return live, jnp.where(live, keep, 0.0)


def rims_kernel(ids, lengths, *refs):
    *shares, head, tail = refs
    tokens = shares[0].shape[0]
    last = (live_rows(ids, lengths) - RIM) * COLS
    for s, share in enumerate(shares):

        @pl.when(ids[2] == s)
        def _():
            head[...] = share[: head.shape[0], :]

        @pl.when((last // tokens) ^ ids[2] == s)
        def _():
            start = pl.multiple_of(lax.rem(last, tokens), RIM * COLS)
            tail[...] = share[pl.ds(start, tail.shape[0]), :]


def edges_kernel(ids, lengths, strip, head, tail, first_sem, last_sem):
    rows = head.shape[0]
    last = pl.multiple_of((live_rows(ids, lengths) - RIM) * COLS, RIM * COLS)
    copies = [
        pltpu.make_async_copy(strip.at[pl.ds(0, rows)], head, first_sem),
        pltpu.make_async_copy(strip.at[pl.ds(last, rows)], tail, last_sem),
    ]
    for copy in copies:
        copy.start()
    for copy in copies:
        copy.wait()


def forward_kernel(
    ids,
    lengths,
    tissue,
    strip,
    cotangent,
    before,
    after,
    taps,
    gain,
    layer_scale,
    sent,
    centred_out,
    inverse,
    framed,
    mixed,
):
    place_strip(framed, [(0, strip)], before, after, live_rows(ids, lengths))
    convolve(framed, taps, ids[1], mixed, False)
    tokens, channels = centred_out.shape
    value = mixed[...].reshape(tokens, channels)
    shifted = value - jnp.sum(value, 1, keepdims=True) / channels
    variance = jnp.sum(shifted * shifted, 1, keepdims=True) / channels
    inv_std = lax.rsqrt(variance + 1e-06)
    centred = shifted * inv_std
    centred_out[...] = centred
    inverse[...] = jnp.broadcast_to(inv_std, inverse.shape)
    sent[0] = (centred * gain[...]).astype(BF16)
    _, keep = kept_rows(ids, lengths, tissue, tokens)
    start = pl.multiple_of(ids[1] * COLS, 16)
    grad_out = cotangent[pl.ds(start, tokens), :].astype(F32)
    sent[1] = (keep * layer_scale[...] * grad_out).astype(BF16)


def summed(blocks):
    value = blocks[0][...].astype(F32)
    for ref in blocks[1:]:
        value = value + ref[...].astype(F32)
    return value


def norm_back_kernel(ids, lengths, tissue, centred, inverse, gain, *refs):
    *blocks, grad_mixed = refs
    tokens, channels = grad_mixed.shape
    live, _ = kept_rows(ids, lengths, tissue, tokens)
    scaled_grad = summed(blocks) * gain[...]
    first_mean = jnp.sum(scaled_grad, 1, keepdims=True) / channels
    second_mean = jnp.sum(scaled_grad * centred[...], 1, keepdims=True) / channels
    value = inverse[:, :1] * (scaled_grad - first_mean - centred[...] * second_mean)
    grad_mixed[...] = jnp.where(live, value, 0.0).astype(BF16)


def output_kernel(ids, lengths, tissue, strip, layer_scale, *refs):
    *blocks, block_out = refs
    tokens = block_out.shape[0]
    start = pl.multiple_of(ids[1] * COLS, 16)
    live, keep = kept_rows(ids, lengths, tissue, tokens)
    inputs = strip[pl.ds(start, tokens), :].astype(F32)
    block = inputs + keep * layer_scale[...] * summed(blocks)
    block_out[...] = jnp.where(live, block, 0.0).astype(BF16)


def join_kernel(*refs):
    *blocks, out = refs
    start = 0
    for ref in blocks:
        out[:, start : start + ref.shape[1], :] = ref[...]
        start += ref.shape[1]


def double_kernel(*refs):
    count = len(refs) // 3
    for held, came, out in zip(refs[:count], refs[count : 2 * count], refs[2 * count :]):
        out[: held.shape[0]] = held[...]
        out[held.shape[0] :] = came[...]


def piece_kernel(scalars, *refs):
    *blocks, out = refs
    rows = blocks[0].shape[1]
    for s, block in enumerate(blocks):
        start = pl.multiple_of((scalars[0] ^ s) * rows, rows)
        out[:, pl.ds(start, rows), :] = block[...]


def weights_kernel(scalars, early, late, up, down_t):
    lines, rows = 2 * early.shape[0], early.shape[2]
    bits = lines.bit_length() - 1
    for e in range(lines):
        apart = sum(lines >> (i + 1) for i in range(bits) if e >> i & 1)
        start = pl.multiple_of((scalars[0] ^ apart) * rows, rows)
        later, entry = divmod(e, lines // 2)
        piece = (early, late)[later]
        up[pl.ds(start, rows), :] = piece[entry, 0]
        down_t[pl.ds(start, rows), :] = piece[entry, 1]


def mlp_kernel(scalars, up, down_t, bias, *refs, owners):
    tokens_of = refs[:owners]
    kept, sent, act_out, grad_out, parts = refs[owners:]
    lines = 2 * kept.shape[0]
    plain, over_tokens = ((1,), (0,)), ((0,), (0,))
    count = tokens_of[0].shape[1]
    step = min(256, count)
    units = act_out.shape[1]
    bias_row = bias[...]
    if bias.shape[1] != units:
        bias_row = bias[:, pl.ds(pl.multiple_of(scalars[1] * units, LANES), units)]
    for index, ref in enumerate(tokens_of):
        for start in range(0, count, step):
            hidden = dot(ref[0, start : start + step, :], up[...], plain) + bias_row
            cdf = 0.5 * (1.0 + lax.erf(hidden * INV_ROOT_TWO))
            slope = cdf + hidden * jnp.exp(-0.5 * hidden * hidden) * INV_ROOT_TAU
            grad_act = dot(ref[1, start : start + step, :], down_t[...], plain)
            rows_out = pl.ds(index * count + start, step)
            act_out[rows_out, :] = (hidden * cdf).astype(BF16)
            grad_out[rows_out, :] = (grad_act * slope).astype(BF16)

    for half, (hidden_side, which) in enumerate(((grad_out, 0), (act_out, 1))):
        total = jnp.zeros((units, parts.shape[1]), F32)
        for index, ref in enumerate(tokens_of):
            rows_in = slice(index * count, (index + 1) * count)
            total = total + dot(hidden_side[rows_in, :], ref[which], over_tokens)
        parts[half * units : (half + 1) * units, :] = total
    width = kept.shape[1]
    for q in range(lines):
        block = parts[q * width : (q + 1) * width, :].astype(BF16)
        same = scalars[0] == q % 2

        @pl.when(same)
        def _():
            kept[q // 2] = block

        @pl.when(jnp.logical_not(same))
        def _():
            sent[q // 2] = block


def partial_kernel(act, grad_hidden, up, down_t, mine, *others):
    across = ((1,), (1,))
    count = mine.shape[1]
    step = min(256, count)
    for index, ref in enumerate((mine,) + others):
        for start in range(0, count, step):
            rows_in = slice(index * count + start, index * count + start + step)
            rows_out = slice(start, start + step)
            ref[0, rows_out, :] = dot(grad_hidden[rows_in, :], up[...], across).astype(ref.dtype)
            ref[1, rows_out, :] = dot(act[rows_in, :], down_t[...], across).astype(ref.dtype)


def add_kernel(mine, *refs):
    others, outs = refs[: -2 * PLANE], refs[-2 * PLANE :]
    tokens = outs[0].shape[0]
    for index, out in enumerate(outs):
        which, strip = divmod(index, PLANE)
        rows_in = slice(strip * tokens, (strip + 1) * tokens)
        total = mine[which, rows_in, :]
        for other in others:
            total = total + other[which, rows_in, :].astype(F32)
        out[...] = total.astype(BF16)


def backward_kernel(ids, lengths, cotangent, before, after, taps, *rest):
    *pieces, grad_features, framed, spread = rest
    tokens = grad_features.shape[0]
    share = spread.shape[0]
    placed = [((ids[2] ^ s) * share, piece) for s, piece in enumerate(pieces)]
    place_strip(framed, placed, before, after, live_rows(ids, lengths))
    convolve(framed, taps, ids[1], spread, True)
    start = pl.multiple_of(ids[1] * COLS, 16)
    value = cotangent[pl.ds(start, tokens), :].astype(F32) + spread[...].reshape(grad_features.shape)
    row = ids[1] + lax.broadcasted_iota(jnp.int32, (tokens, 1), 0) // COLS
    grad_features[...] = jnp.where(row < live_rows(ids, lengths), value, 0.0).astype(BF16)


def dot(left, right, contract, precision=None):
    return lax.dot_general(
        left, right, (contract, ((), ())), precision=precision, preferred_element_type=F32
    )


def hidden_block(member, group):
    return (member & (PLANE - 1)) * (group // PLANE) + (member >> (PLANE.bit_length() - 1))


def ortho_kernel(scalars, *refs):
    *gathered, mine, theirs, whole, gram, first, half = refs
    channels = whole.shape[1]
    if len(gathered) == 1:
        whole[...] = gathered[0][...]
    else:
        rows = gathered[0].shape[0]
        for e, ref in enumerate(gathered):
            block = hidden_block(scalars[2] ^ e, len(gathered))
            whole[pl.ds(pl.multiple_of(block * rows, rows), rows), :] = ref[...]

    plain = ((1,), (0,))
    steps = [pl.ds(i, 256) for i in range(0, channels, 256)]
    value = whole[...]
    squares = jnp.zeros((1, 1), F32)
    for rows in steps:
        product = dot(value[:, rows.start : rows.start + 256], value, ((0,), (0,)))
        row = rows.start + lax.broadcasted_iota(jnp.int32, product.shape, 0)
        column = lax.broadcasted_iota(jnp.int32, product.shape, 1)
        on_diagonal = jnp.where(row == column, product, 0.0)
        squares = squares + jnp.sum(jnp.sum(on_diagonal, 1, keepdims=True), 0, keepdims=True)
        gram[rows, :] = product
    scale = lax.rsqrt(squares + EPS_NORM)
    gram[...] = gram[...] * (scale * scale)

    low = gram[...].astype(BF16)
    for rows in steps:
        first[rows, :] = NS_B * gram[rows, :] + NS_C * dot(low[rows.start : rows.start + 256], low, plain)
    first_low = first[...].astype(BF16)
    for rows in steps:
        product = dot(low[rows.start : rows.start + 256], first_low, plain)
        half[rows, :] = NS_A * gram[rows, :] + product
    half_low = half[...].astype(BF16)
    for rows in steps:
        product = dot(half_low[rows.start : rows.start + 256], first_low, plain)
        gram[rows, :] = NS_A * half[rows, :] + product

    height = mine.shape[0]
    picked = -(-2 * height // 16) * 16
    row = lax.broadcasted_iota(jnp.int32, (picked, channels), 0)
    column = lax.broadcasted_iota(jnp.int32, (picked, channels), 1)
    wanted = jnp.where(row < height, scalars[0] + row, scalars[1] + row - height)
    chosen = (column == wanted) & (row < 2 * height)

    def halves(matrix):
        top = matrix.astype(BF16)
        return top, (matrix - top.astype(F32)).astype(BF16)

    def rows_of(ref):
        if height % 8 == 0:
            starts = [pl.multiple_of(scalars[i], 8) for i in range(2)]
            return jnp.concatenate([ref[pl.ds(start, height), :] for start in starts], 0)
        pick = jnp.where(chosen, 1.0, 0.0).astype(BF16)
        top, rest = halves(ref[...])
        return dot(pick, top, plain) + dot(pick, rest, plain)

    gram_rows = rows_of(gram)
    second = NS_B * gram_rows
    second = second + NS_C * dot(gram_rows.astype(BF16), gram[...].astype(BF16), plain)
    both = (
        jnp.where(chosen, NS_A * NS_A, 0.0)
        + NS_A * (rows_of(first) + second)
        + dot(second.astype(BF16), first_low, plain)
    ) * scale
    both = jnp.concatenate(halves(both), 0)
    across = ((1,), (1,))
    for start in range(0, value.shape[0], 256):
        step = min(256, value.shape[0] - start)
        out = dot(both, value[start : start + step], across)
        out = out[:picked] + out[picked:]
        mine[:, start : start + step] = out[:height]
        theirs[:, start : start + step] = out[height : 2 * height].astype(BF16)


def shards(
    features,
    cotangent,
    depth_kernel,
    ln_gain,
    weight_up,
    bias_up,
    weight_down,
    layer_scale,
    tissue,
    lengths,
):
    tile_rows, columns, channels = features.shape
    tiles = lax.axis_size("tile")
    owners = lax.axis_size("own")
    lines = tiles // PLANE
    half_lines = lines // 2
    line_bits = [1 << i for i in range(lines.bit_length() - 1)]
    tile = lax.axis_index("tile")
    own = lax.axis_index("own")
    place, line = tile & (PLANE - 1), tile >> (PLANE.bit_length() - 1)
    share = tile_rows // owners
    offset = own * share
    tokens = share * columns
    ids = jnp.stack([tile, offset, own]).astype(jnp.int32)
    flags = tissue.reshape(-1)
    strip = features.reshape(tile_rows * columns, channels)
    taps = depth_kernel.reshape(KERNEL * KERNEL, channels)
    gain, scale = ln_gain[None], layer_scale[None]
    frame = pltpu.VMEM((tile_rows + 2 * MARGIN, columns, channels), F32)
    wide = pltpu.VMEM((share, columns, channels), F32)
    rims = [jax.ShapeDtypeStruct((RIM * columns, channels), BF16)] * 2

    height = channels // tiles
    units = weight_up.shape[1] // PLANE
    both_weights = jnp.stack([weight_up, weight_down.T])
    pieces = []
    for s in range(PLANE):
        piece = lax.dynamic_slice_in_dim(both_weights, (place ^ s) * units, units, 2)
        pieces.append(swap(piece, "tile", s) if s else piece)
    if height % 16:
        piece = jnp.concatenate(in_order(pieces, place), 1)
    else:
        (piece,) = call(
            piece_kernel,
            [jax.ShapeDtypeStruct((2, PLANE * height, units), BF16)],
            [],
            10**6,
            place[None], *pieces,
        )

    head, tail = call(
        edges_kernel,
        rims,
        [pltpu.SemaphoreType.DMA] * 2,
        10**6,
        tile[None], lengths, strip,
        scalars=2, apart=1,
    )
    before, after = neighbours(head, tail)
    piece, before, after = lax.optimization_barrier((piece, before, after))
    bias = bias_up[None]
    if units % LANES:
        bias = lax.dynamic_slice_in_dim(bias, place * units, units, 1)

    sent, centred, inverse = call(
        forward_kernel,
        [
            jax.ShapeDtypeStruct((2, tokens, channels), BF16),
            jax.ShapeDtypeStruct((tokens, channels), F32),
            jax.ShapeDtypeStruct((tokens, LANES), F32),
        ],
        [frame, wide],
        10**6,
        ids, lengths, flags, strip, cotangent.reshape(strip.shape),
        before, after, taps, gain, scale,
        scalars=3,
    )
    held = piece[None]
    for bit in line_bits[:0:-1]:
        shape = jax.ShapeDtypeStruct((2 * held.shape[0],) + held.shape[1:], BF16)
        came = swap(held, "tile", PLANE * bit)
        (held,) = call(double_kernel, [shape], [], 10**6, held, came, scalars=0)
    late = swap(held, "tile", PLANE)
    (mine,) = call(
        join_kernel,
        [jax.ShapeDtypeStruct((2, PLANE * tokens, channels), BF16)],
        [],
        10**6,
        sent, *[swap(sent, "tile", s) for s in range(1, PLANE)],
        scalars=0,
    )
    shares = [mine] + [swap(mine, "own", s) for s in range(1, owners)]

    kept = 2 * units // lines
    total_tokens = owners * PLANE * tokens
    half_parts = jax.ShapeDtypeStruct((lines // 2, kept, channels), BF16)
    hidden_shape = jax.ShapeDtypeStruct((total_tokens, units), BF16)
    weight_shape = jax.ShapeDtypeStruct((channels, units), BF16)
    up, down_t = call(
        weights_kernel, [weight_shape, weight_shape], [], 13 * 10**9, line[None], held, late
    )
    reduced, other, act, grad_hidden = call(
        functools.partial(mlp_kernel, owners=owners),
        [half_parts, half_parts, hidden_shape, hidden_shape],
        [pltpu.VMEM((2 * units, channels), F32)],
        5 * 10**9,
        jnp.stack([line & 1, place]), up, down_t, bias, *shares,
    )

    def split(blocks, bit):
        blocks = blocks.reshape(-1, 2, kept, channels)
        which = jnp.where((line & bit) != 0, 1, 0)
        mine = lax.dynamic_slice_in_dim(blocks, which, 1, 1)
        other = lax.dynamic_slice_in_dim(blocks, 1 - which, 1, 1)
        return mine[:, 0], other[:, 0].astype(BF16)

    arrived = swap(other, "tile", PLANE)

    part_shape = (2, PLANE * tokens, channels)
    mine, *others = call(
        partial_kernel,
        [jax.ShapeDtypeStruct(part_shape, F32)]
        + [jax.ShapeDtypeStruct(part_shape, BF16)] * (owners - 1),
        [],
        10**9,
        act, grad_hidden, up, down_t,
        scalars=0,
    )
    others = [swap(value, "own", s + 1) for s, value in enumerate(others)]
    flat = jax.ShapeDtypeStruct((tokens, channels), BF16)
    blocks = call(
        add_kernel,
        [flat] * (2 * PLANE),
        [],
        10**6,
        mine, *others,
        scalars=0,
    )
    blocks = [
        swap(value, "tile", i % PLANE) if i % PLANE else value for i, value in enumerate(blocks)
    ]
    for_norm, for_output = blocks[:PLANE], blocks[PLANE:]
    arrived, for_norm[1] = lax.optimization_barrier((arrived, for_norm[1]))
    reduced = reduced.astype(F32) + arrived.astype(F32)
    for bit in line_bits[1:-1]:
        reduced, other = split(reduced, bit)
        reduced = reduced + swap(other, "tile", PLANE * bit).astype(F32)
    reduced, other = split(reduced, line_bits[-1])
    arrived = swap(other, "tile", PLANE * line_bits[-1])

    (grad_mixed,) = call(
        norm_back_kernel,
        [flat],
        [],
        10**6,
        ids, lengths, flags, centred, inverse, gain, *for_norm,
        scalars=3,
    )
    halves = [grad_mixed] + [swap(grad_mixed, "own", s) for s in range(1, owners)]
    head, tail = call(rims_kernel, rims, [], 10**6, ids, lengths, *halves, scalars=2)
    before, after = neighbours(head, tail)
    arrived, before, after, for_output = lax.optimization_barrier(
        (arrived, before, after, for_output)
    )
    grad_t = (reduced + arrived.astype(F32)).astype(BF16)[0]
    group = PLANE * half_lines
    if group == 8:
        near = [swap(grad_t, "tile", bit) for bit in (1, 2, 4)]
        corner = swap(grad_t, "tile", 7)
        far = [swap(near[1], "tile", 1), swap(near[0], "tile", 4), swap(near[2], "tile", 2)]
        gathered = [grad_t, near[0], near[1], far[0], near[2], far[1], far[2], corner]
    else:
        gathered = [swap(grad_t, "tile", e) if e else grad_t for e in range(group)]

    (grad_features,) = call(
        backward_kernel,
        [flat],
        [frame, wide],
        10**6,
        ids, lengths, cotangent.reshape(strip.shape), before, after, taps, *halves,
        scalars=2,
    )

    other = tile ^ (PLANE * half_lines)
    square = pltpu.VMEM((channels, channels), F32)
    (block_out,) = call(
        output_kernel,
        [flat],
        [],
        10**6,
        ids, lengths, flags, strip, scale, *for_output,
        scalars=3,
    )
    gathered, grad_features, block_out = lax.optimization_barrier(
        (gathered, grad_features, block_out)
    )
    if kept % 16:
        slots = [hidden_block((tile & (group - 1)) ^ e, group) for e in range(group)]
        ordered = jnp.zeros((group, kept, channels), BF16)
        ordered = ordered.at[jnp.stack(slots)].set(jnp.stack(gathered))
        gathered = [ordered.reshape(-1, channels)]
    mine, theirs = call(
        ortho_kernel,
        [
            jax.ShapeDtypeStruct((height, weight_up.shape[1]), F32),
            jax.ShapeDtypeStruct((height, weight_up.shape[1]), BF16),
        ],
        [pltpu.VMEM((weight_up.shape[1], channels), BF16), square, square, square],
        10 * 10**9,
        jnp.stack([tile * height, other * height, tile & (group - 1)]), *gathered,
    )
    theirs = swap(theirs, "tile", PLANE * half_lines)
    theirs = theirs.astype(F32)
    expands = line < half_lines
    muon_up = jnp.where(expands, mine, theirs)
    muon_down = jnp.where(expands, theirs, mine).T
    shape = (share, columns, channels)
    return (block_out.reshape(shape), grad_features.reshape(shape), muon_up, muon_down)


def solution(mesh):
    in_specs = (
        P("tile", None, None),
        P("tile", None, None),
        P(),
        P(),
        P("tile", "own"),
        P("own"),
        P("own", "tile"),
        P(),
        P("tile", None),
        P(),
    )
    out_specs = (
        P(("tile", "own"), None, None),
        P(("tile", "own"), None, None),
        P("tile", "own"),
        P("own", "tile"),
    )
    return jax.shard_map(shards, mesh=mesh, in_specs=in_specs, out_specs=out_specs, check_vma=False)
```

```python
import functools
import math

import jax
import jax.numpy as jnp
from jax import lax
from jax.experimental import pallas as pl
from jax.experimental.pallas import tpu as pltpu
from jax.sharding import PartitionSpec as P

KERNEL = 7
PATCH = 8
COLS = 8
MARGIN = KERNEL // 2
RIM = MARGIN + 1
PLANE = 4
LANES = 128
CHUNK = 8
SLACK = 4 * 2**20

INV_ROOT_TWO = 0.7071067811865476
INV_ROOT_TAU = 0.3989422804014327
NS_A = 3.4445
NS_B = -4.775
NS_C = 2.0315
EPS_NORM = 1e-06
F32 = jnp.float32
BF16 = jnp.bfloat16


def swap(value, axis, bit):
    return lax.ppermute(value, axis, [(i, i ^ bit) for i in range(lax.axis_size(axis))])


def neighbours(first, last):
    devices = lax.axis_size("tile")
    up = [(i, i + 1) for i in range(devices - 1)]
    down = [(i + 1, i) for i in range(devices - 1)]
    return lax.ppermute(last, "tile", up), lax.ppermute(first, "tile", down)


def in_order(blocks, index):
    bit = 1
    while bit < len(blocks):
        odd = (index & bit) != 0
        blocks = [jnp.where(odd, blocks[s ^ bit], blocks[s]) for s in range(len(blocks))]
        bit *= 2
    return blocks


def call(kernel, out_shape, scratch, flops, *operands, scalars=1, apart=0):
    held = sum(a.size * a.dtype.itemsize for a in operands + tuple(out_shape))
    room = sum(math.prod(a.shape) * 4 for a in scratch if hasattr(a, "shape"))
    smem = pl.BlockSpec(memory_space=pltpu.SMEM)
    vmem = pl.BlockSpec(memory_space=pltpu.VMEM)
    return pl.pallas_call(
        kernel,
        out_shape=out_shape,
        in_specs=[smem] * scalars
        + [vmem] * (len(operands) - scalars - apart)
        + [pl.BlockSpec(memory_space=pltpu.HBM)] * apart,
        out_specs=[vmem] * len(out_shape),
        scratch_shapes=scratch,
        compiler_params=pltpu.CompilerParams(vmem_limit_bytes=2 * held + room + SLACK),
        cost_estimate=pl.CostEstimate(flops=flops, bytes_accessed=2**20, transcendentals=0),
    )(*operands)


def convolve(framed, kernel_ref, offset, out_ref, flipped):
    share, columns, channels = out_ref.shape
    chunk = min(CHUNK, share)
    lane_steps = channels // LANES
    column = lax.broadcasted_iota(jnp.int32, (chunk + 2 * MARGIN, columns, LANES), 1)

    def step(index, carry):
        lanes = pl.ds(pl.multiple_of((index % lane_steps) * LANES, LANES), LANES)
        first = (index // lane_steps) * chunk
        rows = framed[pl.ds(offset + first, chunk + 2 * MARGIN), :, lanes]
        total = jnp.zeros((chunk, columns, LANES), F32)
        for col_tap in range(KERNEL):
            reach = col_tap - MARGIN
            moved = rows
            if reach:
                moved = pltpu.roll(rows, (-reach) % columns, 1)
                inside = (column + reach >= 0) & (column + reach < columns)
                moved = jnp.where(inside, moved, 0.0)
            for row_tap in range(KERNEL):
                tap = row_tap * KERNEL + col_tap
                tap = KERNEL * KERNEL - 1 - tap if flipped else tap
                weight = kernel_ref[pl.ds(tap, 1), lanes][None]
                total = total + weight * moved[row_tap : row_tap + chunk]
        out_ref[pl.ds(first, chunk), :, lanes] = total
        return carry

    lax.fori_loop(0, lane_steps * (share // chunk), step, 0)


def place_strip(framed, pieces, before_ref, after_ref, live_rows):
    columns, channels = framed.shape[1:]

    def rows_of(ref):
        value = ref[...].astype(F32)
        return value.reshape(value.shape[0] // columns, columns, channels)

    for start, ref in pieces:
        rows = rows_of(ref)
        framed[pl.ds(start + MARGIN, rows.shape[0])] = rows
    framed[pl.ds(framed.shape[0] - MARGIN, MARGIN)] = jnp.zeros((MARGIN, columns, channels), F32)
    framed[pl.ds(0, MARGIN)] = rows_of(before_ref)[RIM - MARGIN :]
    framed[pl.ds(live_rows + MARGIN, MARGIN)] = rows_of(after_ref)[:MARGIN]


def live_rows(ids, lengths):
    return PATCH * lengths[ids[0]]


def kept_rows(ids, lengths, tissue, tokens):
    row = ids[1] + lax.broadcasted_iota(jnp.int32, (tokens, 1), 0) // COLS
    keep = jnp.zeros((tokens, 1), F32)
    for patch in range(tissue.shape[0]):
        keep = jnp.where(row // PATCH == patch, tissue[patch].astype(F32), keep)
    live = row < live_rows(ids, lengths)
    return live, jnp.where(live, keep, 0.0)


def rims_kernel(ids, lengths, *refs):
    *shares, head, tail = refs
    tokens = shares[0].shape[0]
    last = (live_rows(ids, lengths) - RIM) * COLS
    for s, share in enumerate(shares):

        @pl.when(ids[2] == s)
        def _():
            head[...] = share[: head.shape[0], :]

        @pl.when((last // tokens) ^ ids[2] == s)
        def _():
            start = pl.multiple_of(lax.rem(last, tokens), RIM * COLS)
            tail[...] = share[pl.ds(start, tail.shape[0]), :]


def edges_kernel(ids, lengths, strip, head, tail, first_sem, last_sem):
    rows = head.shape[0]
    last = pl.multiple_of((live_rows(ids, lengths) - RIM) * COLS, RIM * COLS)
    copies = [
        pltpu.make_async_copy(strip.at[pl.ds(0, rows)], head, first_sem),
        pltpu.make_async_copy(strip.at[pl.ds(last, rows)], tail, last_sem),
    ]
    for copy in copies:
        copy.start()
    for copy in copies:
        copy.wait()


def forward_kernel(
    ids,
    lengths,
    tissue,
    strip,
    cotangent,
    before,
    after,
    taps,
    gain,
    layer_scale,
    sent,
    centred_out,
    inverse,
    framed,
    mixed,
):
    place_strip(framed, [(0, strip)], before, after, live_rows(ids, lengths))
    convolve(framed, taps, ids[1], mixed, False)
    tokens, channels = centred_out.shape
    value = mixed[...].reshape(tokens, channels)
    shifted = value - jnp.sum(value, 1, keepdims=True) / channels
    variance = jnp.sum(shifted * shifted, 1, keepdims=True) / channels
    inv_std = lax.rsqrt(variance + 1e-06)
    centred = shifted * inv_std
    centred_out[...] = centred
    inverse[...] = jnp.broadcast_to(inv_std, inverse.shape)
    sent[0] = (centred * gain[...]).astype(BF16)
    _, keep = kept_rows(ids, lengths, tissue, tokens)
    start = pl.multiple_of(ids[1] * COLS, 16)
    grad_out = cotangent[pl.ds(start, tokens), :].astype(F32)
    sent[1] = (keep * layer_scale[...] * grad_out).astype(BF16)


def summed(blocks):
    value = blocks[0][...].astype(F32)
    for ref in blocks[1:]:
        value = value + ref[...].astype(F32)
    return value


def norm_back_kernel(ids, lengths, tissue, centred, inverse, gain, *refs):
    *blocks, grad_mixed = refs
    tokens, channels = grad_mixed.shape
    live, _ = kept_rows(ids, lengths, tissue, tokens)
    scaled_grad = summed(blocks) * gain[...]
    first_mean = jnp.sum(scaled_grad, 1, keepdims=True) / channels
    second_mean = jnp.sum(scaled_grad * centred[...], 1, keepdims=True) / channels
    value = inverse[:, :1] * (scaled_grad - first_mean - centred[...] * second_mean)
    grad_mixed[...] = jnp.where(live, value, 0.0).astype(BF16)


def output_kernel(ids, lengths, tissue, strip, layer_scale, *refs):
    *blocks, block_out = refs
    tokens = block_out.shape[0]
    start = pl.multiple_of(ids[1] * COLS, 16)
    live, keep = kept_rows(ids, lengths, tissue, tokens)
    inputs = strip[pl.ds(start, tokens), :].astype(F32)
    block = inputs + keep * layer_scale[...] * summed(blocks)
    block_out[...] = jnp.where(live, block, 0.0).astype(BF16)


def join_kernel(*refs):
    *blocks, out = refs
    start = 0
    for ref in blocks:
        out[:, start : start + ref.shape[1], :] = ref[...]
        start += ref.shape[1]


def double_kernel(*refs):
    count = len(refs) // 3
    for held, came, out in zip(refs[:count], refs[count : 2 * count], refs[2 * count :]):
        out[: held.shape[0]] = held[...]
        out[held.shape[0] :] = came[...]


def piece_kernel(scalars, *refs):
    *blocks, out = refs
    rows = blocks[0].shape[1]
    for s, block in enumerate(blocks):
        start = pl.multiple_of((scalars[0] ^ s) * rows, rows)
        out[:, pl.ds(start, rows), :] = block[...]


def weights_kernel(scalars, early, late, up, down_t):
    lines, rows = 2 * early.shape[0], early.shape[2]
    bits = lines.bit_length() - 1
    for e in range(lines):
        apart = sum(lines >> (i + 1) for i in range(bits) if e >> i & 1)
        start = pl.multiple_of((scalars[0] ^ apart) * rows, rows)
        later, entry = divmod(e, lines // 2)
        piece = (early, late)[later]
        up[pl.ds(start, rows), :] = piece[entry, 0]
        down_t[pl.ds(start, rows), :] = piece[entry, 1]


def mlp_kernel(scalars, up, down_t, bias, *refs, owners):
    tokens_of = refs[:owners]
    kept, sent, act_out, grad_out, parts = refs[owners:]
    lines = 2 * kept.shape[0]
    plain, over_tokens = ((1,), (0,)), ((0,), (0,))
    count = tokens_of[0].shape[1]
    step = min(256, count)
    units = act_out.shape[1]
    bias_row = bias[...]
    if bias.shape[1] != units:
        bias_row = bias[:, pl.ds(pl.multiple_of(scalars[1] * units, LANES), units)]
    for index, ref in enumerate(tokens_of):
        for start in range(0, count, step):
            hidden = dot(ref[0, start : start + step, :], up[...], plain) + bias_row
            cdf = 0.5 * (1.0 + lax.erf(hidden * INV_ROOT_TWO))
            slope = cdf + hidden * jnp.exp(-0.5 * hidden * hidden) * INV_ROOT_TAU
            grad_act = dot(ref[1, start : start + step, :], down_t[...], plain)
            rows_out = pl.ds(index * count + start, step)
            act_out[rows_out, :] = (hidden * cdf).astype(BF16)
            grad_out[rows_out, :] = (grad_act * slope).astype(BF16)

    for half, (hidden_side, which) in enumerate(((grad_out, 0), (act_out, 1))):
        total = jnp.zeros((units, parts.shape[1]), F32)
        for index, ref in enumerate(tokens_of):
            rows_in = slice(index * count, (index + 1) * count)
            total = total + dot(hidden_side[rows_in, :], ref[which], over_tokens)
        parts[half * units : (half + 1) * units, :] = total
    width = kept.shape[1]
    for q in range(lines):
        block = parts[q * width : (q + 1) * width, :].astype(BF16)
        same = scalars[0] == q % 2

        @pl.when(same)
        def _():
            kept[q // 2] = block

        @pl.when(jnp.logical_not(same))
        def _():
            sent[q // 2] = block


def partial_kernel(act, grad_hidden, up, down_t, mine, *others):
    across = ((1,), (1,))
    count = mine.shape[1]
    step = min(256, count)
    for index, ref in enumerate((mine,) + others):
        for start in range(0, count, step):
            rows_in = slice(index * count + start, index * count + start + step)
            rows_out = slice(start, start + step)
            ref[0, rows_out, :] = dot(grad_hidden[rows_in, :], up[...], across).astype(ref.dtype)
            ref[1, rows_out, :] = dot(act[rows_in, :], down_t[...], across).astype(ref.dtype)


def add_kernel(mine, *refs):
    others, outs = refs[: -2 * PLANE], refs[-2 * PLANE :]
    tokens = outs[0].shape[0]
    for index, out in enumerate(outs):
        which, strip = divmod(index, PLANE)
        rows_in = slice(strip * tokens, (strip + 1) * tokens)
        total = mine[which, rows_in, :]
        for other in others:
            total = total + other[which, rows_in, :].astype(F32)
        out[...] = total.astype(BF16)


def backward_kernel(ids, lengths, cotangent, before, after, taps, *rest):
    *pieces, grad_features, framed, spread = rest
    tokens = grad_features.shape[0]
    share = spread.shape[0]
    placed = [((ids[2] ^ s) * share, piece) for s, piece in enumerate(pieces)]
    place_strip(framed, placed, before, after, live_rows(ids, lengths))
    convolve(framed, taps, ids[1], spread, True)
    start = pl.multiple_of(ids[1] * COLS, 16)
    value = cotangent[pl.ds(start, tokens), :].astype(F32) + spread[...].reshape(grad_features.shape)
    row = ids[1] + lax.broadcasted_iota(jnp.int32, (tokens, 1), 0) // COLS
    grad_features[...] = jnp.where(row < live_rows(ids, lengths), value, 0.0).astype(BF16)


def dot(left, right, contract, precision=None):
    return lax.dot_general(
        left, right, (contract, ((), ())), precision=precision, preferred_element_type=F32
    )


def hidden_block(member, group):
    return (member & (PLANE - 1)) * (group // PLANE) + (member >> (PLANE.bit_length() - 1))


def ortho_kernel(scalars, *refs):
    *gathered, mine, theirs, whole, gram, first, half = refs
    channels = whole.shape[1]
    if len(gathered) == 1:
        whole[...] = gathered[0][...]
    else:
        rows = gathered[0].shape[0]
        for e, ref in enumerate(gathered):
            block = hidden_block(scalars[2] ^ e, len(gathered))
            whole[pl.ds(pl.multiple_of(block * rows, rows), rows), :] = ref[...]

    plain = ((1,), (0,))
    steps = [pl.ds(i, 256) for i in range(0, channels, 256)]
    value = whole[...]
    squares = jnp.zeros((1, 1), F32)
    for rows in steps:
        product = dot(value[:, rows.start : rows.start + 256], value, ((0,), (0,)))
        row = rows.start + lax.broadcasted_iota(jnp.int32, product.shape, 0)
        column = lax.broadcasted_iota(jnp.int32, product.shape, 1)
        on_diagonal = jnp.where(row == column, product, 0.0)
        squares = squares + jnp.sum(jnp.sum(on_diagonal, 1, keepdims=True), 0, keepdims=True)
        gram[rows, :] = product
    scale = lax.rsqrt(squares + EPS_NORM)
    gram[...] = gram[...] * (scale * scale)

    low = gram[...].astype(BF16)
    for rows in steps:
        first[rows, :] = NS_B * gram[rows, :] + NS_C * dot(low[rows.start : rows.start + 256], low, plain)
    first_low = first[...].astype(BF16)
    for rows in steps:
        product = dot(low[rows.start : rows.start + 256], first_low, plain)
        half[rows, :] = NS_A * gram[rows, :] + product
    half_low = half[...].astype(BF16)
    for rows in steps:
        product = dot(half_low[rows.start : rows.start + 256], first_low, plain)
        gram[rows, :] = NS_A * half[rows, :] + product

    height = mine.shape[0]
    picked = -(-2 * height // 16) * 16
    row = lax.broadcasted_iota(jnp.int32, (picked, channels), 0)
    column = lax.broadcasted_iota(jnp.int32, (picked, channels), 1)
    wanted = jnp.where(row < height, scalars[0] + row, scalars[1] + row - height)
    chosen = (column == wanted) & (row < 2 * height)

    def halves(matrix):
        top = matrix.astype(BF16)
        return top, (matrix - top.astype(F32)).astype(BF16)

    def rows_of(ref):
        if height % 8 == 0:
            starts = [pl.multiple_of(scalars[i], 8) for i in range(2)]
            return jnp.concatenate([ref[pl.ds(start, height), :] for start in starts], 0)
        pick = jnp.where(chosen, 1.0, 0.0).astype(BF16)
        top, rest = halves(ref[...])
        return dot(pick, top, plain) + dot(pick, rest, plain)

    gram_rows = rows_of(gram)
    second = NS_B * gram_rows
    second = second + NS_C * dot(gram_rows.astype(BF16), gram[...].astype(BF16), plain)
    both = (
        jnp.where(chosen, NS_A * NS_A, 0.0)
        + NS_A * (rows_of(first) + second)
        + dot(second.astype(BF16), first_low, plain)
    ) * scale
    both = jnp.concatenate(halves(both), 0)
    across = ((1,), (1,))
    for start in range(0, value.shape[0], 256):
        step = min(256, value.shape[0] - start)
        out = dot(both, value[start : start + step], across)
        out = out[:picked] + out[picked:]
        mine[:, start : start + step] = out[:height]
        theirs[:, start : start + step] = out[height : 2 * height].astype(BF16)


def shards(
    features,
    cotangent,
    depth_kernel,
    ln_gain,
    weight_up,
    bias_up,
    weight_down,
    layer_scale,
    tissue,
    lengths,
):
    tile_rows, columns, channels = features.shape
    tiles = lax.axis_size("tile")
    owners = lax.axis_size("own")
    lines = tiles // PLANE
    half_lines = lines // 2
    line_bits = [1 << i for i in range(lines.bit_length() - 1)]
    tile = lax.axis_index("tile")
    own = lax.axis_index("own")
    place, line = tile & (PLANE - 1), tile >> (PLANE.bit_length() - 1)
    share = tile_rows // owners
    offset = own * share
    tokens = share * columns
    ids = jnp.stack([tile, offset, own]).astype(jnp.int32)
    flags = tissue.reshape(-1)
    strip = features.reshape(tile_rows * columns, channels)
    taps = depth_kernel.reshape(KERNEL * KERNEL, channels)
    gain, scale = ln_gain[None], layer_scale[None]
    frame = pltpu.VMEM((tile_rows + 2 * MARGIN, columns, channels), F32)
    wide = pltpu.VMEM((share, columns, channels), F32)
    rims = [jax.ShapeDtypeStruct((RIM * columns, channels), BF16)] * 2

    height = channels // tiles
    units = weight_up.shape[1] // PLANE
    both_weights = jnp.stack([weight_up, weight_down.T])
    pieces = []
    for s in range(PLANE):
        piece = lax.dynamic_slice_in_dim(both_weights, (place ^ s) * units, units, 2)
        pieces.append(swap(piece, "tile", s) if s else piece)
    if height % 16:
        piece = jnp.concatenate(in_order(pieces, place), 1)
    else:
        (piece,) = call(
            piece_kernel,
            [jax.ShapeDtypeStruct((2, PLANE * height, units), BF16)],
            [],
            10**6,
            place[None], *pieces,
        )

    head, tail = call(
        edges_kernel,
        rims,
        [pltpu.SemaphoreType.DMA] * 2,
        10**6,
        tile[None], lengths, strip,
        scalars=2, apart=1,
    )
    before, after = neighbours(head, tail)
    piece, before, after = lax.optimization_barrier((piece, before, after))
    bias = bias_up[None]
    if units % LANES:
        bias = lax.dynamic_slice_in_dim(bias, place * units, units, 1)

    sent, centred, inverse = call(
        forward_kernel,
        [
            jax.ShapeDtypeStruct((2, tokens, channels), BF16),
            jax.ShapeDtypeStruct((tokens, channels), F32),
            jax.ShapeDtypeStruct((tokens, LANES), F32),
        ],
        [frame, wide],
        10**6,
        ids, lengths, flags, strip, cotangent.reshape(strip.shape),
        before, after, taps, gain, scale,
        scalars=3,
    )
    held = piece[None]
    for bit in line_bits[:0:-1]:
        shape = jax.ShapeDtypeStruct((2 * held.shape[0],) + held.shape[1:], BF16)
        came = swap(held, "tile", PLANE * bit)
        (held,) = call(double_kernel, [shape], [], 10**6, held, came, scalars=0)
    late = swap(held, "tile", PLANE)
    (mine,) = call(
        join_kernel,
        [jax.ShapeDtypeStruct((2, PLANE * tokens, channels), BF16)],
        [],
        10**6,
        sent, *[swap(sent, "tile", s) for s in range(1, PLANE)],
        scalars=0,
    )
    shares = [mine] + [swap(mine, "own", s) for s in range(1, owners)]

    kept = 2 * units // lines
    total_tokens = owners * PLANE * tokens
    half_parts = jax.ShapeDtypeStruct((lines // 2, kept, channels), BF16)
    hidden_shape = jax.ShapeDtypeStruct((total_tokens, units), BF16)
    weight_shape = jax.ShapeDtypeStruct((channels, units), BF16)
    up, down_t = call(
        weights_kernel, [weight_shape, weight_shape], [], 13 * 10**9, line[None], held, late
    )
    reduced, other, act, grad_hidden = call(
        functools.partial(mlp_kernel, owners=owners),
        [half_parts, half_parts, hidden_shape, hidden_shape],
        [pltpu.VMEM((2 * units, channels), F32)],
        5 * 10**9,
        jnp.stack([line & 1, place]), up, down_t, bias, *shares,
    )

    def split(blocks, bit):
        blocks = blocks.reshape(-1, 2, kept, channels)
        which = jnp.where((line & bit) != 0, 1, 0)
        mine = lax.dynamic_slice_in_dim(blocks, which, 1, 1)
        other = lax.dynamic_slice_in_dim(blocks, 1 - which, 1, 1)
        return mine[:, 0], other[:, 0].astype(BF16)

    arrived = swap(other, "tile", PLANE)

    part_shape = (2, PLANE * tokens, channels)
    mine, *others = call(
        partial_kernel,
        [jax.ShapeDtypeStruct(part_shape, F32)]
        + [jax.ShapeDtypeStruct(part_shape, BF16)] * (owners - 1),
        [],
        10**9,
        act, grad_hidden, up, down_t,
        scalars=0,
    )
    others = [swap(value, "own", s + 1) for s, value in enumerate(others)]
    flat = jax.ShapeDtypeStruct((tokens, channels), BF16)
    blocks = call(
        add_kernel,
        [flat] * (2 * PLANE),
        [],
        10**6,
        mine, *others,
        scalars=0,
    )
    blocks = [
        swap(value, "tile", i % PLANE) if i % PLANE else value for i, value in enumerate(blocks)
    ]
    for_norm, for_output = blocks[:PLANE], blocks[PLANE:]
    arrived, for_norm[1] = lax.optimization_barrier((arrived, for_norm[1]))
    reduced = reduced.astype(F32) + arrived.astype(F32)
    for bit in line_bits[1:-1]:
        reduced, other = split(reduced, bit)
        reduced = reduced + swap(other, "tile", PLANE * bit).astype(F32)
    reduced, other = split(reduced, line_bits[-1])
    arrived = swap(other, "tile", PLANE * line_bits[-1])

    (grad_mixed,) = call(
        norm_back_kernel,
        [flat],
        [],
        10**6,
        ids, lengths, flags, centred, inverse, gain, *for_norm,
        scalars=3,
    )
    halves = [grad_mixed] + [swap(grad_mixed, "own", s) for s in range(1, owners)]
    head, tail = call(rims_kernel, rims, [], 10**6, ids, lengths, *halves, scalars=2)
    before, after = neighbours(head, tail)
    arrived, before, after = lax.optimization_barrier((arrived, before, after))
    grad_t = (reduced + arrived.astype(F32)).astype(BF16)[0]
    group = PLANE * half_lines
    if group == 8:
        near = [swap(grad_t, "tile", bit) for bit in (1, 2, 4)]
        corner = swap(grad_t, "tile", 7)
        far = [swap(near[1], "tile", 1), swap(near[0], "tile", 4), swap(near[2], "tile", 2)]
        gathered = [grad_t, near[0], near[1], far[0], near[2], far[1], far[2], corner]
    else:
        gathered = [swap(grad_t, "tile", e) if e else grad_t for e in range(group)]

    (grad_features,) = call(
        backward_kernel,
        [flat],
        [frame, wide],
        10**6,
        ids, lengths, cotangent.reshape(strip.shape), before, after, taps, *halves,
        scalars=2,
    )

    other = tile ^ (PLANE * half_lines)
    square = pltpu.VMEM((channels, channels), F32)
    (block_out,) = call(
        output_kernel,
        [flat],
        [],
        10**6,
        ids, lengths, flags, strip, scale, *for_output,
        scalars=3,
    )
    gathered, grad_features, block_out = lax.optimization_barrier(
        (gathered, grad_features, block_out)
    )
    if kept % 16:
        slots = [hidden_block((tile & (group - 1)) ^ e, group) for e in range(group)]
        ordered = jnp.zeros((group, kept, channels), BF16)
        ordered = ordered.at[jnp.stack(slots)].set(jnp.stack(gathered))
        gathered = [ordered.reshape(-1, channels)]
    mine, theirs = call(
        ortho_kernel,
        [
            jax.ShapeDtypeStruct((height, weight_up.shape[1]), F32),
            jax.ShapeDtypeStruct((height, weight_up.shape[1]), BF16),
        ],
        [pltpu.VMEM((weight_up.shape[1], channels), BF16), square, square, square],
        10 * 10**9,
        jnp.stack([tile * height, other * height, tile & (group - 1)]), *gathered,
    )
    theirs = swap(theirs, "tile", PLANE * half_lines)
    theirs = theirs.astype(F32)
    expands = line < half_lines
    muon_up = jnp.where(expands, mine, theirs)
    muon_down = jnp.where(expands, theirs, mine).T
    shape = (share, columns, channels)
    return (block_out.reshape(shape), grad_features.reshape(shape), muon_up, muon_down)


def solution(mesh):
    in_specs = (
        P("tile", None, None),
        P("tile", None, None),
        P(),
        P(),
        P("tile", "own"),
        P("own"),
        P("own", "tile"),
        P(),
        P("tile", None),
        P(),
    )
    out_specs = (
        P(("tile", "own"), None, None),
        P(("tile", "own"), None, None),
        P("tile", "own"),
        P("own", "tile"),
    )
    return jax.shard_map(shards, mesh=mesh, in_specs=in_specs, out_specs=out_specs, check_vma=False)
```
